32 devices in a mesh: nodes: 8 (over y, x, core), cols: 4 (over z).
Axes of the slice: x: 2, y: 2, z: 4, core: 2. Of those that a mesh axis runs over, the one named last changes fastest.
Arguments:
- features: float32 [4, 2048, 100], P('cols', 'nodes'), may hold values from -6 to 6
- adjacency: int32 [4, 2048, 2048], P('cols', 'nodes'), may hold values from 0 to 1, as said below
- node_mask: int32 [4, 2048], P('cols', 'nodes'), may hold values from 0 to 1
- labels: int32 [4, 2048], P('cols', 'nodes'), may hold values from 0 to 46
- label_mask: int32 [4, 2048], P('cols', 'nodes'), may hold values 0 or 1
- weight_first: float32 [200, 256], P(None, 'cols'), may hold values from -0.4375 to 0.4375
- weight_rest: float32 [2, 512, 256], P(None, None, 'cols'), may hold values from -0.25 to 0.25
- norm_params: float32 [2, 3, 256], replicated, may hold values from -3 to 4
- weight_head: float32 [256, 47], replicated, may hold values from -0.375 to 0.375
- bias_head: float32 [47], replicated, may hold values from -3 to 3
- moment_first: float32 [200, 256], P(None, 'cols'), may hold values from -1.5258789e-05 to 1.5258789e-05
- moment_rest: float32 [2, 512, 256], P(None, None, 'cols'), may hold values from -1.5258789e-05 to 1.5258789e-05
- moment_norm: float32 [2, 3, 256], replicated, may hold values from -5.340576e-05 to 5.340576e-05
- moment_head: float32 [256, 47], replicated, may hold values from -1.5258789e-05 to 1.5258789e-05
- moment_bias: float32 [47], replicated, may hold values from -5.340576e-05 to 5.340576e-05
- square_first: float32 [200, 256], P(None, 'cols'), may hold values from 6.789984e-13 to 2.7159937e-12
- square_rest: float32 [2, 512, 256], P(None, None, 'cols'), may hold values from 6.789984e-13 to 2.7159937e-12
- square_norm: float32 [2, 3, 256], replicated, may hold values from 6.789984e-12 to 2.7159936e-11
- square_head: float32 [256, 47], replicated, may hold values from 6.789984e-13 to 2.7159937e-12
- square_bias: float32 [47], replicated, may hold values from 6.789984e-12 to 2.7159936e-11
- average_first: float32 [200, 256], P(None, 'cols'), may hold values from -0.4375 to 0.4375
- average_rest: float32 [2, 512, 256], P(None, None, 'cols'), may hold values from -0.25 to 0.25
- average_norm: float32 [2, 3, 256], replicated, may hold values from -0.5 to 1.5
- average_head: float32 [256, 47], replicated, may hold values from -0.375 to 0.375
- average_bias: float32 [47], replicated, may hold values from -3 to 3
Outputs:
- loss_total: float32 [], replicated
- label_count: float32 [], replicated
- gradient_norm: float32 [], replicated
- momentum_first: float32 [200, 256], P(None, 'cols')
- variance_first: float32 [200, 256], P(None, 'cols')
- trained_first: float32 [200, 256], P(None, 'cols')
- averaged_first: float32 [200, 256], P(None, 'cols')
- momentum_rest: float32 [2, 512, 256], P(None, None, 'cols')
- variance_rest: float32 [2, 512, 256], P(None, None, 'cols')
- trained_rest: float32 [2, 512, 256], P(None, None, 'cols')
- averaged_rest: float32 [2, 512, 256], P(None, None, 'cols')
- momentum_norm: float32 [2, 3, 256], replicated
- variance_norm: float32 [2, 3, 256], replicated
- trained_norm: float32 [2, 3, 256], replicated
- averaged_norm: float32 [2, 3, 256], replicated
- momentum_head: float32 [256, 47], replicated
- variance_head: float32 [256, 47], replicated
- trained_head: float32 [256, 47], replicated
- averaged_head: float32 [256, 47], replicated
- momentum_bias: float32 [47], replicated
- variance_bias: float32 [47], replicated
- trained_bias: float32 [47], replicated
- averaged_bias: float32 [47], replicated
The draws below stay inside these ranges and needn't reach their ends.
Inputs may be any that keep to these rules, and one draw needn't show every extreme that they name: adjacency[s, i, j] is 1 only where both nodes are real (node_mask 1).
All inputs are finite; a program needn't handle non-finite values. No bound on the sum of `label_mask` on one device may be relied on, other than what follows from the above.
Results may differ from the reference program's by a relative error of at most 0.0003.
Values sent between devices are 32-bit elements; how exact they have to be, the bound alone decides.
A program may use at most 128 MiB of HBM per device.

```python
import math
import jax
import jax.numpy as jnp
from jax import lax

FEAT = 100
HID = 256
CLASSES = 47
LAYERS = 3
ADAM_STEP = 10
G = 2048
SUBS = 4
PARAMS = 589103


def node_validity(key):
    key = jax.random.fold_in(key, 11)
    rows = jnp.arange(G, dtype=jnp.int32)
    chance = 300 + 600 * rows // G
    draws = jax.random.randint(key, (SUBS, G), 0, 1000)
    return (draws < chance[None, :]).astype(jnp.int32)


def draw_node_mask(key, part):
    return node_validity(key)


def draw_adjacency(key, part):
    valid = node_validity(key)
    key = jax.random.fold_in(key, 2)
    rows = jnp.arange(G, dtype=jnp.int32)
    spacing = jnp.abs(rows[:, None] - rows[None, :])
    limit = jnp.where((spacing >= 1) & (spacing <= 3), 6 * G // 10, 6)
    draws = jax.random.randint(key, (SUBS, G, G), 0, G)
    edges = (draws < limit[None, :, :]).astype(jnp.int32)
    return edges * valid[:, :, None] * valid[:, None, :]


def draw_norm_params(key, part):
    key = jax.random.fold_in(key, 5)
    first_key, second_key = jax.random.split(key)
    ramp = 0.5 + 1.5 * jnp.arange(HID, dtype=jnp.float32) / HID
    gains = ramp[None, :] * (1.0 + 0.1 * jnp.clip(jax.random.normal(first_key, (LAYERS, HID), jnp.float32), -3.0, 3.0))
    shifts = 0.3 * jnp.clip(jax.random.normal(second_key, (LAYERS, HID), jnp.float32), -3.0, 3.0)
    return jnp.stack([gains, shifts]).astype(jnp.float32)


def place_ends(array, own_key, least, largest):
    place = [jax.random.randint(jax.random.fold_in(own_key, axis), (), 0, length) for axis, length in enumerate(array.shape)]
    widest = array.shape.index(max(array.shape))
    next_to = place[:widest] + [(place[widest] + 1) % array.shape[widest]] + place[widest + 1:]
    return array.at[tuple(place)].set(least).at[tuple(next_to)].set(largest)


def level_of(rng, dims, cuts, low, top_value):
    loudness, own = 1.0, jax.random.fold_in(rng, 6)
    for axis_at, shards_of in cuts:
        steps = jnp.exp(jax.random.uniform(jax.random.fold_in(own, axis_at), (shards_of,), jnp.float32, low / len(cuts), top_value / len(cuts)))
        loudness = loudness * jnp.repeat(steps, dims[axis_at] // shards_of).reshape([-1 if axis == axis_at else 1 for axis in range(len(dims))])
    return loudness


def gaussian(key, shape, deviation, reach, cuts=(), held_as=jnp.bfloat16):
    loudness = level_of(key, shape, cuts, -0.22, 0.18) if cuts else 1.0
    array = jax.random.normal(key, shape, jnp.float32) * deviation * loudness
    return jnp.minimum(jnp.maximum(array, -reach), reach).astype(held_as)


def setup_inputs(seed: int = 0) -> dict:
    streams_of = jax.random.split(jax.random.key(seed), 26)
    return {
        "features": gaussian(streams_of[0], (SUBS, G, FEAT), 1.0, 6.0, ((0, 4), (1, 8)), jnp.float32),
        "adjacency": draw_adjacency(jax.random.fold_in(streams_of[25], 71), 0),
        "node_mask": draw_node_mask(jax.random.fold_in(streams_of[25], 71), 0),
        "labels": place_ends(jax.random.randint(streams_of[3], (SUBS, G), 0, CLASSES), jax.random.fold_in(streams_of[3], 1), 0, CLASSES - 1).astype(jnp.int32),
        "label_mask": place_ends((jax.random.randint(streams_of[4], (SUBS, G), 0, 2) < 1).astype(jnp.int32), jax.random.fold_in(streams_of[4], 1), 0, 1),
        "weight_first": gaussian(streams_of[5], (2 * FEAT, HID), (2 * FEAT) ** -0.5, 0.4375, ((1, 4),), jnp.float32),
        "weight_rest": gaussian(streams_of[6], (LAYERS - 1, 2 * HID, HID), (2 * HID) ** -0.5, 0.25, ((2, 4),), jnp.float32),
        "norm_params": draw_norm_params(jax.random.fold_in(streams_of[25], 71), 0),
        "weight_head": gaussian(streams_of[8], (HID, CLASSES), HID ** -0.5, 0.375, (), jnp.float32),
        "bias_head": gaussian(streams_of[9], (CLASSES,), 0.5, 3.0, (), jnp.float32),
        "moment_first": gaussian(streams_of[10], (2 * FEAT, HID), (0.0022 / PARAMS ** 0.5), 1.52587890625e-05, ((1, 4),), jnp.float32),
        "moment_rest": gaussian(streams_of[11], (LAYERS - 1, 2 * HID, HID), (0.0022 / PARAMS ** 0.5), 1.52587890625e-05, ((2, 4),), jnp.float32),
        "moment_norm": gaussian(streams_of[12], (2, LAYERS, HID), (0.0066 / PARAMS ** 0.5), 5.340576171875e-05, (), jnp.float32),
        "moment_head": gaussian(streams_of[13], (HID, CLASSES), (0.0022 / PARAMS ** 0.5), 1.52587890625e-05, (), jnp.float32),
        "moment_bias": gaussian(streams_of[14], (CLASSES,), (0.0066 / PARAMS ** 0.5), 5.340576171875e-05, (), jnp.float32),
        "square_first": jnp.clip(jnp.exp(math.log(2.7159936626108827e-12) - 1.3862944 * jax.random.uniform(streams_of[15], (2 * FEAT, HID), jnp.float32) ** level_of(streams_of[15], (2 * FEAT, HID), ((1, 4),), -0.2, 0.2)), 6.789984156527207e-13, 2.7159936626108827e-12),
        "square_rest": jnp.clip(jnp.exp(math.log(2.7159936626108827e-12) - 1.3862944 * jax.random.uniform(streams_of[16], (LAYERS - 1, 2 * HID, HID), jnp.float32) ** level_of(streams_of[16], (LAYERS - 1, 2 * HID, HID), ((2, 4),), -0.2, 0.2)), 6.789984156527207e-13, 2.7159936626108827e-12),
        "square_norm": jnp.clip(jnp.exp(jax.random.uniform(streams_of[17], (2, LAYERS, HID), jnp.float32, math.log(6.789983939686772e-12), math.log(2.715993575874709e-11))), 6.789983939686772e-12, 2.715993575874709e-11),
        "square_head": jnp.clip(jnp.exp(jax.random.uniform(streams_of[18], (HID, CLASSES), jnp.float32, math.log(6.789984156527207e-13), math.log(2.7159936626108827e-12))), 6.789984156527207e-13, 2.7159936626108827e-12),
        "square_bias": jnp.clip(jnp.exp(jax.random.uniform(streams_of[19], (CLASSES,), jnp.float32, math.log(6.789983939686772e-12), math.log(2.715993575874709e-11))), 6.789983939686772e-12, 2.715993575874709e-11),
        "average_first": gaussian(streams_of[20], (2 * FEAT, HID), (2 * FEAT) ** -0.5, 0.4375, ((1, 4),), jnp.float32),
        "average_rest": gaussian(streams_of[21], (LAYERS - 1, 2 * HID, HID), (2 * HID) ** -0.5, 0.25, ((2, 4),), jnp.float32),
        "average_norm": jnp.clip(jax.random.uniform(streams_of[22], (2, LAYERS, HID), jnp.float32, -0.5, 1.5), -0.5, 1.5),
        "average_head": gaussian(streams_of[23], (HID, CLASSES), HID ** -0.5, 0.375, (), jnp.float32),
        "average_bias": gaussian(streams_of[24], (CLASSES,), 0.5, 3.0, (), jnp.float32),
    }


HIGH = lax.Precision.HIGHEST
CLIP = 0.02
RATE_MATRIX = 0.03
RATE_SMALL = 0.3
BETA_ONE = 0.9
BETA_TWO = 0.999
ADAM_EPS = 1e-08
DECAY = 0.01
AVERAGE = 0.9
NORM_EPS = 1e-05

def aggregate_all(adjacency, hidden, degree):

    def one_graph(pair):
        adj_one, hid_one = pair
        return jnp.dot(adj_one.astype(hid_one.dtype), hid_one, precision=HIGH)
    return lax.map(jax.checkpoint(one_graph), (adjacency, hidden)) / degree

def forward(params, features, adjacency, degree, valid, onehot, counted):
    weight_first, weight_rest, norm_params, weight_head, bias_head = params
    hidden = features
    total = jnp.sum(valid)
    for layer in range(LAYERS):
        weight = weight_first if layer == 0 else weight_rest[layer - 1]
        inputs = jnp.concatenate([hidden, aggregate_all(adjacency, hidden, degree)], axis=2)
        linear = jnp.einsum('sgk,kd->sgd', inputs, weight, precision=HIGH)
        active = jax.nn.gelu(linear)
        mean = lax.optimization_barrier(jnp.sum(valid * active, axis=(0, 1))) / total
        var = lax.optimization_barrier(jnp.sum(valid * active * active, axis=(0, 1))) / total - mean * mean
        normed = (active - mean) * lax.rsqrt(var + NORM_EPS)
        hidden = norm_params[0, layer] * normed + norm_params[1, layer]
    logits = jnp.einsum('sgk,kc->sgc', hidden, weight_head, precision=HIGH) + bias_head
    logp = jax.nn.log_softmax(logits, axis=-1)
    return -jnp.sum(counted * lax.optimization_barrier(jnp.sum(onehot * logp, axis=-1)))

def adamw(weight, first, second, average, grad, rate):
    first = BETA_ONE * first + (1.0 - BETA_ONE) * grad
    second = BETA_TWO * second + (1.0 - BETA_TWO) * grad * grad
    fix_one = 1.0 - BETA_ONE ** ADAM_STEP
    fix_two = 1.0 - BETA_TWO ** ADAM_STEP
    update = first / fix_one / (jnp.sqrt(second / fix_two) + ADAM_EPS)
    weight = weight - rate * (update + DECAY * weight)
    average = AVERAGE * average + (1.0 - AVERAGE) * weight
    return (first, second, weight, average)

def reference(features, adjacency, node_mask, labels, label_mask, weight_first, weight_rest, norm_params, weight_head, bias_head, moment_first, moment_rest, moment_norm, moment_head, moment_bias, square_first, square_rest, square_norm, square_head, square_bias, average_first, average_rest, average_norm, average_head, average_bias):
    ftype = features.dtype
    degree = jnp.maximum(lax.optimization_barrier(jnp.sum(adjacency, axis=2)), 1).astype(ftype)[:, :, None]
    valid = node_mask.astype(ftype)[:, :, None]
    onehot = (labels[:, :, None] == jnp.arange(CLASSES, dtype=jnp.int32)[None, None, :]).astype(ftype)
    counted = (label_mask * node_mask).astype(ftype)
    label_count = jnp.sum(counted)
    params = (weight_first, weight_rest, norm_params, weight_head, bias_head)

    def loss_of(params):
        return forward(params, features, adjacency, degree, valid, onehot, counted)
    loss_total, pullback = jax.vjp(loss_of, params)
    grads = pullback(jnp.ones_like(loss_total) / label_count)[0]
    squares = sum((jnp.sum(g * g) for g in grads))
    gradient_norm = jnp.sqrt(squares)
    scale = CLIP / jnp.maximum(gradient_norm, CLIP)
    rates = (RATE_MATRIX, RATE_MATRIX, RATE_SMALL, RATE_MATRIX, RATE_SMALL)
    moments = (moment_first, moment_rest, moment_norm, moment_head, moment_bias)
    seconds = (square_first, square_rest, square_norm, square_head, square_bias)
    averages = (average_first, average_rest, average_norm, average_head, average_bias)
    result = [adamw(params[i], moments[i], seconds[i], averages[i], grads[i] * scale, rates[i]) for i in range(5)]
    return (loss_total, label_count, gradient_norm, result[0][0], result[0][1], result[0][2], result[0][3], result[1][0], result[1][1], result[1][2], result[1][3], result[2][0], result[2][1], result[2][2], result[2][3], result[3][0], result[3][1], result[3][2], result[3][3], result[4][0], result[4][1], result[4][2], result[4][3])
```

```python
import functools
import types

import jax
import jax.numpy as jnp
from jax import lax
from jax.experimental import pallas as pl
from jax.experimental.pallas import tpu as pltpu
from jax.sharding import PartitionSpec as P

LAYERS = 3
ADAM_STEP = 10
CLIP = 0.02
RATE_MATRIX = 0.03
RATE_SMALL = 0.3
BETA_ONE = 0.9
BETA_TWO = 0.999
ADAM_EPS = 1e-08
DECAY = 0.01
AVERAGE = 0.9
NORM_EPS = 1e-05

MESH = pl.DeviceIdType.MESH
F32 = jnp.float32
BF16 = jnp.bfloat16
LANES = 128
GELU_OUT = 0.7978845608028654
GELU_CUBE = 0.044715


def split(value):
    high = value.astype(BF16)
    return high, (value - high.astype(F32)).astype(BF16)


def dot(left, right):
    return lax.dot_general(left, right, (((1,), (0,)), ((), ())), preferred_element_type=F32)


def dot_t(left, right):
    return lax.dot_general(left, right, (((1,), (1,)), ((), ())), preferred_element_type=F32)


def dot3(left, right):
    (lh, ll), (rh, rl) = left, right
    return dot(lh, rh) + (dot(lh, rl) + dot(ll, rh))


def dot3_t(left, right):
    (lh, ll), (rh, rl) = left, right
    return dot_t(lh, rh) + (dot_t(lh, rl) + dot_t(ll, rh))


def remote(src, dst, send, recv, device):
    return pltpu.make_async_remote_copy(
        src_ref=src, dst_ref=dst, send_sem=send, recv_sem=recv, device_id=device, device_id_type=MESH
    )


def wait_bytes(ref, sem):
    pltpu.make_async_copy(ref, ref, sem).wait()


def flip(index, distance):
    bit = 1
    while bit <= distance:
        if distance & bit:
            index = index + (1 - 2 * lax.rem(lax.div(index, bit), 2)) * bit
        bit *= 2
    return index


def step_kernel(d, *refs):
    v = types.SimpleNamespace(**dict(zip(d.names, refs, strict=True)))
    NN, NC, R, H, FP, HC, CH, L = d.NN, d.NC, d.R, d.H, d.FP, d.HC, d.CH, LAYERS
    NDEV, RPP, PPC, HV = d.NDEV, d.RPP, d.PPC, d.HV
    n, c = lax.axis_index("nodes"), lax.axis_index("cols")
    me = n * NC + c
    ch, k = lax.div(n, 2), lax.rem(n, 2)
    sib = (ch * 2 + 1 - k, c)

    def device(index):
        return lax.div(index, NC), lax.rem(index, NC)

    def rows(i, size):
        return pl.ds(pl.multiple_of(i * size, size), size)

    barrier = pltpu.get_barrier_semaphore()

    def greet(i, carry):
        pl.semaphore_signal(
            barrier, inc=1, device_id=device(lax.rem(me + i, NDEV)), device_id_type=MESH
        )
        return carry

    lax.fori_loop(1, NDEV, greet, 0)

    def adj_load(j):
        return pltpu.make_async_copy(
            v.adj.at[:, rows(j, R)], v.adjb.at[lax.rem(j, d.NS)], v.ld.at[lax.rem(j, d.NS)]
        )

    for j in range(min(NN, d.NS)):
        adj_load(j).start()
    v.xg[n] = jnp.zeros((R, FP), F32)
    v.xg[n, :, : d.F] = v.feat[...]

    v.wpad[...] = jnp.zeros(v.wpad.shape, F32)
    v.wpad[: d.F, :HC] = v.w0[: d.F, :]
    v.wpad[FP : FP + d.F, :HC] = v.w0[d.F :, :]
    v.wt0[rows(c, HC), :] = v.wpad[: 2 * FP, :].T[:HC]
    for i in range(L - 1):
        v.wpad[:, :HC] = v.wr[i]
        v.wtr[i, rows(c, HC), :] = v.wpad[...].T[:HC]
    pl.semaphore_wait(barrier, NDEV - 1)

    def ag_send(g, src, buf):
        for dd in reversed(range(1, CH)):
            remote(
                src, buf.at[n], v.s_xy.at[g, dd], v.r_xy.at[g, dd], (flip(ch, dd) * 2 + k, c)
            ).start()
        remote(src, buf.at[n], v.s_sb.at[g, 0], v.r_sb.at[g, 0], sib).start()

    def ag_forward(g, buf, dd):
        j = flip(ch, dd) * 2 + k
        wait_bytes(buf.at[j], v.r_xy.at[g, dd])
        remote(buf.at[j], buf.at[j], v.s_sb.at[g, dd], v.r_sb.at[g, dd], sib).start()
        return j

    def ag_sibling(g, buf, dd):
        j = flip(ch, dd) * 2 + 1 - k
        wait_bytes(buf.at[j], v.r_sb.at[g, dd])
        return j

    def ag_drain(g, src):
        for dd in range(CH):
            if dd:
                wait_bytes(src, v.s_xy.at[g, dd])
            wait_bytes(src, v.s_sb.at[g, dd])

    def ar_send(a):
        def one(i, carry):
            remote(
                v.arb.at[a, me],
                v.arb.at[a, me],
                v.s_ar.at[a],
                v.r_ar.at[a],
                device(lax.rem(me + i, NDEV)),
            ).start()
            return carry

        lax.fori_loop(1, NDEV, one, 0)

    def ar_put(a, vectors):
        at = 0
        for vec in vectors:
            for i in range(vec.shape[1] // LANES):
                v.arb[a, me, at : at + 1, :] = vec[:, i * LANES : (i + 1) * LANES]
                at += 1
        if at < 8:
            v.arb[a, me, at:, :] = jnp.zeros((8 - at, LANES), F32)

    def ar_wait(a):
        wait_bytes(v.arb.at[a, pl.ds(0, NDEV - 1)], v.r_ar.at[a])
        return jnp.sum(v.arb[a], axis=0)

    def vec(total, i):
        return jnp.concatenate([total[i * HV + j : i * HV + j + 1] for j in range(HV)], axis=1)

    ag_send(0, v.xg.at[n], v.xg)
    for l in range(L):
        ref = v.wt0 if l == 0 else v.wtr.at[l - 1]
        for dd in range(1, NC):
            block = ref.at[rows(c, HC), :]
            remote(block, block, v.s_w.at[l], v.r_w.at[l], (n, lax.rem(c + dd, NC))).start()

    eye = lax.broadcasted_iota(jnp.int32, (R, R), 0) == lax.broadcasted_iota(jnp.int32, (R, R), 1)
    ones = jnp.ones((R, LANES), BF16)

    def column(row):
        return dot(jnp.where(eye, row.astype(F32), 0.0).astype(BF16), ones)

    v.valid[...] = column(v.nm[...])
    v.counted[...] = column(v.lm[...] * v.nm[...])
    v.label[...] = column(v.lb[...])

    v.invdeg[...] = jnp.zeros((R, LANES), F32)

    def adj_block(j, carry):
        adj_load(j).wait()
        block = v.adjb[lax.rem(j, d.NS)].astype(F32)
        if NN > d.NS:

            @pl.when(j + d.NS < NN)
            def _():
                adj_load(j + d.NS).start()

        half = block.astype(BF16)
        v.abf[j] = half
        v.at[j] = block.T.astype(BF16)
        v.invdeg[...] += dot(half, ones)
        return carry

    lax.fori_loop(0, NN, adj_block, 0)
    degree = v.invdeg[...]
    v.linked[...] = jnp.minimum(degree, 1.0)
    v.invdeg[...] = 1.0 / jnp.maximum(degree, 1.0)

    def wide(value):
        return jnp.concatenate([value] * HV, axis=1) if HV > 1 else value

    def gather_dot(g, buf, own, width):
        def add(j, block, first=False):
            high, low = split(block)
            a = v.abf[j]
            part = dot(jnp.concatenate([a, a], axis=1), jnp.concatenate([high, low], axis=0))
            if first:
                v.agg[:, :width] = part
            else:
                v.agg[:, :width] += part

        add(n, own[...], True)
        j = ag_sibling(g, buf, 0)
        add(j, buf[j])
        for dd in range(1, CH):
            j = ag_forward(g, buf, dd)
            add(j, buf[j])
        for dd in range(1, CH):
            j = ag_sibling(g, buf, dd)
            add(j, buf[j])

    RC = min(R, 64)

    def activate(l):
        def chunk(i, carry):
            r = rows(i, RC)
            x = v.lin[r, :]
            square = x * x
            t = jnp.tanh(GELU_OUT * x * (1.0 + GELU_CUBE * square))
            half = 0.5 * (1.0 + t)
            act = x * half
            v.acts[l, r, :] = act
            v.gp[l, r, :] = half + (0.5 * GELU_OUT) * x * (1.0 - t * t) * (
                1.0 + (3.0 * GELU_CUBE) * square
            )
            masked = wide(v.valid[r, :]) * act
            return (
                carry[0] + jnp.sum(masked.reshape(RC // 8, 8, H), axis=0),
                carry[1] + jnp.sum((masked * act).reshape(RC // 8, 8, H), axis=0),
            )

        zero = jnp.zeros((8, H), F32)
        one, two = lax.fori_loop(0, R // RC, chunk, (zero, zero))
        return jnp.sum(one, axis=0, keepdims=True), jnp.sum(two, axis=0, keepdims=True)

    def keep_stats(l, total):
        count = jnp.max(v.count[0:1, :], axis=1, keepdims=True)
        mean = vec(total, 0) / count
        var = vec(total, 1) / count - mean * mean
        inverse = lax.rsqrt(var + NORM_EPS)
        gain, shift = v.npar[0, l : l + 1, :], v.npar[1, l : l + 1, :]
        v.vecs[l, 0:1, :] = mean
        v.vecs[l, 1:2, :] = inverse
        v.vecs[l, 2:3, :] = gain * inverse
        v.vecs[l, 3:4, :] = shift - mean * (gain * inverse)
        v.vecs[l, 4:5, :] = gain

    gather_dot(0, v.xg, v.xg.at[n], FP)
    v.inh[0, :, :FP], v.inl[0, :, :FP] = split(v.xg[n])
    v.inh[0, :, FP : 2 * FP], v.inl[0, :, FP : 2 * FP] = split(v.agg[:, :FP] * v.invdeg[...])
    wait_bytes(v.wt0.at[pl.ds(0, (NC - 1) * HC)], v.r_w.at[0])
    v.w0h[...], v.w0l[...] = split(v.wt0[...])
    v.lin[...] = dot3_t(
        (v.inh[0, :, : 2 * FP], v.inl[0, :, : 2 * FP]), (v.w0h[...], v.w0l[...])
    )
    one, two = activate(0)
    ag_send(1, v.acts.at[0], v.ag.at[0])
    ar_put(
        0,
        [
            one,
            two,
            jnp.sum(v.valid[...], axis=0, keepdims=True),
            jnp.sum(v.counted[...], axis=0, keepdims=True),
        ],
    )
    ar_send(0)

    for l in range(1, L):
        wait_bytes(v.wtr.at[l - 1, pl.ds(0, (NC - 1) * HC)], v.r_w.at[l])
        v.wh[l - 1], v.wl[l - 1] = split(v.wtr[l - 1])
        total = ar_wait(l - 1)
        if l == 1:
            v.count[...] = total[2 * HV : 2 * HV + 2]
        keep_stats(l - 1, total)
        scale, shift = v.vecs[l - 1, 2:3, :], v.vecs[l - 1, 3:4, :]
        v.inh[l, :, :H], v.inl[l, :, :H] = split(v.acts[l - 1] * scale + shift)
        v.lin[...] = dot3_t(
            (v.inh[l, :, :H], v.inl[l, :, :H]), (v.wh[l - 1, :, :H], v.wl[l - 1, :, :H])
        )
        gather_dot(l, v.ag.at[l - 1], v.acts.at[l - 1], H)
        v.inh[l, :, H:], v.inl[l, :, H:] = split(
            v.agg[...] * wide(v.invdeg[...]) * scale + wide(v.linked[...]) * shift
        )
        v.lin[...] += dot3_t(
            (v.inh[l, :, H:], v.inl[l, :, H:]), (v.wh[l - 1, :, H:], v.wl[l - 1, :, H:])
        )
        one, two = activate(l)
        if l < L - 1:
            ag_send(l + 1, v.acts.at[l], v.ag.at[l])
        ar_put(l, [one, two])
        ar_send(l)

    v.whp[...] = jnp.zeros(v.whp.shape, F32)
    v.whp[:, : d.C] = v.whd[...]
    head = split(v.whp[...])
    lane = lax.broadcasted_iota(jnp.int32, (R, LANES), 1)
    onehot = jnp.where(lane.astype(F32) == v.label[...], 1.0, 0.0)
    for g in (1, 2):
        ag_drain(g, v.acts.at[0])
    keep_stats(L - 1, ar_wait(L - 1))
    last = split(v.acts[L - 1] * v.vecs[L - 1, 2:3, :] + v.vecs[L - 1, 3:4, :])
    logits = dot3(last, head) + v.bias[...]
    real = lane < d.C
    top = jnp.max(jnp.where(real, logits, -3.0e38), axis=1, keepdims=True)
    moved = logits - top
    power = jnp.where(real, jnp.exp(moved), 0.0)
    total = jnp.sum(power, axis=1, keepdims=True)
    logp = moved - jnp.log(total)
    counted = v.counted[...]
    label_count = jnp.max(v.count[1:2, :], axis=1, keepdims=True)
    g_logits = counted * (power / total - onehot) / label_count
    gl_split = split(g_logits)
    v.gout[...] = dot3_t(gl_split, head)

    def norm_sums(l):
        mean, inverse = v.vecs[l, 0:1, :], v.vecs[l, 1:2, :]

        def chunk(i, carry):
            r = rows(i, RC)
            g = v.gout[r, :]
            normed = (v.acts[l, r, :] - mean) * inverse
            return (
                carry[0] + jnp.sum((g * normed).reshape(RC // 8, 8, H), axis=0),
                carry[1] + jnp.sum(g.reshape(RC // 8, 8, H), axis=0),
            )

        zero = jnp.zeros((8, H), F32)
        one, two = lax.fori_loop(0, R // RC, chunk, (zero, zero))
        return jnp.sum(one, axis=0, keepdims=True), jnp.sum(two, axis=0, keepdims=True)

    ar_put(3, norm_sums(L - 1))
    ar_send(3)
    rows_loss = jnp.sum(jnp.where(real, onehot * logp, 0.0), axis=1, keepdims=True) * counted
    ar_put(
        6,
        [
            -jnp.sum(rows_loss, axis=0, keepdims=True),
            jnp.sum(g_logits, axis=0, keepdims=True),
        ],
    )
    ar_send(6)
    last_t = split((v.acts[L - 1] * v.vecs[L - 1, 2:3, :] + v.vecs[L - 1, 3:4, :]).T)
    v.hg[...] = dot3(last_t, gl_split)

    HP, HPC = d.HP, d.HPC

    def head_scatter(i, carry):
        t = lax.rem(me + i, NDEV)

        def go():
            remote(
                v.hg.at[rows(t, HP), :], v.hrecv.at[me], v.s_h.at[0], v.r_h.at[0], device(t)
            ).start()

        if HPC == NDEV:
            go()
        else:
            pl.when(t < HPC)(go)
        return carry

    lax.fori_loop(1, NDEV, head_scatter, 0)

    def others(index, size, ref_of, init):
        return lax.fori_loop(1, size, lambda i, s: s + ref_of(lax.rem(index + i, size)), init)

    def head_gather():
        def go():
            wait_bytes(v.hrecv.at[pl.ds(0, NDEV - 1)], v.r_h.at[0])
            piece = others(me, NDEV, lambda s: v.hrecv[s], v.hg[rows(me, HP), :])
            v.hfin[rows(me, HP), :] = piece

            def one(i, carry):
                block = v.hfin.at[rows(me, HP), :]
                remote(
                    block, block, v.s_h.at[1], v.r_h.at[1], device(lax.rem(me + i, NDEV))
                ).start()
                return carry

            lax.fori_loop(1, NDEV, one, 0)

        if HPC == NDEV:
            go()
        else:
            pl.when(me < HPC)(go)

    def cols_send(i):
        for dd in range(1, NC):
            t = lax.rem(c + dd, NC)
            remote(v.dwb.at[i, t], v.zrecv.at[i, c], v.s_z.at[i], v.r_z.at[i], (n, t)).start()

    def nodes_send(i):
        wait_bytes(v.zrecv.at[i, pl.ds(0, NC - 1)], v.r_z.at[i])
        v.zs[i] = others(c, NC, lambda s: v.zrecv[i, s], v.dwb[i, c])

        def one(j, carry):
            t = lax.rem(n + j, NN)

            def go():
                remote(
                    v.zs.at[i, rows(t, RPP), :], v.nrecv.at[i, n], v.s_n.at[i], v.r_n.at[i], (t, c)
                ).start()

            if PPC == NN:
                go()
            else:
                pl.when(t < PPC)(go)
            return carry

        lax.fori_loop(1, NN, one, 0)

    def reducer(fn):
        if PPC == NN:
            fn()
        else:
            pl.when(n < PPC)(fn)

    def pieces_out(i, fin, piece):
        fin[rows(n, RPP), :] = piece
        square = piece * piece
        for j in range(square.shape[1] // LANES):
            v.sq[...] += jnp.sum(
                square[:, j * LANES : (j + 1) * LANES].reshape(RPP // 8, 8, LANES), axis=0
            )

        def one(j, carry):
            block = fin.at[rows(n, RPP), :]
            remote(
                block, block, v.s_f.at[i], v.r_f.at[i], (lax.rem(n + j, NN), c)
            ).start()
            return carry

        lax.fori_loop(1, NN, one, 0)

    def nodes_gather(i):
        def go():
            wait_bytes(v.nrecv.at[i, pl.ds(0, NN - 1)], v.r_n.at[i])
            piece = others(n, NN, lambda s: v.nrecv[i, s], v.zs[i, rows(n, RPP), :])
            pieces_out(i, v.fin.at[i], piece)

        reducer(go)

    v.sq[...] = jnp.zeros((8, LANES), F32)

    def linear_grad(l, a):
        total = ar_wait(a)
        g_gain, g_shift = vec(total, 0), vec(total, 1)
        v.gn[0, l : l + 1, :] = g_gain
        v.gn[1, l : l + 1, :] = g_shift
        mean, inverse, scale = v.vecs[l, 0:1, :], v.vecs[l, 1:2, :], v.vecs[l, 2:3, :]
        count = jnp.max(v.count[0:1, :], axis=1, keepdims=True)
        by_one = scale * g_shift / count
        by_normed = scale * g_gain / count

        def chunk(i, carry):
            r = rows(i, RC)
            normed = (v.acts[l, r, :] - mean) * inverse
            g_active = scale * v.gout[r, :] - wide(v.valid[r, :]) * (by_one + normed * by_normed)
            g_linear = v.gp[l, r, :] * g_active
            v.lin[r, :] = g_linear
            v.glh[r, :], v.gll[r, :] = split(g_linear)
            return carry

        lax.fori_loop(0, R // RC, chunk, 0)

    def weight_grad(l, width):
        return dot3(split(v.lin[...].T), (v.inh[l, :, :width], v.inl[l, :, :width]))

    order = list(reversed(range(1, CH))) + [0]

    def scatter_drain(g):
        for dd in range(CH):
            wait_bytes(v.ag.at[0, dd], v.s_rs.at[g, 0, dd])
            if dd:
                wait_bytes(v.ag.at[0, dd], v.s_rs.at[g, 1, dd])

    for l in (2, 1):
        a = 5 - l
        g = l - 1
        linear_grad(l, a)
        gl = (v.glh[...], v.gll[...])
        spread = dot3(gl, (v.wh[l - 1, :, H:], v.wl[l - 1, :, H:])) * wide(v.invdeg[...])
        high, low = split(spread)
        v.spread[:R, :] = high
        v.spread[R:, :] = low
        out, srecv, crecv = v.ag.at[1], v.ag.at[0, :CH], v.ag.at[0, CH:]
        if l < L - 1:
            scatter_drain(g + 1)

        def partial(j):
            t = v.at[j]
            return dot(jnp.concatenate([t, t], axis=1), v.spread[...])

        for dd in order:
            out[dd] = partial(flip(ch, dd) * 2 + 1 - k)
            remote(out.at[dd], srecv.at[dd], v.s_rs.at[g, 0, dd], v.r_rs.at[g, 0, dd], sib).start()
        for dd in order:
            part = partial(flip(ch, dd) * 2 + k)
            wait_bytes(srecv.at[dd], v.r_rs.at[g, 0, dd])
            out[CH + dd] = part + srecv[dd]
            if dd:
                remote(
                    out.at[CH + dd],
                    crecv.at[dd],
                    v.s_rs.at[g, 1, dd],
                    v.r_rs.at[g, 1, dd],
                    (flip(ch, dd) * 2 + k, c),
                ).start()
        v.gout[...] = out[CH] + dot3(
            gl, (v.wh[l - 1, :, :H], v.wl[l - 1, :, :H])
        )
        grad = weight_grad(l, 2 * H)
        for t in range(NC):
            v.dwb[l - 1, t] = grad[t * HC : (t + 1) * HC, :]
        cols_send(l - 1)
        if l == 2:
            head_gather()
        else:
            nodes_gather(1)
        for dd in range(1, CH):
            wait_bytes(crecv.at[dd], v.r_rs.at[g, 1, dd])
            v.gout[...] += crecv[dd]
        ar_put(a + 1, norm_sums(l - 1))
        ar_send(a + 1)
        nodes_send(l - 1)

    linear_grad(0, 5)
    grad = weight_grad(0, 2 * FP)
    for t in range(NC):
        v.d0[t] = grad[t * HC : (t + 1) * HC, :]

    def first_scatter(i, carry):
        t = lax.rem(me + i, NDEV)
        tn, tc = device(t)

        def go():
            remote(
                v.d0.at[tc, rows(tn, RPP), :], v.recv0.at[me], v.s_0.at[0], v.r_0.at[0], (tn, tc)
            ).start()

        if PPC == NN:
            go()
        else:
            pl.when(tn < PPC)(go)
        return carry

    lax.fori_loop(1, NDEV, first_scatter, 0)
    nodes_gather(0)

    def first_gather():
        wait_bytes(v.recv0.at[pl.ds(0, NDEV - 1)], v.r_0.at[0])
        piece = others(me, NDEV, lambda s: v.recv0[s], v.d0[c, rows(n, RPP), :])
        pieces_out(2, v.fin0, piece)

    reducer(first_gather)
    ar_put(7, [jnp.sum(v.sq[...], axis=0, keepdims=True)])
    ar_send(7)

    total = ar_wait(6)
    bias_grad = total[1:2]
    v.misc[...] = jnp.zeros((8, LANES), F32)
    v.misc[0:1, :] = total[0:1]
    v.misc[1:2, :] = v.count[1:2, :]
    v.misc[3:4, :] = bias_grad

    def fin_wait(i, fin):
        if PPC == NN:
            wait_bytes(fin.at[pl.ds(0, (NN - 1) * RPP), :], v.r_f.at[i])
        else:

            @pl.when(n < PPC)
            def _():
                wait_bytes(fin.at[pl.ds(0, (PPC - 1) * RPP), :], v.r_f.at[i])

            @pl.when(n >= PPC)
            def _():
                wait_bytes(fin.at[pl.ds(0, PPC * RPP), :], v.r_f.at[i])

    if HPC == NDEV:
        wait_bytes(v.hfin.at[pl.ds(0, (NDEV - 1) * HP), :], v.r_h.at[1])
    else:

        @pl.when(me < HPC)
        def _():
            wait_bytes(v.hfin.at[pl.ds(0, (HPC - 1) * HP), :], v.r_h.at[1])

        @pl.when(me >= HPC)
        def _():
            wait_bytes(v.hfin.at[pl.ds(0, HPC * HP), :], v.r_h.at[1])

    head_grad = v.hfin[...]
    v.gh[...] = head_grad[:, : d.C]
    replicated = jnp.sum(head_grad * head_grad, axis=0, keepdims=True) + bias_grad * bias_grad
    small = jnp.zeros((1, H), F32)
    for i in range(2):
        small += jnp.sum(v.gn[i] * v.gn[i], axis=0, keepdims=True)
    for j in range(HV):
        replicated += small[:, j * LANES : (j + 1) * LANES]

    for i in range(L - 1):
        fin_wait(i, v.fin.at[i])
        v.wpad[...] = jnp.zeros(v.wpad.shape, F32)
        v.wpadt[:HC, :] = v.fin[i]
        v.gr[i] = v.wpadt[...].T[:, :HC]
    total = ar_wait(7)
    squares = jnp.sum(total[0:1] + replicated, axis=1, keepdims=True)
    norm = jnp.sqrt(squares)
    v.misc[2:3, :] = jnp.broadcast_to(norm, (1, LANES))
    v.misc[4:5, :] = jnp.broadcast_to(CLIP / jnp.maximum(norm, CLIP), (1, LANES))
    fin_wait(2, v.fin0)
    v.wpadt[:HC, : 2 * FP] = v.fin0[...]
    first_grad = v.wpadt[:, : 2 * FP].T
    v.g0[: d.F, :] = first_grad[: d.F, :HC]
    v.g0[d.F :, :] = first_grad[FP : FP + d.F, :HC]

    ag_drain(0, v.xg.at[0])
    for l in range(L):
        ref = v.wt0 if l == 0 else v.wtr.at[l - 1]
        wait_bytes(ref.at[pl.ds(0, (NC - 1) * HC)], v.s_w.at[l])
    for a in range(8):
        wait_bytes(v.arb.at[a, pl.ds(0, NDEV - 1)], v.s_ar.at[a])
    for i in range(L - 1):
        wait_bytes(v.zrecv.at[i, pl.ds(0, NC - 1)], v.s_z.at[i])

    scatter_drain(0)

    if PPC == NN:
        for i in range(L - 1):
            wait_bytes(v.nrecv.at[i, pl.ds(0, NN - 1)], v.s_n.at[i])
        wait_bytes(v.recv0.at[pl.ds(0, NDEV - 1)], v.s_0.at[0])
    else:

        @pl.when(n < PPC)
        def _():
            for i in range(L - 1):
                wait_bytes(v.nrecv.at[i, pl.ds(0, PPC - 1)], v.s_n.at[i])
            wait_bytes(v.recv0.at[pl.ds(0, PPC * NC - 1)], v.s_0.at[0])

        @pl.when(n >= PPC)
        def _():
            for i in range(L - 1):
                wait_bytes(v.nrecv.at[i, pl.ds(0, PPC)], v.s_n.at[i])
            wait_bytes(v.recv0.at[pl.ds(0, PPC * NC)], v.s_0.at[0])

    def drain_fin():
        for i in range(L - 1):
            wait_bytes(v.nrecv.at[i, pl.ds(0, NN - 1)], v.s_f.at[i])
        wait_bytes(v.recv0.at[pl.ds(0, NN - 1)], v.s_f.at[2])

    reducer(drain_fin)

    def drain_head():
        wait_bytes(v.hrecv.at[pl.ds(0, NDEV - 1)], v.s_h.at[1])

    if HPC == NDEV:
        wait_bytes(v.hrecv.at[pl.ds(0, NDEV - 1)], v.s_h.at[0])
        drain_head()
    else:

        @pl.when(me < HPC)
        def _():
            wait_bytes(v.hrecv.at[pl.ds(0, HPC - 1)], v.s_h.at[0])
            drain_head()

        @pl.when(me >= HPC)
        def _():
            wait_bytes(v.hrecv.at[pl.ds(0, HPC)], v.s_h.at[0])


def gradients(NN, NC, feat, adj, nm, lb, lm, w0, wr, npar, whd, bias):
    R, F = feat.shape
    H, C = whd.shape
    HC = w0.shape[1]
    CH, NDEV = NN // 2, NN * NC
    FP = -(-F // LANES) * LANES
    RPP = max(8, HC // NN)
    HP = max(8, H // NDEV)
    NS = min(NN, 8)
    d = types.SimpleNamespace(
        NN=NN, NC=NC, R=R, F=F, H=H, C=C, HC=HC, CH=CH, NDEV=NDEV, FP=FP, RPP=RPP, NS=NS,
        PPC=HC // RPP, HP=HP, HPC=H // HP, HV=H // LANES,
    )
    dma = pltpu.SemaphoreType.DMA
    L = LAYERS
    scratch = {
        "xg": pltpu.VMEM((NN, R, FP), F32),
        "ag": pltpu.VMEM((L - 1, NN, R, H), F32),
        "acts": pltpu.VMEM((L, R, H), F32),
        "gp": pltpu.VMEM((L, R, H), F32),
        "adjb": pltpu.VMEM((NS, R, R), jnp.int32),
        "abf": pltpu.VMEM((NN, R, R), BF16),
        "at": pltpu.VMEM((NN, R, R), BF16),
        "wpad": pltpu.VMEM((2 * H, LANES), F32),
        "wpadt": pltpu.VMEM((LANES, 2 * H), F32),
        "wt0": pltpu.VMEM((H, 2 * FP), F32),
        "wtr": pltpu.VMEM((L - 1, H, 2 * H), F32),
        "w0h": pltpu.VMEM((H, 2 * FP), BF16),
        "w0l": pltpu.VMEM((H, 2 * FP), BF16),
        "wh": pltpu.VMEM((L - 1, H, 2 * H), BF16),
        "wl": pltpu.VMEM((L - 1, H, 2 * H), BF16),
        "whp": pltpu.VMEM((H, LANES), F32),
        "inh": pltpu.VMEM((L, R, 2 * H), BF16),
        "inl": pltpu.VMEM((L, R, 2 * H), BF16),
        "agg": pltpu.VMEM((R, max(H, FP)), F32),
        "lin": pltpu.VMEM((R, H), F32),
        "gout": pltpu.VMEM((R, H), F32),
        "glh": pltpu.VMEM((R, H), BF16),
        "gll": pltpu.VMEM((R, H), BF16),
        "spread": pltpu.VMEM((2 * R, H), BF16),
        "valid": pltpu.VMEM((R, LANES), F32),
        "counted": pltpu.VMEM((R, LANES), F32),
        "label": pltpu.VMEM((R, LANES), F32),
        "invdeg": pltpu.VMEM((R, LANES), F32),
        "linked": pltpu.VMEM((R, LANES), F32),
        "count": pltpu.VMEM((2, LANES), F32),
        "vecs": pltpu.VMEM((L, 8, H), F32),
        "sq": pltpu.VMEM((8, LANES), F32),
        "arb": pltpu.VMEM((8, NDEV, 8, LANES), F32),
        "dwb": pltpu.VMEM((L - 1, NC, HC, 2 * H), F32),
        "zrecv": pltpu.VMEM((L - 1, NC, HC, 2 * H), F32),
        "zs": pltpu.VMEM((L - 1, HC, 2 * H), F32),
        "nrecv": pltpu.VMEM((L - 1, NN, RPP, 2 * H), F32),
        "fin": pltpu.VMEM((L - 1, HC, 2 * H), F32),
        "d0": pltpu.VMEM((NC, HC, 2 * FP), F32),
        "recv0": pltpu.VMEM((NDEV, RPP, 2 * FP), F32),
        "fin0": pltpu.VMEM((HC, 2 * FP), F32),
        "hg": pltpu.VMEM((H, LANES), F32),
        "hrecv": pltpu.VMEM((NDEV, HP, LANES), F32),
        "hfin": pltpu.VMEM((H, LANES), F32),
        "ld": dma((NS,)),
        "s_xy": dma((L, CH)),
        "r_xy": dma((L, CH)),
        "s_sb": dma((L, CH)),
        "r_sb": dma((L, CH)),
        "s_w": dma((L,)),
        "r_w": dma((L,)),
        "s_ar": dma((8,)),
        "r_ar": dma((8,)),
        "s_rs": dma((L - 1, 2, CH)),
        "r_rs": dma((L - 1, 2, CH)),
        "s_z": dma((L - 1,)),
        "r_z": dma((L - 1,)),
        "s_n": dma((L - 1,)),
        "r_n": dma((L - 1,)),
        "s_f": dma((L,)),
        "r_f": dma((L,)),
        "s_0": dma((1,)),
        "r_0": dma((1,)),
        "s_h": dma((2,)),
        "r_h": dma((2,)),
    }
    ins = ["feat", "adj", "nm", "lb", "lm", "w0", "wr", "npar", "whd", "bias"]
    outs = ["g0", "gr", "gn", "gh", "misc"]
    d.names = ins + outs + list(scratch)
    vmem = pl.BlockSpec(memory_space=pltpu.VMEM)
    specs = [vmem] * len(ins)
    specs[1] = pl.BlockSpec(memory_space=pl.ANY)
    return pl.pallas_call(
        functools.partial(step_kernel, d),
        out_shape=[
            jax.ShapeDtypeStruct(w0.shape, F32),
            jax.ShapeDtypeStruct(wr.shape, F32),
            jax.ShapeDtypeStruct(npar.shape, F32),
            jax.ShapeDtypeStruct(whd.shape, F32),
            jax.ShapeDtypeStruct((8, LANES), F32),
        ],
        in_specs=specs,
        out_specs=[vmem] * len(outs),
        scratch_shapes=list(scratch.values()),
        compiler_params=pltpu.CompilerParams(
            collective_id=0, has_side_effects=True, vmem_limit_bytes=60 * 2**20
        ),
    )(feat, adj, nm, lb, lm, w0, wr, npar, whd, bias)


def adamw(weight, first, second, average, grad, rate):
    first = BETA_ONE * first + (1.0 - BETA_ONE) * grad
    second = BETA_TWO * second + (1.0 - BETA_TWO) * grad * grad
    fix_one = 1.0 - BETA_ONE**ADAM_STEP
    fix_two = 1.0 - BETA_TWO**ADAM_STEP
    update = first / fix_one / (jnp.sqrt(second / fix_two) + ADAM_EPS)
    weight = weight - rate * (update + DECAY * weight)
    average = AVERAGE * average + (1.0 - AVERAGE) * weight
    return (first, second, weight, average)


def local(
    nodes, cols, features, adjacency, node_mask, labels, label_mask,
    weight_first, weight_rest, norm_params, weight_head, bias_head,
    moment_first, moment_rest, moment_norm, moment_head, moment_bias,
    square_first, square_rest, square_norm, square_head, square_bias,
    average_first, average_rest, average_norm, average_head, average_bias,
):
    classes = weight_head.shape[1]
    bias = jnp.pad(bias_head[None, :], ((0, 0), (0, LANES - classes)))
    grad_first, grad_rest, grad_norm_params, grad_head, misc = gradients(
        nodes, cols, features[0], adjacency[0], node_mask, labels, label_mask,
        weight_first, weight_rest, norm_params, weight_head, bias,
    )
    loss_total, label_count, gradient_norm, scale = (misc[i, 0] for i in (0, 1, 2, 4))
    grad_bias = misc[3, :classes]
    first_out = adamw(
        weight_first, moment_first, square_first, average_first, grad_first * scale, RATE_MATRIX
    )
    rest_out = adamw(
        weight_rest, moment_rest, square_rest, average_rest, grad_rest * scale, RATE_MATRIX
    )
    norm_out = adamw(
        norm_params, moment_norm, square_norm, average_norm, grad_norm_params * scale, RATE_SMALL
    )
    head_out = adamw(
        weight_head, moment_head, square_head, average_head, grad_head * scale, RATE_MATRIX
    )
    bias_out = adamw(
        bias_head, moment_bias, square_bias, average_bias, grad_bias * scale, RATE_SMALL
    )
    return (
        loss_total, label_count, gradient_norm,
        *first_out, *rest_out, *norm_out, *head_out, *bias_out,
    )


def solution(mesh):
    rows, first, rest, all_of = P("cols", "nodes", None), P(None, "cols"), P(None, None, "cols"), P()
    state = [first, rest, all_of, all_of, all_of]
    return jax.shard_map(
        functools.partial(local, mesh.shape["nodes"], mesh.shape["cols"]),
        mesh=mesh,
        in_specs=(rows, rows) + (P("cols", "nodes"),) * 3 + tuple(state * 4),
        out_specs=(all_of,) * 3 + tuple(spec for spec in state for _ in range(4)),
        check_vma=False,
    )
```

```python
import functools
import types

import jax
import jax.numpy as jnp
from jax import lax
from jax.experimental import pallas as pl
from jax.experimental.pallas import tpu as pltpu
from jax.sharding import PartitionSpec as P

LAYERS = 3
ADAM_STEP = 10
CLIP = 0.02
RATE_MATRIX = 0.03
RATE_SMALL = 0.3
BETA_ONE = 0.9
BETA_TWO = 0.999
ADAM_EPS = 1e-08
DECAY = 0.01
AVERAGE = 0.9
NORM_EPS = 1e-05

MESH = pl.DeviceIdType.MESH
F32 = jnp.float32
BF16 = jnp.bfloat16
LANES = 128
GELU_OUT = 0.7978845608028654
GELU_CUBE = 0.044715


def cat(values, axis):
    return values[0] if len(values) == 1 else jnp.concatenate(values, axis=axis)


def split(value):
    high = value.astype(BF16)
    return high, (value - high.astype(F32)).astype(BF16)


def dot(left, right):
    return lax.dot_general(left, right, (((1,), (0,)), ((), ())), preferred_element_type=F32)


def dot_t(left, right):
    return lax.dot_general(left, right, (((1,), (1,)), ((), ())), preferred_element_type=F32)


def dot3(left, right):
    (lh, ll), (rh, rl) = left, right
    return dot(cat([lh, lh, ll], 1), cat([rh, rl, rh], 0))


def dot3_t(left, right):
    (lh, ll), (rh, rl) = left, right
    return dot_t(cat([lh, lh, ll], 1), cat([rh, rl, rh], 1))


def remote(src, dst, send, recv, device):
    return pltpu.make_async_remote_copy(
        src_ref=src, dst_ref=dst, send_sem=send, recv_sem=recv, device_id=device, device_id_type=MESH
    )


def wait_bytes(ref, sem):
    pltpu.make_async_copy(ref, ref, sem).wait()


def flip(index, distance):
    bit = 1
    while bit <= distance:
        if distance & bit:
            index = index + (1 - 2 * lax.rem(lax.div(index, bit), 2)) * bit
        bit *= 2
    return index


def step_kernel(d, *refs):
    v = types.SimpleNamespace(**dict(zip(d.names, refs, strict=True)))
    NN, NC, R, H, HC, CH, L = d.NN, d.NC, d.R, d.H, d.HC, d.CH, LAYERS
    NDEV, RPP, PPC, HV, F, FR, CR = d.NDEV, d.RPP, d.PPC, d.HV, d.F, d.FR, d.CR
    n, c = lax.axis_index("nodes"), lax.axis_index("cols")
    me = n * NC + c
    ch, k = lax.div(n, 2), lax.rem(n, 2)
    sib = (ch * 2 + 1 - k, c)
    drains = []

    def device(index):
        return lax.div(index, NC), lax.rem(index, NC)

    def peer(dd):
        return flip(ch, dd) * 2 + k, c

    def rows(i, size):
        return pl.ds(pl.multiple_of(i * size, size), size)

    def send(src, dst, ssem, rsem, dev):
        remote(src, dst, ssem, rsem, dev).start()
        drains.append(lambda: wait_bytes(src, ssem))

    def either(always, condition, fn, other=None):
        if always:
            fn()
        else:
            pl.when(condition)(fn)
            if other is not None:
                pl.when(jnp.logical_not(condition))(other)

    barrier = pltpu.get_barrier_semaphore()

    def greet(i, carry):
        pl.semaphore_signal(
            barrier, inc=1, device_id=device(lax.rem(me + i, NDEV)), device_id_type=MESH
        )
        return carry

    lax.fori_loop(1, NDEV, greet, 0)

    def adj_cols(j, core):
        return v.adj.at[:, rows(j * 2 + core, R)]

    loads = [pltpu.make_async_copy(v.wr.at[i], v.wtr.at[i, rows(c, HC), :], v.ld.at[i]) for i in range(L - 1)]
    for copy in loads:
        copy.start()
    for j in range(CH):
        pltpu.make_async_copy(adj_cols(j, k), v.adjb.at[0, j], v.ld.at[L + j]).start()
    v.xown[:F, :] = v.feat[...]
    v.xown[F:, :] = jnp.ones((FR - F, R), F32)
    v.wt0[rows(c, HC), :] = jnp.zeros((HC, 2 * FR), F32)
    v.wt0[rows(c, HC), :F] = v.w0[:, :F]
    v.wt0[rows(c, HC), FR : FR + F] = v.w0[:, F:]
    pl.semaphore_wait(barrier, NDEV - 1)

    def halves(ref):
        size = ref.shape[0]
        first = -(-size // 16) * 8
        return ref.at[:first], ref.at[first:]

    def ag_send(g, src, buf, part):
        s, r = v.s_ag.at[g], v.r_ag.at[g]
        mine = halves(src)
        slot = halves(buf.at[ch])
        if CH == 4:
            send(mine[part], slot[part], s.at[part], r.at[part], peer(1))
            if part == 1:
                send(mine[1], slot[1], s.at[3], r.at[3], peer(2))
                send(mine[0], slot[0], s.at[2], r.at[2], peer(2))
        elif part == 1:
            for dd in reversed(range(1, CH)):
                send(src, buf.at[ch], s.at[dd], r.at[dd], peer(dd))

    def ag_blocks(g, src, buf, add):
        s, r = v.s_ag.at[g], v.r_ag.at[g]
        for part in range(2):
            add(ch, part, halves(src)[part])
        if CH == 4:
            x, y, z = (halves(buf.at[flip(ch, dd)]) for dd in (1, 2, 3))
            wait_bytes(x[0], r.at[0])
            send(x[0], x[0], s.at[4], r.at[4], peer(2))
            wait_bytes(y[1], r.at[3])
            send(y[1], y[1], s.at[5], r.at[5], peer(1))
            add(flip(ch, 1), 0, x[0])
            add(flip(ch, 2), 1, y[1])
            wait_bytes(x[1], r.at[1])
            add(flip(ch, 1), 1, x[1])
            wait_bytes(y[0], r.at[2])
            add(flip(ch, 2), 0, y[0])
            wait_bytes(z[0], r.at[4])
            add(flip(ch, 3), 0, z[0])
            wait_bytes(z[1], r.at[5])
            add(flip(ch, 3), 1, z[1])
        else:
            for dd in range(1, CH):
                wait_bytes(buf.at[flip(ch, dd)], r.at[dd])
                for part in range(2):
                    add(flip(ch, dd), part, halves(buf.at[flip(ch, dd)])[part])

    def ar_send(a):
        def one(i, carry):
            remote(
                v.arb.at[a, me], v.arb.at[a, me], v.s_ar.at[a], v.r_ar.at[a],
                device(lax.rem(me + i, NDEV)),
            ).start()
            return carry

        lax.fori_loop(1, NDEV, one, 0)
        drains.append(lambda: wait_bytes(v.arb.at[a, pl.ds(0, NDEV - 1)], v.s_ar.at[a]))

    def ar_put(a, vectors):
        at = 0
        for vec in vectors:
            for i in range(vec.shape[1] // LANES):
                v.arb[a, me, at : at + 1, :] = vec[:, i * LANES : (i + 1) * LANES]
                at += 1
        if at < 8:
            v.arb[a, me, at:, :] = jnp.zeros((8 - at, LANES), F32)

    def ar_wait(a):
        wait_bytes(v.arb.at[a, pl.ds(0, NDEV - 1)], v.r_ar.at[a])
        return jnp.sum(v.arb[a], axis=0)

    def vec(total, i):
        return cat([total[i * HV + j : i * HV + j + 1] for j in range(HV)], 1)

    for part in range(2):
        ag_send(0, v.xown, v.xg, part)
    for j in range(CH):
        send(adj_cols(j, 1 - k), v.adjb.at[1, j], v.s_adj.at[j], v.r_adj.at[j], sib)
    for l in range(L):
        if l:
            loads[l - 1].wait()
        ref = v.wt0 if l == 0 else v.wtr.at[l - 1]
        for dd in range(1, NC):
            block = ref.at[rows(c, HC), :]
            remote(block, block, v.s_w.at[l], v.r_w.at[l], (n, lax.rem(c + dd, NC))).start()
        drains.append(lambda ref=ref, l=l: wait_bytes(ref.at[pl.ds(0, (NC - 1) * HC)], v.s_w.at[l]))

    def column(row):
        return jnp.broadcast_to(row.astype(F32), (LANES, R)).T

    v.valid[...] = column(v.nm[...])
    v.counted[...] = column(v.lm[...] * v.nm[...])
    v.label[...] = column(v.lb[...])
    v.whp[...] = jnp.zeros(v.whp.shape, F32)
    v.whp[: d.C, :] = v.whd[...]
    v.biasp[...] = jnp.zeros(v.biasp.shape, F32)
    v.biasp[:, : d.C] = v.bias[...]

    def adj_block(j, side):
        block = v.adjb[side, j].astype(F32)
        v.abf[j, side * R : (side + 1) * R, :] = block.astype(BF16)
        v.at[side, j] = block.T.astype(BF16)

    def adj_own(j, carry):
        pltpu.make_async_copy(adj_cols(j, k), v.adjb.at[0, j], v.ld.at[L + j]).wait()
        adj_block(j, 0)
        return carry

    def adj_sib(j, carry):
        wait_bytes(v.adjb.at[1, j], v.r_adj.at[j])
        adj_block(j, 1)
        return carry

    lax.fori_loop(0, CH, adj_own, 0)
    lax.fori_loop(0, CH, adj_sib, 0)

    def wide(value):
        return cat([value] * HV, 1)

    RC = min(R // 2, 64)
    HALF = R // 2

    def activate(l, part):
        def chunk(i, carry):
            r = rows(i, RC)
            x = v.lin[r, :]
            square = x * x
            t = jnp.tanh(GELU_OUT * x * (1.0 + GELU_CUBE * square))
            half = 0.5 * (1.0 + t)
            act = x * half
            v.acts[l, r, :] = act
            v.gp[l, r, :] = half + (0.5 * GELU_OUT) * x * (1.0 - t * t) * (
                1.0 + (3.0 * GELU_CUBE) * square
            )
            masked = wide(v.valid[r, :]) * act
            return (
                carry[0] + jnp.sum(masked.reshape(RC // 8, 8, H), axis=0),
                carry[1] + jnp.sum((masked * act).reshape(RC // 8, 8, H), axis=0),
            )

        zero = jnp.zeros((8, H), F32)
        per = HALF // RC
        return lax.fori_loop(part * per, (part + 1) * per, chunk, (zero, zero))

    def over_rows(value):
        return jnp.sum(value, axis=0, keepdims=True)

    def keep_stats(l, total):
        count = jnp.max(v.count[0:1, :], axis=1, keepdims=True)
        mean = vec(total, 0) / count
        var = vec(total, 1) / count - mean * mean
        inverse = lax.rsqrt(var + NORM_EPS)
        gain, shift = v.npar[l, 0:1, :], v.npar[l, 1:2, :]
        v.vecs[l, 0:1, :] = mean
        v.vecs[l, 1:2, :] = inverse
        v.vecs[l, 2:3, :] = gain * inverse
        v.vecs[l, 3:4, :] = shift - mean * (gain * inverse)

    def finish(l, part_lin):
        sums = []
        for part in range(2):
            part_lin(part)
            sums.append(activate(l, part))
            if l < L - 1:
                ag_send(l + 1, v.acts.at[l], v.ag.at[l], part)
        message = [over_rows(sums[0][i] + sums[1][i]) for i in range(2)]
        if l == 0:
            message += [over_rows(v.valid[...]), over_rows(v.counted[...])]
        ar_put(l, message)
        ar_send(l)

    first_rows = len(drains)
    def add_first(chip, part, ref):
        high, low = split(ref[...])
        a = v.abf[chip]
        got = dot_t(cat([high, low], 1), cat([a, a], 1))
        first = -(-FR // 16) * 8
        r = slice(0, first) if part == 0 else slice(first, FR)
        seen = v.aggt[r, :]
        v.aggt[r, :] = seen + got

    v.aggt[...] = jnp.zeros((FR, 2 * R), F32)
    ag_blocks(0, v.xown, v.xg, add_first)
    v.part0[...] = v.aggt[:, R:]
    send(v.part0, v.part0r, v.s_sib.at[0], v.r_sib.at[0], sib)
    wait_bytes(v.wt0.at[pl.ds(0, (NC - 1) * HC)], v.r_w.at[0])
    v.w0h[...], v.w0l[...] = split(v.wt0[...])
    feature = lax.broadcasted_iota(jnp.int32, (FR, R), 0) < F
    v.in0h[:FR, :], v.in0l[:FR, :] = split(jnp.where(feature, v.xown[...], 0.0))
    wait_bytes(v.part0r, v.r_sib.at[0])
    total = v.aggt[:, :R] + v.part0r[...]
    degree = total[F : F + 1, :]
    v.in0h[FR:, :], v.in0l[FR:, :] = split(
        jnp.where(feature, total * (1.0 / jnp.maximum(degree, 1.0)), 0.0)
    )
    v.lin[...] = dot3((v.w0h[...], v.w0l[...]), (v.in0h[...], v.in0l[...])).T
    finish(0, lambda part: None)
    degree = column(degree)
    v.degree[...] = degree
    v.linked[...] = jnp.minimum(degree, 1.0)
    v.invdeg[...] = 1.0 / jnp.maximum(degree, 1.0)

    for l in range(1, L):
        wait_bytes(v.wtr.at[l - 1, pl.ds(0, (NC - 1) * HC)], v.r_w.at[l])
        v.wh[l - 1], v.wl[l - 1] = split(v.wtr[l - 1])
        total = ar_wait(l - 1)
        if l == 1:
            v.count[...] = total[2 * HV : 2 * HV + 2]
        keep_stats(l - 1, total)
        scale, shift = v.vecs[l - 1, 2:3, :], v.vecs[l - 1, 3:4, :]
        v.inh[l - 1, :, :H], v.inl[l - 1, :, :H] = split(v.acts[l - 1] * scale + shift)
        v.lin[...] = dot3_t(
            (v.inh[l - 1, :, :H], v.inl[l - 1, :, :H]), (v.wh[l - 1, :, :H], v.wl[l - 1, :, :H])
        )
        v.agg[...] = jnp.zeros((2 * R, H), F32)

        def add(chip, part, ref):
            high, low = split(ref[...])
            a = v.abf[chip, :, part * HALF : (part + 1) * HALF]
            v.agg[...] += dot(cat([a, a], 1), cat([high, low], 0))

        ag_blocks(l, v.acts.at[l - 1], v.ag.at[l - 1], add)
        v.parts[l - 1] = v.agg[R:, :]
        send(v.parts.at[l - 1], v.partr.at[l - 1], v.s_sib.at[l], v.r_sib.at[l], sib)
        wait_bytes(v.partr.at[l - 1], v.r_sib.at[l])

        def part_lin(part):
            r = slice(part * HALF, (part + 1) * HALF)
            agg = v.agg[r, :] + v.partr[l - 1, r, :]
            v.kept[l - 1, r, :] = agg
            v.inh[l - 1, r, H:], v.inl[l - 1, r, H:] = split(
                agg * wide(v.invdeg[r, :]) * scale + wide(v.linked[r, :]) * shift
            )
            v.lin[r, :] += dot3_t(
                (v.inh[l - 1, r, H:], v.inl[l - 1, r, H:]), (v.wh[l - 1, :, H:], v.wl[l - 1, :, H:])
            )

        finish(l, part_lin)

    for drain in drains[first_rows:]:
        drain()
    del drains[first_rows:]

    head = split(v.whp[...])
    lane = lax.broadcasted_iota(jnp.int32, (R, LANES), 1)
    onehot = jnp.where(lane.astype(F32) == v.label[...], 1.0, 0.0)
    real = lane < d.C
    counted = v.counted[...]
    label_count = jnp.max(v.count[1:2, :], axis=1, keepdims=True)
    keep_stats(L - 1, ar_wait(L - 1))
    last = split(v.acts[L - 1] * v.vecs[L - 1, 2:3, :] + v.vecs[L - 1, 3:4, :])
    logits = dot3_t(last, head) + v.biasp[...]
    top = jnp.max(jnp.where(real, logits, -3.0e38), axis=1, keepdims=True)
    moved = logits - top
    power = jnp.where(real, jnp.exp(moved), 0.0)
    power_sum = jnp.sum(power, axis=1, keepdims=True)
    g_logits = counted * (power / power_sum - onehot) / label_count
    gl_split = split(g_logits)
    v.gout[...] = dot3(gl_split, head)

    def last_sums():
        mean, inverse = v.vecs[L - 1, 0:1, :], v.vecs[L - 1, 1:2, :]

        def chunk(i, carry):
            r = rows(i, RC)
            g = v.gout[r, :]
            normed = (v.acts[L - 1, r, :] - mean) * inverse
            return (
                carry[0] + jnp.sum((g * normed).reshape(RC // 8, 8, H), axis=0),
                carry[1] + jnp.sum(g.reshape(RC // 8, 8, H), axis=0),
            )

        zero = jnp.zeros((8, H), F32)
        return [over_rows(s) for s in lax.fori_loop(0, R // RC, chunk, (zero, zero))]

    ar_put(3, last_sums())
    ar_send(3)
    logp = moved - jnp.log(power_sum)
    rows_loss = jnp.sum(jnp.where(real, onehot * logp, 0.0), axis=1, keepdims=True) * counted
    ar_put(6, [-over_rows(rows_loss), over_rows(g_logits)])
    ar_send(6)
    head_grad = dot3(split(g_logits.T[:CR, :]), last)
    HT = d.HT
    for t in range(HT):
        i, j = t // HV, t % HV
        v.hg[t] = head_grad[8 * i : 8 * i + 8, j * LANES : (j + 1) * LANES]

    def others(index, size, ref_of, init):
        return lax.fori_loop(1, size, lambda i, s: s + ref_of(lax.rem(index + i, size)), init)

    def head_scatter(i, carry):
        t = lax.rem(me + i, NDEV)

        def go():
            remote(v.hg.at[t], v.hrecv.at[me], v.s_h.at[0], v.r_h.at[0], device(t)).start()

        either(HT == NDEV, t < HT, go)
        return carry

    lax.fori_loop(1, NDEV, head_scatter, 0)
    drains.append(
        lambda: either(
            HT == NDEV,
            me < HT,
            lambda: wait_bytes(v.hrecv.at[pl.ds(0, HT - 1)], v.s_h.at[0]),
            lambda: wait_bytes(v.hrecv.at[pl.ds(0, HT)], v.s_h.at[0]),
        )
    )

    def head_gather():
        def go():
            wait_bytes(v.hrecv.at[pl.ds(0, NDEV - 1)], v.r_h.at[0])
            v.hfin[me] = others(me, NDEV, lambda s: v.hrecv[s], v.hg[me])

            def one(i, carry):
                remote(
                    v.hfin.at[me], v.hfin.at[me], v.s_h.at[1], v.r_h.at[1],
                    device(lax.rem(me + i, NDEV)),
                ).start()
                return carry

            lax.fori_loop(1, NDEV, one, 0)

        either(HT == NDEV, me < HT, go)
        drains.append(
            lambda: either(
                HT == NDEV,
                me < HT,
                lambda: wait_bytes(v.hrecv.at[pl.ds(0, NDEV - 1)], v.s_h.at[1]),
            )
        )

    def cols_send(i):
        for dd in range(1, NC):
            t = lax.rem(c + dd, NC)
            remote(v.dwb.at[i, t], v.zrecv.at[i, c], v.s_z.at[i], v.r_z.at[i], (n, t)).start()
        drains.append(lambda: wait_bytes(v.zrecv.at[i, pl.ds(0, NC - 1)], v.s_z.at[i]))

    def nodes_send(i):
        wait_bytes(v.zrecv.at[i, pl.ds(0, NC - 1)], v.r_z.at[i])
        v.zs[i] = others(c, NC, lambda s: v.zrecv[i, s], v.dwb[i, c])

        def one(j, carry):
            t = lax.rem(n + j, NN)
            either(
                PPC == NN,
                t < PPC,
                lambda: remote(
                    v.zs.at[i, rows(t, RPP), :], v.nrecv.at[i, n], v.s_n.at[i], v.r_n.at[i], (t, c)
                ).start(),
            )
            return carry

        lax.fori_loop(1, NN, one, 0)
        drains.append(
            lambda: either(
                PPC == NN,
                n < PPC,
                lambda: wait_bytes(v.nrecv.at[i, pl.ds(0, PPC - 1)], v.s_n.at[i]),
                lambda: wait_bytes(v.nrecv.at[i, pl.ds(0, PPC)], v.s_n.at[i]),
            )
        )

    def pieces_out(i, fin, piece):
        fin[rows(n, RPP), :] = piece
        square = jnp.sum((piece * piece).reshape(RPP // 8, 8, piece.shape[1]), axis=0)
        v.sq[...] += jnp.sum(square, axis=1, keepdims=True)

        def one(j, carry):
            block = fin.at[rows(n, RPP), :]
            remote(block, block, v.s_f.at[i], v.r_f.at[i], (lax.rem(n + j, NN), c)).start()
            return carry

        lax.fori_loop(1, NN, one, 0)

    def pieces_drain(i, like):
        drains.append(
            lambda: either(
                PPC == NN, n < PPC, lambda: wait_bytes(like.at[pl.ds(0, NN - 1)], v.s_f.at[i])
            )
        )

    def nodes_gather(i):
        def go():
            wait_bytes(v.nrecv.at[i, pl.ds(0, NN - 1)], v.r_n.at[i])
            piece = others(n, NN, lambda s: v.nrecv[i, s], v.zs[i, rows(n, RPP), :])
            pieces_out(i, v.fin.at[i], piece)

        either(PPC == NN, n < PPC, go)
        pieces_drain(i, v.nrecv.at[i])

    v.sq[...] = jnp.zeros((8, LANES), F32)

    def linear_grad(l, a):
        total = ar_wait(a)
        g_gain, g_shift = vec(total, 0), vec(total, 1)
        v.gn[l, 0:1, :] = g_gain
        v.gn[l, 1:2, :] = g_shift
        mean, inverse, scale = v.vecs[l, 0:1, :], v.vecs[l, 1:2, :], v.vecs[l, 2:3, :]
        count = jnp.max(v.count[0:1, :], axis=1, keepdims=True)
        by_one = scale * g_shift / count
        by_normed = scale * g_gain / count

        def chunk(i, carry):
            r = rows(i, RC)
            normed = (v.acts[l, r, :] - mean) * inverse
            g_active = scale * v.gout[r, :] - wide(v.valid[r, :]) * (by_one + normed * by_normed)
            g_linear = v.gp[l, r, :] * g_active
            v.lin[r, :] = g_linear
            v.glh[r, :], v.gll[r, :] = split(g_linear)
            return carry

        lax.fori_loop(0, R // RC, chunk, 0)

    for l in (2, 1):
        g = l - 1
        linear_grad(l, 5 - l)
        gl = (v.glh[...], v.gll[...])
        back = v.ag.at[2 - l]
        v.spread[...] = dot3(gl, (v.wh[g, :, H:], v.wl[g, :, H:])) * wide(v.invdeg[...])
        v.spreads[g] = v.spread[...]
        send(v.spreads.at[g], v.spreadr.at[g], v.s_sib.at[L + g], v.r_sib.at[L + g], sib)
        if g == 0:
            for drain in scatter_drains:
                drain()
        own = cat(list(split(v.spread[...])), 0)
        for dd in reversed(range(CH)):
            t = v.at[0, flip(ch, dd)]
            v.out[dd] = dot(cat([t, t], 1), own)
        wait_bytes(v.spreadr.at[g], v.r_sib.at[L + g])
        other = cat(list(split(v.spreadr[g])), 0)

        def complete(dd):
            t = v.at[1, flip(ch, dd)]
            v.out[dd] += dot(cat([t, t], 1), other)

        s, r = v.s_rs.at[g], v.r_rs.at[g]
        kept_drains, drains = drains, []
        if CH == 4:
            x, y, z = (halves(v.out.at[dd]) for dd in (1, 2, 3))
            from_x, from_y, via = (halves(back.at[i]) for i in range(3))
            complete(3)
            send(z[0], via[0], s.at[0], r.at[0], peer(1))
            send(z[1], via[1], s.at[1], r.at[1], peer(2))
            complete(1)
            send(x[0], from_x[0], s.at[2], r.at[2], peer(1))
            complete(2)
            send(y[1], from_y[1], s.at[3], r.at[3], peer(2))
            complete(0)
            wait_bytes(via[0], r.at[0])
            y[0][...] += via[0][...]
            send(y[0], from_y[0], s.at[5], r.at[5], peer(2))
            wait_bytes(via[1], r.at[1])
            x[1][...] += via[1][...]
            send(x[1], from_x[1], s.at[4], r.at[4], peer(1))
        else:
            for dd in reversed(range(1, CH)):
                complete(dd)
                send(v.out.at[dd], back.at[dd], s.at[dd], r.at[dd], peer(dd))
            complete(0)
        scatter_drains, drains = drains, kept_drains

        v.gout[...] = dot3(gl, (v.wh[g, :, :H], v.wl[g, :, :H]))
        mean, inverse = v.vecs[g, 0:1, :], v.vecs[g, 1:2, :]

        def chunk(i, carry):
            r = rows(i, RC)
            self, spread, degree = v.gout[r, :], v.spread[r, :], wide(v.degree[r, :])
            normed = (v.acts[g, r, :] - mean) * inverse
            reached = (v.kept[g, r, :] - degree * mean) * inverse
            v.gout[r, :] = self + v.out[0, r, :]
            return (
                carry[0] + jnp.sum((self * normed + spread * reached).reshape(RC // 8, 8, H), axis=0),
                carry[1] + jnp.sum((self + spread * degree).reshape(RC // 8, 8, H), axis=0),
            )

        zero = jnp.zeros((8, H), F32)
        ar_put(6 - l, [over_rows(s) for s in lax.fori_loop(0, R // RC, chunk, (zero, zero))])
        ar_send(6 - l)
        if l == 1:
            nodes_send(1)
        grad = dot3(split(v.lin[...].T), (v.inh[g], v.inl[g]))
        for t in range(NC):
            v.dwb[g, t] = grad[t * HC : (t + 1) * HC, :]
        cols_send(g)
        if l == 1:
            head_gather()
        if CH == 4:
            for half, i in ((from_x[0], 2), (from_y[1], 3), (from_y[0], 5), (from_x[1], 4)):
                wait_bytes(half, r.at[i])
            v.gout[...] += back[0] + back[1]
        else:
            for dd in range(1, CH):
                wait_bytes(back.at[dd], r.at[dd])
                v.gout[...] += back[dd]
    drains += scatter_drains

    linear_grad(0, 5)
    grad = dot3_t(split(v.lin[...].T), (v.in0h[...], v.in0l[...]))
    for t in range(NC):
        v.d0[t] = grad[t * HC : (t + 1) * HC, :]

    def first_scatter(i, carry):
        tn, tc = device(lax.rem(me + i, NDEV))
        either(
            PPC == NN,
            tn < PPC,
            lambda: remote(
                v.d0.at[tc, rows(tn, RPP), :], v.recv0.at[me], v.s_0.at[0], v.r_0.at[0], (tn, tc)
            ).start(),
        )
        return carry

    lax.fori_loop(1, NDEV, first_scatter, 0)
    drains.append(
        lambda: either(
            PPC == NN,
            n < PPC,
            lambda: wait_bytes(v.recv0.at[pl.ds(0, PPC * NC - 1)], v.s_0.at[0]),
            lambda: wait_bytes(v.recv0.at[pl.ds(0, PPC * NC)], v.s_0.at[0]),
        )
    )
    nodes_send(0)
    nodes_gather(1)
    nodes_gather(0)

    def first_gather():
        wait_bytes(v.recv0.at[pl.ds(0, NDEV - 1)], v.r_0.at[0])
        piece = others(me, NDEV, lambda s: v.recv0[s], v.d0[c, rows(n, RPP), :])
        pieces_out(L - 1, v.fin0, piece)

    either(PPC == NN, n < PPC, first_gather)
    pieces_drain(L - 1, v.recv0)
    ar_put(7, [over_rows(v.sq[...])])
    ar_send(7)

    total = ar_wait(6)
    bias_grad = total[1:2]
    v.misc[...] = jnp.zeros((8, LANES), F32)
    v.misc[0:1, :] = total[0:1]
    v.misc[1:2, :] = v.count[1:2, :]
    v.misc[3:4, :] = bias_grad

    def fin_wait(i, fin):
        either(
            PPC == NN,
            n < PPC,
            lambda: wait_bytes(fin.at[pl.ds(0, (PPC - 1) * RPP), :], v.r_f.at[i]),
            lambda: wait_bytes(fin.at[pl.ds(0, PPC * RPP), :], v.r_f.at[i]),
        )

    either(
        HT == NDEV,
        me < HT,
        lambda: wait_bytes(v.hfin.at[pl.ds(0, HT - 1)], v.r_h.at[1]),
        lambda: wait_bytes(v.hfin.at[pl.ds(0, HT)], v.r_h.at[1]),
    )
    square = jnp.zeros((8, LANES), F32)
    for t in range(HT):
        i, j = t // HV, t % HV
        tile = v.hfin[t]
        v.gh[8 * i : 8 * i + 8, j * LANES : (j + 1) * LANES] = tile
        square += tile * tile
    replicated = over_rows(square) + bias_grad * bias_grad
    small = jnp.zeros((1, H), F32)
    for l in range(L):
        small += over_rows(v.gn[l] * v.gn[l])
    for j in range(HV):
        replicated += small[:, j * LANES : (j + 1) * LANES]

    for i in range(L - 1):
        fin_wait(i, v.fin.at[i])
        v.gr[i] = v.fin[i]
    total = ar_wait(7)
    squares = total[0:1, 0:1] + jnp.sum(replicated, axis=1, keepdims=True)
    norm = jnp.sqrt(squares)
    v.misc[2:3, :] = jnp.broadcast_to(norm, (1, LANES))
    v.misc[4:5, :] = jnp.broadcast_to(CLIP / jnp.maximum(norm, CLIP), (1, LANES))
    fin_wait(L - 1, v.fin0)
    v.g0[:, :F] = v.fin0[:, :F]
    v.g0[:, F:] = v.fin0[:, FR : FR + F]

    for drain in drains:
        drain()


def gradients(NN, NC, feat, adj, nm, lb, lm, w0, wr, npar, whd, bias):
    F, R = feat.shape
    C, H = whd.shape
    HC = w0.shape[0]
    CH, NDEV = NN // 2, NN * NC
    up = lambda size: -(-size // 8) * 8
    FR, CR = up(F + 1), up(C)
    RPP = max(8, HC // NN)
    HV = H // LANES
    d = types.SimpleNamespace(
        NN=NN, NC=NC, R=R, F=F, H=H, C=C, HC=HC, CH=CH, NDEV=NDEV, FR=FR, CR=CR, RPP=RPP,
        PPC=HC // RPP, HV=HV, HT=CR // 8 * HV,
    )
    dma = pltpu.SemaphoreType.DMA
    L = LAYERS
    scratch = {
        "xown": pltpu.VMEM((FR, R), F32),
        "xg": pltpu.VMEM((CH, FR, R), F32),
        "ag": pltpu.VMEM((L - 1, CH, R, H), F32),
        "acts": pltpu.VMEM((L, R, H), F32),
        "gp": pltpu.VMEM((L, R, H), F32),
        "adjb": pltpu.VMEM((2, CH, R, R), jnp.int32),
        "abf": pltpu.VMEM((CH, 2 * R, R), BF16),
        "at": pltpu.VMEM((2, CH, R, R), BF16),
        "wt0": pltpu.VMEM((H, 2 * FR), F32),
        "wtr": pltpu.VMEM((L - 1, H, 2 * H), F32),
        "w0h": pltpu.VMEM((H, 2 * FR), BF16),
        "w0l": pltpu.VMEM((H, 2 * FR), BF16),
        "wh": pltpu.VMEM((L - 1, H, 2 * H), BF16),
        "wl": pltpu.VMEM((L - 1, H, 2 * H), BF16),
        "whp": pltpu.VMEM((LANES, H), F32),
        "biasp": pltpu.VMEM((1, LANES), F32),
        "in0h": pltpu.VMEM((2 * FR, R), BF16),
        "in0l": pltpu.VMEM((2 * FR, R), BF16),
        "inh": pltpu.VMEM((L - 1, R, 2 * H), BF16),
        "inl": pltpu.VMEM((L - 1, R, 2 * H), BF16),
        "aggt": pltpu.VMEM((FR, 2 * R), F32),
        "part0": pltpu.VMEM((FR, R), F32),
        "part0r": pltpu.VMEM((FR, R), F32),
        "agg": pltpu.VMEM((2 * R, H), F32),
        "parts": pltpu.VMEM((L - 1, R, H), F32),
        "partr": pltpu.VMEM((L - 1, R, H), F32),
        "kept": pltpu.VMEM((L - 1, R, H), F32),
        "lin": pltpu.VMEM((R, H), F32),
        "gout": pltpu.VMEM((R, H), F32),
        "glh": pltpu.VMEM((R, H), BF16),
        "gll": pltpu.VMEM((R, H), BF16),
        "spread": pltpu.VMEM((R, H), F32),
        "spreads": pltpu.VMEM((L - 1, R, H), F32),
        "spreadr": pltpu.VMEM((L - 1, R, H), F32),
        "out": pltpu.VMEM((CH, R, H), F32),
        "valid": pltpu.VMEM((R, LANES), F32),
        "counted": pltpu.VMEM((R, LANES), F32),
        "label": pltpu.VMEM((R, LANES), F32),
        "degree": pltpu.VMEM((R, LANES), F32),
        "invdeg": pltpu.VMEM((R, LANES), F32),
        "linked": pltpu.VMEM((R, LANES), F32),
        "count": pltpu.VMEM((2, LANES), F32),
        "vecs": pltpu.VMEM((L, 8, H), F32),
        "sq": pltpu.VMEM((8, LANES), F32),
        "arb": pltpu.VMEM((8, NDEV, 8, LANES), F32),
        "dwb": pltpu.VMEM((L - 1, NC, HC, 2 * H), F32),
        "zrecv": pltpu.VMEM((L - 1, NC, HC, 2 * H), F32),
        "zs": pltpu.VMEM((L - 1, HC, 2 * H), F32),
        "nrecv": pltpu.VMEM((L - 1, NN, RPP, 2 * H), F32),
        "fin": pltpu.VMEM((L - 1, HC, 2 * H), F32),
        "d0": pltpu.VMEM((NC, HC, 2 * FR), F32),
        "recv0": pltpu.VMEM((NDEV, RPP, 2 * FR), F32),
        "fin0": pltpu.VMEM((HC, 2 * FR), F32),
        "hg": pltpu.VMEM((d.HT, 8, LANES), F32),
        "hrecv": pltpu.VMEM((NDEV, 8, LANES), F32),
        "hfin": pltpu.VMEM((d.HT, 8, LANES), F32),
        "ld": dma((L + CH,)),
        "s_adj": dma((CH,)),
        "r_adj": dma((CH,)),
        "s_ag": dma((L, max(CH, 6))),
        "r_ag": dma((L, max(CH, 6))),
        "s_sib": dma((2 * L - 1,)),
        "r_sib": dma((2 * L - 1,)),
        "s_w": dma((L,)),
        "r_w": dma((L,)),
        "s_ar": dma((8,)),
        "r_ar": dma((8,)),
        "s_rs": dma((L - 1, max(CH, 6))),
        "r_rs": dma((L - 1, max(CH, 6))),
        "s_z": dma((L - 1,)),
        "r_z": dma((L - 1,)),
        "s_n": dma((L - 1,)),
        "r_n": dma((L - 1,)),
        "s_f": dma((L,)),
        "r_f": dma((L,)),
        "s_0": dma((1,)),
        "r_0": dma((1,)),
        "s_h": dma((2,)),
        "r_h": dma((2,)),
    }
    ins = ["feat", "adj", "nm", "lb", "lm", "w0", "wr", "npar", "whd", "bias"]
    outs = ["g0", "gr", "gn", "gh", "misc"]
    d.names = ins + outs + list(scratch)
    vmem = pl.BlockSpec(memory_space=pltpu.VMEM)
    specs = [vmem] * len(ins)
    for name in ("adj", "wr"):
        specs[ins.index(name)] = pl.BlockSpec(memory_space=pl.ANY)
    return pl.pallas_call(
        functools.partial(step_kernel, d),
        out_shape=[
            jax.ShapeDtypeStruct(w0.shape, F32),
            jax.ShapeDtypeStruct(wr.shape, F32),
            jax.ShapeDtypeStruct(npar.shape, F32),
            jax.ShapeDtypeStruct((CR, H), F32),
            jax.ShapeDtypeStruct((8, LANES), F32),
        ],
        in_specs=specs,
        out_specs=[vmem] * len(outs),
        scratch_shapes=list(scratch.values()),
        compiler_params=pltpu.CompilerParams(
            collective_id=0, has_side_effects=True, vmem_limit_bytes=60 * 2**20
        ),
    )(feat, adj, nm, lb, lm, w0, wr, npar, whd, bias)


def adamw(weight, first, second, average, grad, rate):
    first = BETA_ONE * first + (1.0 - BETA_ONE) * grad
    second = BETA_TWO * second + (1.0 - BETA_TWO) * grad * grad
    fix_one = 1.0 - BETA_ONE**ADAM_STEP
    fix_two = 1.0 - BETA_TWO**ADAM_STEP
    update = first / fix_one / (jnp.sqrt(second / fix_two) + ADAM_EPS)
    weight = weight - rate * (update + DECAY * weight)
    average = AVERAGE * average + (1.0 - AVERAGE) * weight
    return (first, second, weight, average)


def update_kernel(*refs):
    grads, state, scalars, results = refs[:5], refs[5:25], refs[25:28], refs[28:]
    misc = grads[4]
    scale = misc[4:5, 0:1]
    for i in range(3):
        scalars[i][...] = misc[i : i + 1, 0:1]
    for group in range(5):
        weight, first, second, average = (state[group + 5 * i] for i in (0, 1, 2, 3))
        rate = RATE_SMALL if group in (2, 4) else RATE_MATRIX
        shape = weight.shape
        if group == 4:
            grad = misc[3:4, : shape[1]]
        elif group == 3:
            grad = grads[3][: shape[0], :]
        else:
            grad = grads[group][...]
        done = adamw(weight[...], first[...], second[...], average[...], grad * scale, rate)
        for ref, value in zip(results[4 * group : 4 * group + 4], done, strict=True):
            ref[...] = value


def local(
    nodes, cols, features, adjacency, node_mask, labels, label_mask, *state
):
    turn = (
        lambda a: a.T,
        lambda a: a.transpose(0, 2, 1),
        lambda a: a.transpose(1, 0, 2),
        lambda a: a.T,
        lambda a: a.reshape(1, -1),
    )
    back = turn[:4] + (lambda a: a.reshape(-1),)
    state = [turn[i % 5](a) for i, a in enumerate(state)]
    grads = gradients(
        nodes, cols, features[0].T, adjacency[0], node_mask, labels, label_mask, *state[:5]
    )
    outs = [jax.ShapeDtypeStruct((1, 1), F32)] * 3
    outs += [jax.ShapeDtypeStruct(a.shape, F32) for a in state[:5] for _ in range(4)]
    done = pl.pallas_call(update_kernel, out_shape=outs)(*grads, *state)
    return (
        *(a.reshape(()) for a in done[:3]),
        *(back[i // 4](a) for i, a in enumerate(done[3:])),
    )


def solution(mesh):
    rows, first, rest, all_of = P("cols", "nodes", None), P(None, "cols"), P(None, None, "cols"), P()
    state = [first, rest, all_of, all_of, all_of]
    return jax.shard_map(
        functools.partial(local, mesh.shape["nodes"], mesh.shape["cols"]),
        mesh=mesh,
        in_specs=(rows, rows) + (P("cols", "nodes"),) * 3 + tuple(state * 4),
        out_specs=(all_of,) * 3 + tuple(spec for spec in state for _ in range(4)),
        check_vma=False,
    )
```

```python
import functools
import types

import jax
import jax.numpy as jnp
from jax import lax
from jax.experimental import pallas as pl
from jax.experimental.pallas import tpu as pltpu
from jax.sharding import PartitionSpec as P

LAYERS = 3
ADAM_STEP = 10
CLIP = 0.02
RATE_MATRIX = 0.03
RATE_SMALL = 0.3
BETA_ONE = 0.9
BETA_TWO = 0.999
ADAM_EPS = 1e-08
DECAY = 0.01
AVERAGE = 0.9
NORM_EPS = 1e-05

MESH = pl.DeviceIdType.MESH
F32 = jnp.float32
BF16 = jnp.bfloat16
LANES = 128
GELU_OUT = 0.7978845608028654
GELU_CUBE = 0.044715


def cat(values, axis):
    return values[0] if len(values) == 1 else jnp.concatenate(values, axis=axis)


def split(value):
    high = value.astype(BF16)
    return high, (value - high.astype(F32)).astype(BF16)


def dot(left, right):
    return lax.dot_general(left, right, (((1,), (0,)), ((), ())), preferred_element_type=F32)


def dot_t(left, right):
    return lax.dot_general(left, right, (((1,), (1,)), ((), ())), preferred_element_type=F32)


def dot3(left, right):
    (lh, ll), (rh, rl) = left, right
    return dot(cat([lh, lh, ll], 1), cat([rh, rl, rh], 0))


def dot3_t(left, right):
    (lh, ll), (rh, rl) = left, right
    return dot_t(cat([lh, lh, ll], 1), cat([rh, rl, rh], 1))


def remote(src, dst, send, recv, device):
    return pltpu.make_async_remote_copy(
        src_ref=src, dst_ref=dst, send_sem=send, recv_sem=recv, device_id=device, device_id_type=MESH
    )


def wait_bytes(ref, sem):
    pltpu.make_async_copy(ref, ref, sem).wait()


def flip(index, distance):
    bit = 1
    while bit <= distance:
        if distance & bit:
            index = index + (1 - 2 * lax.rem(lax.div(index, bit), 2)) * bit
        bit *= 2
    return index


def step_kernel(d, *refs):
    v = types.SimpleNamespace(**dict(zip(d.names, refs, strict=True)))
    NN, NC, R, H, HC, CH, L = d.NN, d.NC, d.R, d.H, d.HC, d.CH, LAYERS
    NDEV, RPP, PPC, PH, HV, F, FR, CR = d.NDEV, d.RPP, d.PPC, d.PH, d.HV, d.F, d.FR, d.CR
    n, c = lax.axis_index("nodes"), lax.axis_index("cols")
    me = n * NC + c
    ch, k = lax.div(n, 2), lax.rem(n, 2)
    sib = (ch * 2 + 1 - k, c)
    drains = []

    def device(index):
        return lax.div(index, NC), lax.rem(index, NC)

    def peer(dd):
        return flip(ch, dd) * 2 + k, c

    def rows(i, size):
        return pl.ds(pl.multiple_of(i * size, size), size)

    def send(src, dst, ssem, rsem, dev):
        remote(src, dst, ssem, rsem, dev).start()
        drains.append(lambda: wait_bytes(src, ssem))

    def either(always, condition, fn, other=None):
        if always:
            fn()
            return

        @pl.when(condition)
        def _():
            fn()

        if other is not None:

            @pl.when(jnp.logical_not(condition))
            def _():
                other()

    barrier = pltpu.get_barrier_semaphore()

    def greet(i, carry):
        pl.semaphore_signal(
            barrier, inc=1, device_id=device(lax.rem(me + i, NDEV)), device_id_type=MESH
        )
        return carry

    lax.fori_loop(1, NDEV, greet, 0)

    def adj_cols(j, core):
        return v.adj.at[:, rows(j * 2 + core, R)]

    own_rows = rows(c, HC)
    w_loads = [
        pltpu.make_async_copy(v.wr.at[i], v.wtr.at[i, own_rows, :], v.ld.at[i]) for i in range(L - 1)
    ]
    small_loads = [
        pltpu.make_async_copy(getattr(v, name), getattr(v, name + "_in"), v.ld.at[L - 1 + i])
        for i, name in enumerate(d.small)
    ]
    for copy in small_loads + w_loads:
        copy.start()
    base = L - 1 + len(d.small)
    for j in range(CH):
        pltpu.make_async_copy(adj_cols(j, k), v.adjb.at[0, j], v.ld.at[base + j]).start()
    for copy in small_loads:
        copy.wait()
    v.xown[:F, :] = v.feat_in[...]
    v.xown[F:, :] = jnp.ones((FR - F, R), F32)
    v.wt0[own_rows, :] = jnp.zeros((HC, 2 * FR), F32)
    v.wt0[own_rows, :F] = v.w0_in[:, :F]
    v.wt0[own_rows, FR : FR + F] = v.w0_in[:, F:]
    pl.semaphore_wait(barrier, NDEV - 1)

    def halves(ref):
        size = ref.shape[0]
        first = -(-size // 16) * 8
        return ref.at[:first], ref.at[first:]

    def ag_send(g, src, buf, part):
        s, r = v.s_ag.at[g], v.r_ag.at[g]
        mine = halves(src)
        slot = halves(buf.at[ch])
        if CH == 4:
            send(mine[part], slot[part], s.at[part], r.at[part], peer(1))
            if part == 1:
                send(mine[1], slot[1], s.at[3], r.at[3], peer(2))
                send(mine[0], slot[0], s.at[2], r.at[2], peer(2))
        elif part == 1:
            for dd in reversed(range(1, CH)):
                send(src, buf.at[ch], s.at[dd], r.at[dd], peer(dd))

    def ag_forward(g, buf):
        s, r = v.s_ag.at[g], v.r_ag.at[g]
        if CH == 4:
            x, y = (halves(buf.at[flip(ch, dd)]) for dd in (1, 2))
            wait_bytes(x[0], r.at[0])
            send(x[0], x[0], s.at[4], r.at[4], peer(2))
            wait_bytes(y[1], r.at[3])
            send(y[1], y[1], s.at[5], r.at[5], peer(1))

    def ag_blocks(g, buf, add):
        r = v.r_ag.at[g]
        if CH == 4:
            x, y, z = (halves(buf.at[flip(ch, dd)]) for dd in (1, 2, 3))
            add(flip(ch, 1), 0, x[0])
            add(flip(ch, 2), 1, y[1])
            wait_bytes(x[1], r.at[1])
            add(flip(ch, 1), 1, x[1])
            wait_bytes(y[0], r.at[2])
            add(flip(ch, 2), 0, y[0])
            wait_bytes(z[0], r.at[4])
            add(flip(ch, 3), 0, z[0])
            wait_bytes(z[1], r.at[5])
            add(flip(ch, 3), 1, z[1])
        else:
            for dd in range(1, CH):
                wait_bytes(buf.at[flip(ch, dd)], r.at[dd])
                for part in range(2):
                    add(flip(ch, dd), part, halves(buf.at[flip(ch, dd)])[part])

    def ar_send(a):
        def one(i, carry):
            remote(
                v.arb.at[a, me], v.arb.at[a, me], v.s_ar.at[a], v.r_ar.at[a],
                device(lax.rem(me + i, NDEV)),
            ).start()
            return carry

        lax.fori_loop(1, NDEV, one, 0)
        drains.append(lambda: wait_bytes(v.arb.at[a, pl.ds(0, NDEV - 1)], v.s_ar.at[a]))

    def ar_put(a, vectors):
        at = 0
        for vec in vectors:
            for i in range(vec.shape[1] // LANES):
                v.arb[a, me, at : at + 1, :] = vec[:, i * LANES : (i + 1) * LANES]
                at += 1
        if at < 4:
            v.arb[a, me, at:, :] = jnp.zeros((4 - at, LANES), F32)

    def ar_wait(a):
        wait_bytes(v.arb.at[a, pl.ds(0, NDEV - 1)], v.r_ar.at[a])
        return jnp.sum(v.arb[a], axis=0)

    def vec(total, i):
        return cat([total[i * HV + j : i * HV + j + 1] for j in range(HV)], 1)

    for part in range(2):
        ag_send(0, v.xown, v.xg, part)

    def w_ref(l):
        return v.wt0 if l == 0 else v.wtr.at[l - 1]

    def w_half(l, dd, core):
        at = lax.rem(c + dd, NC) * HC + core * (HC // 2)
        return w_ref(l).at[pl.ds(pl.multiple_of(at, HC // 2), HC // 2), :]

    def w_send(l):
        block = w_half(l, 0, k)
        for dd in range(1, NC):
            send(block, block, v.s_w.at[l, dd], v.r_w.at[l, dd], (n, lax.rem(c + dd, NC)))

    def w_pass(l):
        for dd in range(1, NC):
            block = w_half(l, NC - dd, k)
            wait_bytes(block, v.r_w.at[l, dd])
            send(block, block, v.s_wp.at[l, dd], v.r_wp.at[l, dd], sib)

    def w_wait(l):
        for dd in range(1, NC):
            wait_bytes(w_half(l, NC - dd, 1 - k), v.r_wp.at[l, dd])

    w_send(0)
    for j in range(CH):
        send(adj_cols(j, 1 - k), v.adjb.at[1, j], v.s_adj.at[j], v.r_adj.at[j], sib)
    w_loads[0].wait()
    w_send(1)
    for copy in w_loads[1:]:
        copy.wait()

    def column(row):
        return jnp.broadcast_to(row.astype(F32), (LANES, R)).T

    v.valid[...] = column(v.nm_in[...])
    v.counted[...] = column(v.lm_in[...] * v.nm_in[...])
    v.label[...] = column(v.lb_in[...])
    v.whp[...] = jnp.zeros(v.whp.shape, F32)
    v.whp[: d.C, :] = v.whd_in[...]
    v.biasp[...] = jnp.zeros(v.biasp.shape, F32)
    v.biasp[:, : d.C] = v.bias_in[...]
    ar_put(
        8,
        [
            jnp.sum(v.valid[...], axis=0, keepdims=True),
            jnp.sum(v.counted[...], axis=0, keepdims=True),
        ],
    )
    ar_send(8)

    def adj_own(j, carry):
        pltpu.make_async_copy(adj_cols(j, k), v.adjb.at[0, j], v.ld.at[base + j]).wait()
        v.abf[j, :R, :] = v.adjb[0, j].astype(F32).astype(BF16)
        return carry

    def adj_sib(j, carry):
        wait_bytes(v.adjb.at[1, j], v.r_adj.at[j])
        v.abf[j, R:, :] = v.adjb[1, j].astype(F32).astype(BF16)
        return carry

    def adj_turn(j, carry):
        for side in range(2):
            v.at[side, j] = v.adjb[side, j].astype(F32).T.astype(BF16)
        return carry

    lax.fori_loop(0, CH, adj_own, 0)
    first_rows = len(drains)
    ag_forward(0, v.xg)
    lax.fori_loop(0, CH, adj_sib, 0)

    def wide(value):
        return cat([value] * HV, 1)

    RC = min(R // 2, 64)
    HALF = R // 2

    def activate(l, part):
        def chunk(i, carry):
            r = rows(i, RC)
            x = v.lin[r, :]
            square = x * x
            t = jnp.tanh(GELU_OUT * x * (1.0 + GELU_CUBE * square))
            half = 0.5 * (1.0 + t)
            act = x * half
            v.acts[l, r, :] = act
            v.gp[l, r, :] = half + (0.5 * GELU_OUT) * x * (1.0 - t * t) * (
                1.0 + (3.0 * GELU_CUBE) * square
            )
            masked = wide(v.valid[r, :]) * act
            return (
                carry[0] + jnp.sum(masked.reshape(RC // 8, 8, H), axis=0),
                carry[1] + jnp.sum((masked * act).reshape(RC // 8, 8, H), axis=0),
            )

        zero = jnp.zeros((8, H), F32)
        per = HALF // RC
        return lax.fori_loop(part * per, (part + 1) * per, chunk, (zero, zero))

    def over_rows(value):
        return jnp.sum(value, axis=0, keepdims=True)

    def keep_stats(l, total):
        count = jnp.max(v.count[0:1, :], axis=1, keepdims=True)
        mean = vec(total, 0) / count
        var = vec(total, 1) / count - mean * mean
        inverse = lax.rsqrt(var + NORM_EPS)
        gain, shift = v.npar_in[l, 0:1, :], v.npar_in[l, 1:2, :]
        v.vecs[l, 0:1, :] = mean
        v.vecs[l, 1:2, :] = inverse
        v.vecs[l, 2:3, :] = gain * inverse
        v.vecs[l, 3:4, :] = shift - mean * (gain * inverse)

    def finish(l, part_lin):
        sums = []
        for part in range(2):
            part_lin(part)
            sums.append(activate(l, part))
            if l < L - 1:
                ag_send(l + 1, v.acts.at[l], v.ag.at[l], part)
        ar_put(l, [over_rows(sums[0][i] + sums[1][i]) for i in range(2)])
        ar_send(l)

    def add_first(chip, part, ref):
        high, low = split(ref[...])
        a = v.abf[chip]
        got = dot_t(cat([high, low], 1), cat([a, a], 1))
        first = -(-FR // 16) * 8
        r = slice(0, first) if part == 0 else slice(first, FR)
        seen = v.aggt[r, :]
        v.aggt[r, :] = seen + got

    v.aggt[...] = jnp.zeros((FR, 2 * R), F32)
    for part in range(2):
        add_first(ch, part, halves(v.xown)[part])
    w_pass(0)
    ag_blocks(0, v.xg, add_first)
    v.part0[...] = v.aggt[:, R:]
    send(v.part0, v.part0r, v.s_sib.at[0, 0], v.r_sib.at[0, 0], sib)
    w_wait(0)
    v.w0h[...], v.w0l[...] = split(v.wt0[...])
    feature = lax.broadcasted_iota(jnp.int32, (FR, R), 0) < F
    v.in0h[:FR, :], v.in0l[:FR, :] = split(jnp.where(feature, v.xown[...], 0.0))
    wait_bytes(v.part0r, v.r_sib.at[0, 0])
    total = v.aggt[:, :R] + v.part0r[...]
    degree = total[F : F + 1, :]
    v.in0h[FR:, :], v.in0l[FR:, :] = split(
        jnp.where(feature, total * (1.0 / jnp.maximum(degree, 1.0)), 0.0)
    )
    v.lin[...] = dot3((v.w0h[...], v.w0l[...]), (v.in0h[...], v.in0l[...])).T
    finish(0, lambda part: None)
    degree = column(degree)
    v.degree[...] = degree
    v.linked[...] = jnp.minimum(degree, 1.0)
    v.invdeg[...] = 1.0 / jnp.maximum(degree, 1.0)
    v.count[...] = ar_wait(8)[0:2]

    for l in range(1, L):
        if l == 1:
            lax.fori_loop(0, CH, adj_turn, 0)
        w_pass(l)
        ag_forward(l, v.ag.at[l - 1])
        w_wait(l)
        v.wh[l - 1], v.wl[l - 1] = split(v.wtr[l - 1])
        total = ar_wait(l - 1)
        if l < L - 1:
            w_send(l + 1)
        keep_stats(l - 1, total)
        scale, shift = v.vecs[l - 1, 2:3, :], v.vecs[l - 1, 3:4, :]
        v.inh[l - 1, :, :H], v.inl[l - 1, :, :H] = split(v.acts[l - 1] * scale + shift)
        v.lin[...] = dot3_t(
            (v.inh[l - 1, :, :H], v.inl[l - 1, :, :H]), (v.wh[l - 1, :, :H], v.wl[l - 1, :, :H])
        )

        def add(chip, part, ref):
            high, low = split(ref[...])
            a = v.abf[chip, :, part * HALF : (part + 1) * HALF]
            v.agg[...] += dot(cat([a, a], 1), cat([high, low], 0))

        high, low = split(v.acts[l - 1])
        a = v.abf[ch]
        v.agg[...] = dot(cat([a, a], 1), cat([high, low], 0))
        ag_blocks(l, v.ag.at[l - 1], add)
        parts, partr = halves(v.parts.at[l - 1]), halves(v.partr.at[l - 1])
        for part in range(2):
            parts[part][...] = v.agg[R + part * HALF : R + (part + 1) * HALF, :]
            send(parts[part], partr[part], v.s_sib.at[l, part], v.r_sib.at[l, part], sib)

        def part_lin(part):
            r = slice(part * HALF, (part + 1) * HALF)
            wait_bytes(partr[part], v.r_sib.at[l, part])
            agg = v.agg[r, :] + partr[part][...]
            v.kept[l - 1, r, :] = agg
            v.inh[l - 1, r, H:], v.inl[l - 1, r, H:] = split(
                agg * wide(v.invdeg[r, :]) * scale + wide(v.linked[r, :]) * shift
            )
            v.lin[r, :] += dot3_t(
                (v.inh[l - 1, r, H:], v.inl[l - 1, r, H:]), (v.wh[l - 1, :, H:], v.wl[l - 1, :, H:])
            )

        finish(l, part_lin)

    for drain in drains[first_rows:]:
        drain()
    del drains[first_rows:]

    head = split(v.whp[...])
    lane = lax.broadcasted_iota(jnp.int32, (R, LANES), 1)
    onehot = jnp.where(lane.astype(F32) == v.label[...], 1.0, 0.0)
    real = lane < d.C
    counted = v.counted[...]
    label_count = jnp.max(v.count[1:2, :], axis=1, keepdims=True)
    keep_stats(L - 1, ar_wait(L - 1))
    last = split(v.acts[L - 1] * v.vecs[L - 1, 2:3, :] + v.vecs[L - 1, 3:4, :])
    logits = dot3_t(last, head) + v.biasp[...]
    top = jnp.max(jnp.where(real, logits, -3.0e38), axis=1, keepdims=True)
    moved = logits - top
    power = jnp.where(real, jnp.exp(moved), 0.0)
    power_sum = jnp.sum(power, axis=1, keepdims=True)
    g_logits = counted * (power / power_sum - onehot) / label_count
    gl_split = split(g_logits)
    v.gout[...] = dot3(gl_split, head)

    def last_sums():
        mean, inverse = v.vecs[L - 1, 0:1, :], v.vecs[L - 1, 1:2, :]

        def chunk(i, carry):
            r = rows(i, RC)
            g = v.gout[r, :]
            normed = (v.acts[L - 1, r, :] - mean) * inverse
            return (
                carry[0] + jnp.sum((g * normed).reshape(RC // 8, 8, H), axis=0),
                carry[1] + jnp.sum(g.reshape(RC // 8, 8, H), axis=0),
            )

        zero = jnp.zeros((8, H), F32)
        return [over_rows(s) for s in lax.fori_loop(0, R // RC, chunk, (zero, zero))]

    ar_put(3, last_sums())
    ar_send(3)
    logp = moved - jnp.log(power_sum)
    rows_loss = jnp.sum(jnp.where(real, onehot * logp, 0.0), axis=1, keepdims=True) * counted
    ar_put(6, [-over_rows(rows_loss), over_rows(g_logits)])
    ar_send(6)
    head_grad = dot3(split(g_logits.T[:CR, :]), last)
    HT = d.HT
    for t in range(HT):
        i, j = t // HV, t % HV
        v.hg[t] = head_grad[8 * i : 8 * i + 8, j * LANES : (j + 1) * LANES]

    def others(index, size, ref_of, init):
        return lax.fori_loop(1, size, lambda i, s: s + ref_of(lax.rem(index + i, size)), init)

    def head_scatter(i, carry):
        t = lax.rem(me + i, NDEV)

        def go():
            remote(v.hg.at[t], v.hrecv.at[me], v.s_h.at[0], v.r_h.at[0], device(t)).start()

        either(HT == NDEV, t < HT, go)
        return carry

    lax.fori_loop(1, NDEV, head_scatter, 0)
    drains.append(
        lambda: either(
            HT == NDEV,
            me < HT,
            lambda: wait_bytes(v.hrecv.at[pl.ds(0, HT - 1)], v.s_h.at[0]),
            lambda: wait_bytes(v.hrecv.at[pl.ds(0, HT)], v.s_h.at[0]),
        )
    )

    def head_gather():
        def go():
            wait_bytes(v.hrecv.at[pl.ds(0, NDEV - 1)], v.r_h.at[0])
            v.hfin[me] = others(me, NDEV, lambda s: v.hrecv[s], v.hg[me])

            def one(i, carry):
                remote(
                    v.hfin.at[me], v.hfin.at[me], v.s_h.at[1], v.r_h.at[1],
                    device(lax.rem(me + i, NDEV)),
                ).start()
                return carry

            lax.fori_loop(1, NDEV, one, 0)

        either(HT == NDEV, me < HT, go)
        drains.append(
            lambda: either(
                HT == NDEV,
                me < HT,
                lambda: wait_bytes(v.hrecv.at[pl.ds(0, NDEV - 1)], v.s_h.at[1]),
            )
        )

    def sibling_send(i):
        send(v.dwb.at[i, 1 - k], v.dwr.at[i], v.s_d.at[i], v.r_d.at[i], sib)

    def cols_send(i):
        wait_bytes(v.dwr.at[i], v.r_d.at[i])
        v.dwb[i, k] += v.dwr[i]
        for dd in range(1, NC):
            t = lax.rem(c + dd, NC)
            remote(v.dwb.at[i, k, t], v.zrecv.at[i, c], v.s_z.at[i], v.r_z.at[i], (n, t)).start()
        drains.append(lambda: wait_bytes(v.zrecv.at[i, pl.ds(0, NC - 1)], v.s_z.at[i]))

    def nodes_send(i):
        wait_bytes(v.zrecv.at[i, pl.ds(0, NC - 1)], v.r_z.at[i])
        v.zs[i] = others(c, NC, lambda s: v.zrecv[i, s], v.dwb[i, k, c])

        def one(j, carry):
            t = lax.rem(ch + j, CH)
            either(
                PH == CH,
                t < PH,
                lambda: remote(
                    v.zs.at[i, rows(t, RPP), :], v.nrecv.at[i, ch], v.s_n.at[i], v.r_n.at[i],
                    (t * 2 + k, c),
                ).start(),
            )
            return carry

        lax.fori_loop(1, CH, one, 0)
        drains.append(
            lambda: either(
                PH == CH,
                ch < PH,
                lambda: wait_bytes(v.zs.at[i, pl.ds(0, (PH - 1) * RPP), :], v.s_n.at[i]),
                lambda: wait_bytes(v.zs.at[i, pl.ds(0, PH * RPP), :], v.s_n.at[i]),
            )
        )

    def pieces_out(i, fin, at, piece):
        mine = pl.ds(pl.multiple_of(at, RPP), RPP)
        fin[mine, :] = piece
        square = jnp.sum((piece * piece).reshape(RPP // 8, 8, piece.shape[1]), axis=0)
        v.sq[...] += jnp.sum(square, axis=1, keepdims=True)

        def one(j, carry):
            block = fin.at[mine, :]
            remote(block, block, v.s_f.at[i], v.r_f.at[i], (lax.rem(n + j, NN), c)).start()
            return carry

        lax.fori_loop(1, NN, one, 0)

    def pieces_drain(i, fin):
        drains.append(
            lambda: either(
                PPC == NN,
                n < PPC if i == L - 1 else ch < PH,
                lambda: lax.fori_loop(
                    1, NN, lambda j, carry: (wait_bytes(fin.at[pl.ds(0, RPP), :], v.s_f.at[i]), carry)[1], 0
                ),
            )
        )

    def nodes_gather(i):
        def go():
            wait_bytes(v.nrecv.at[i, pl.ds(0, CH - 1)], v.r_n.at[i])
            piece = others(ch, CH, lambda s: v.nrecv[i, s], v.zs[i, rows(ch, RPP), :])
            pieces_out(i, v.fin.at[i], k * (HC // 2) + ch * RPP, piece)

        either(PH == CH, ch < PH, go)
        pieces_drain(i, v.fin.at[i])

    v.sq[...] = jnp.zeros((8, LANES), F32)

    def linear_grad(l, a):
        total = ar_wait(a)
        g_gain, g_shift = vec(total, 0), vec(total, 1)
        v.gn[l, 0:1, :] = g_gain
        v.gn[l, 1:2, :] = g_shift
        mean, inverse, scale = v.vecs[l, 0:1, :], v.vecs[l, 1:2, :], v.vecs[l, 2:3, :]
        count = jnp.max(v.count[0:1, :], axis=1, keepdims=True)
        by_one = scale * g_shift / count
        by_normed = scale * g_gain / count

        def chunk(i, carry):
            r = rows(i, RC)
            normed = (v.acts[l, r, :] - mean) * inverse
            g_active = scale * v.gout[r, :] - wide(v.valid[r, :]) * (by_one + normed * by_normed)
            g_linear = v.gp[l, r, :] * g_active
            v.lin[r, :] = g_linear
            v.glh[r, :], v.gll[r, :] = split(g_linear)
            return carry

        lax.fori_loop(0, R // RC, chunk, 0)

    for l in (2, 1):
        g = l - 1
        linear_grad(l, 5 - l)
        gl = (v.glh[...], v.gll[...])
        back = v.ag.at[2 - l]
        v.spread[...] = dot3(gl, (v.wh[g, :, H:], v.wl[g, :, H:])) * wide(v.invdeg[...])
        v.spreads[g] = v.spread[...]
        send(v.spreads.at[g], v.spreadr.at[g], v.s_sib.at[L + g, 0], v.r_sib.at[L + g, 0], sib)
        if g == 0:
            for drain in scatter_drains:
                drain()
        own = cat(list(split(v.spread[...])), 0)
        for dd in reversed(range(CH)):
            t = v.at[0, flip(ch, dd)]
            v.out[dd] = dot(cat([t, t], 1), own)
        wait_bytes(v.spreadr.at[g], v.r_sib.at[L + g, 0])
        other = cat(list(split(v.spreadr[g])), 0)

        def complete(dd):
            t = v.at[1, flip(ch, dd)]
            v.out[dd] += dot(cat([t, t], 1), other)

        s, r = v.s_rs.at[g], v.r_rs.at[g]
        kept_drains, drains = drains, []
        if CH == 4:
            x, y, z = (halves(v.out.at[dd]) for dd in (1, 2, 3))
            from_x, from_y, via = (halves(back.at[i]) for i in range(3))
            complete(3)
            send(z[0], via[0], s.at[0], r.at[0], peer(1))
            send(z[1], via[1], s.at[1], r.at[1], peer(2))
            complete(1)
            send(x[0], from_x[0], s.at[2], r.at[2], peer(1))
            complete(2)
            send(y[1], from_y[1], s.at[3], r.at[3], peer(2))
            complete(0)
            wait_bytes(via[0], r.at[0])
            y[0][...] += via[0][...]
            send(y[0], from_y[0], s.at[5], r.at[5], peer(2))
            wait_bytes(via[1], r.at[1])
            x[1][...] += via[1][...]
            send(x[1], from_x[1], s.at[4], r.at[4], peer(1))
        else:
            for dd in reversed(range(1, CH)):
                complete(dd)
                send(v.out.at[dd], back.at[dd], s.at[dd], r.at[dd], peer(dd))
            complete(0)
        scatter_drains, drains = drains, kept_drains

        if l == 1:
            cols_send(1)
        v.gout[...] = dot3(gl, (v.wh[g, :, :H], v.wl[g, :, :H]))
        mean, inverse = v.vecs[g, 0:1, :], v.vecs[g, 1:2, :]

        def chunk(i, carry):
            r = rows(i, RC)
            self, spread, degree = v.gout[r, :], v.spread[r, :], wide(v.degree[r, :])
            normed = (v.acts[g, r, :] - mean) * inverse
            reached = (v.kept[g, r, :] - degree * mean) * inverse
            v.gout[r, :] = self + v.out[0, r, :]
            return (
                carry[0] + jnp.sum((self * normed + spread * reached).reshape(RC // 8, 8, H), axis=0),
                carry[1] + jnp.sum((self + spread * degree).reshape(RC // 8, 8, H), axis=0),
            )

        zero = jnp.zeros((8, H), F32)
        ar_put(6 - l, [over_rows(s) for s in lax.fori_loop(0, R // RC, chunk, (zero, zero))])
        ar_send(6 - l)
        grad = dot3(split(v.lin[...].T), (v.inh[g], v.inl[g]))
        for t in range(NC):
            for half in range(2):
                at = t * HC + half * (HC // 2)
                v.dwb[g, half, t] = grad[at : at + HC // 2, :]
        sibling_send(g)
        if l == 1:
            nodes_send(1)
            head_gather()
            cols_send(0)
        if CH == 4:
            for half, i in ((from_x[0], 2), (from_y[1], 3), (from_y[0], 5), (from_x[1], 4)):
                wait_bytes(half, r.at[i])
            v.gout[...] += back[0] + back[1]
        else:
            for dd in range(1, CH):
                wait_bytes(back.at[dd], r.at[dd])
                v.gout[...] += back[dd]
    drains += scatter_drains

    linear_grad(0, 5)
    grad = dot3_t(split(v.lin[...].T), (v.in0h[...], v.in0l[...]))
    for t in range(NC):
        v.d0[t] = grad[t * HC : (t + 1) * HC, :]

    def first_scatter(i, carry):
        tn, tc = device(lax.rem(me + i, NDEV))
        either(
            PPC == NN,
            tn < PPC,
            lambda: remote(
                v.d0.at[tc, rows(tn, RPP), :], v.recv0.at[me], v.s_0.at[0], v.r_0.at[0], (tn, tc)
            ).start(),
        )
        return carry

    lax.fori_loop(1, NDEV, first_scatter, 0)
    drains.append(
        lambda: either(
            PPC == NN,
            n < PPC,
            lambda: wait_bytes(v.recv0.at[pl.ds(0, PPC * NC - 1)], v.s_0.at[0]),
            lambda: wait_bytes(v.recv0.at[pl.ds(0, PPC * NC)], v.s_0.at[0]),
        )
    )
    nodes_gather(1)
    nodes_send(0)
    nodes_gather(0)

    def first_gather():
        wait_bytes(v.recv0.at[pl.ds(0, NDEV - 1)], v.r_0.at[0])
        piece = others(me, NDEV, lambda s: v.recv0[s], v.d0[c, rows(n, RPP), :])
        pieces_out(L - 1, v.fin0, n * RPP, piece)

    either(PPC == NN, n < PPC, first_gather)
    pieces_drain(L - 1, v.fin0)
    ar_put(7, [over_rows(v.sq[...])])
    ar_send(7)

    total = ar_wait(6)
    bias_grad = total[1:2]
    v.misc[...] = jnp.zeros((8, LANES), F32)
    v.misc[0:1, :] = total[0:1]
    v.misc[1:2, :] = v.count[1:2, :]
    v.misc[3:4, :] = bias_grad

    def fin_wait(i, fin):
        either(
            PPC == NN,
            n < PPC if i == L - 1 else ch < PH,
            lambda: wait_bytes(fin.at[pl.ds(0, (PPC - 1) * RPP), :], v.r_f.at[i]),
            lambda: wait_bytes(fin.at[pl.ds(0, PPC * RPP), :], v.r_f.at[i]),
        )

    either(
        HT == NDEV,
        me < HT,
        lambda: wait_bytes(v.hfin.at[pl.ds(0, HT - 1)], v.r_h.at[1]),
        lambda: wait_bytes(v.hfin.at[pl.ds(0, HT)], v.r_h.at[1]),
    )
    square = jnp.zeros((8, LANES), F32)
    for t in range(HT):
        i, j = t // HV, t % HV
        tile = v.hfin[t]
        v.gh[8 * i : 8 * i + 8, j * LANES : (j + 1) * LANES] = tile
        square += tile * tile
    replicated = over_rows(square) + bias_grad * bias_grad
    small = jnp.zeros((1, H), F32)
    for l in range(L):
        small += over_rows(v.gn[l] * v.gn[l])
    for j in range(HV):
        replicated += small[:, j * LANES : (j + 1) * LANES]

    for i in range(L - 1):
        fin_wait(i, v.fin.at[i])
        v.gr[i] = v.fin[i]
    total = ar_wait(7)
    squares = total[0:1, 0:1] + jnp.sum(replicated, axis=1, keepdims=True)
    norm = jnp.sqrt(squares)
    v.misc[2:3, :] = jnp.broadcast_to(norm, (1, LANES))
    v.misc[4:5, :] = jnp.broadcast_to(CLIP / jnp.maximum(norm, CLIP), (1, LANES))
    fin_wait(L - 1, v.fin0)
    v.g0[:, :F] = v.fin0[:, :F]
    v.g0[:, F:] = v.fin0[:, FR : FR + F]

    for drain in drains:
        drain()


def gradients(NN, NC, feat, adj, nm, lb, lm, w0, wr, npar, whd, bias):
    F, R = feat.shape
    C, H = whd.shape
    HC = w0.shape[0]
    CH, NDEV = NN // 2, NN * NC
    up = lambda size: -(-size // 8) * 8
    FR, CR = up(F + 1), up(C)
    RPP = max(8, HC // NN)
    HV = H // LANES
    d = types.SimpleNamespace(
        NN=NN, NC=NC, R=R, F=F, H=H, C=C, HC=HC, CH=CH, NDEV=NDEV, FR=FR, CR=CR, RPP=RPP,
        PPC=HC // RPP, PH=HC // RPP // 2, HV=HV, HT=CR // 8 * HV,
    )
    dma = pltpu.SemaphoreType.DMA
    L = LAYERS
    inputs = {
        "feat": feat, "adj": adj, "nm": nm, "lb": lb, "lm": lm, "w0": w0, "wr": wr, "npar": npar,
        "whd": whd, "bias": bias,
    }
    small = [name for name in inputs if name not in ("adj", "wr")]
    d.small = small
    scratch = {
        "xown": pltpu.VMEM((FR, R), F32),
        "xg": pltpu.VMEM((CH, FR, R), F32),
        "ag": pltpu.VMEM((L - 1, CH, R, H), F32),
        "acts": pltpu.VMEM((L, R, H), F32),
        "gp": pltpu.VMEM((L, R, H), F32),
        "adjb": pltpu.VMEM((2, CH, R, R), jnp.int32),
        "abf": pltpu.VMEM((CH, 2 * R, R), BF16),
        "at": pltpu.VMEM((2, CH, R, R), BF16),
        "wt0": pltpu.VMEM((H, 2 * FR), F32),
        "wtr": pltpu.VMEM((L - 1, H, 2 * H), F32),
        "w0h": pltpu.VMEM((H, 2 * FR), BF16),
        "w0l": pltpu.VMEM((H, 2 * FR), BF16),
        "wh": pltpu.VMEM((L - 1, H, 2 * H), BF16),
        "wl": pltpu.VMEM((L - 1, H, 2 * H), BF16),
        "whp": pltpu.VMEM((LANES, H), F32),
        "biasp": pltpu.VMEM((1, LANES), F32),
        "in0h": pltpu.VMEM((2 * FR, R), BF16),
        "in0l": pltpu.VMEM((2 * FR, R), BF16),
        "inh": pltpu.VMEM((L - 1, R, 2 * H), BF16),
        "inl": pltpu.VMEM((L - 1, R, 2 * H), BF16),
        "aggt": pltpu.VMEM((FR, 2 * R), F32),
        "part0": pltpu.VMEM((FR, R), F32),
        "part0r": pltpu.VMEM((FR, R), F32),
        "agg": pltpu.VMEM((2 * R, H), F32),
        "parts": pltpu.VMEM((L - 1, R, H), F32),
        "partr": pltpu.VMEM((L - 1, R, H), F32),
        "kept": pltpu.VMEM((L - 1, R, H), F32),
        "lin": pltpu.VMEM((R, H), F32),
        "gout": pltpu.VMEM((R, H), F32),
        "glh": pltpu.VMEM((R, H), BF16),
        "gll": pltpu.VMEM((R, H), BF16),
        "spread": pltpu.VMEM((R, H), F32),
        "spreads": pltpu.VMEM((L - 1, R, H), F32),
        "spreadr": pltpu.VMEM((L - 1, R, H), F32),
        "out": pltpu.VMEM((CH, R, H), F32),
        "valid": pltpu.VMEM((R, LANES), F32),
        "counted": pltpu.VMEM((R, LANES), F32),
        "label": pltpu.VMEM((R, LANES), F32),
        "degree": pltpu.VMEM((R, LANES), F32),
        "invdeg": pltpu.VMEM((R, LANES), F32),
        "linked": pltpu.VMEM((R, LANES), F32),
        "count": pltpu.VMEM((2, LANES), F32),
        "vecs": pltpu.VMEM((L, 8, H), F32),
        "sq": pltpu.VMEM((8, LANES), F32),
        "arb": pltpu.VMEM((9, NDEV, 4, LANES), F32),
        "dwb": pltpu.VMEM((L - 1, 2, NC, HC // 2, 2 * H), F32),
        "dwr": pltpu.VMEM((L - 1, NC, HC // 2, 2 * H), F32),
        "zrecv": pltpu.VMEM((L - 1, NC, HC // 2, 2 * H), F32),
        "zs": pltpu.VMEM((L - 1, HC // 2, 2 * H), F32),
        "nrecv": pltpu.VMEM((L - 1, CH, RPP, 2 * H), F32),
        "fin": pltpu.VMEM((L - 1, HC, 2 * H), F32),
        "d0": pltpu.VMEM((NC, HC, 2 * FR), F32),
        "recv0": pltpu.VMEM((NDEV, RPP, 2 * FR), F32),
        "fin0": pltpu.VMEM((HC, 2 * FR), F32),
        "hg": pltpu.VMEM((d.HT, 8, LANES), F32),
        "hrecv": pltpu.VMEM((NDEV, 8, LANES), F32),
        "hfin": pltpu.VMEM((d.HT, 8, LANES), F32),
        "ld": dma((L - 1 + len(small) + CH,)),
        "s_adj": dma((CH,)),
        "r_adj": dma((CH,)),
        "s_ag": dma((L, max(CH, 6))),
        "r_ag": dma((L, max(CH, 6))),
        "s_sib": dma((2 * L - 1, 2)),
        "r_sib": dma((2 * L - 1, 2)),
        "s_w": dma((L, NC)),
        "r_w": dma((L, NC)),
        "s_wp": dma((L, NC)),
        "r_wp": dma((L, NC)),
        "s_d": dma((L - 1,)),
        "r_d": dma((L - 1,)),
        "s_ar": dma((9,)),
        "r_ar": dma((9,)),
        "s_rs": dma((L - 1, max(CH, 6))),
        "r_rs": dma((L - 1, max(CH, 6))),
        "s_z": dma((L - 1,)),
        "r_z": dma((L - 1,)),
        "s_n": dma((L - 1,)),
        "r_n": dma((L - 1,)),
        "s_f": dma((L,)),
        "r_f": dma((L,)),
        "s_0": dma((1,)),
        "r_0": dma((1,)),
        "s_h": dma((2,)),
        "r_h": dma((2,)),
    }
    for name in small:
        scratch[name + "_in"] = pltpu.VMEM(inputs[name].shape, inputs[name].dtype)
    ins = list(inputs)
    outs = ["g0", "gr", "gn", "gh", "misc"]
    d.names = ins + outs + list(scratch)
    vmem = pl.BlockSpec(memory_space=pltpu.VMEM)
    return pl.pallas_call(
        functools.partial(step_kernel, d),
        out_shape=[
            jax.ShapeDtypeStruct(w0.shape, F32),
            jax.ShapeDtypeStruct(wr.shape, F32),
            jax.ShapeDtypeStruct(npar.shape, F32),
            jax.ShapeDtypeStruct((CR, H), F32),
            jax.ShapeDtypeStruct((8, LANES), F32),
        ],
        in_specs=[pl.BlockSpec(memory_space=pl.ANY)] * len(ins),
        out_specs=[vmem] * len(outs),
        scratch_shapes=list(scratch.values()),
        compiler_params=pltpu.CompilerParams(
            collective_id=0, has_side_effects=True, vmem_limit_bytes=60 * 2**20
        ),
    )(*inputs.values())


def adamw(weight, first, second, average, grad, rate):
    first = BETA_ONE * first + (1.0 - BETA_ONE) * grad
    second = BETA_TWO * second + (1.0 - BETA_TWO) * grad * grad
    fix_one = 1.0 - BETA_ONE**ADAM_STEP
    fix_two = 1.0 - BETA_TWO**ADAM_STEP
    update = first / fix_one / (jnp.sqrt(second / fix_two) + ADAM_EPS)
    weight = weight - rate * (update + DECAY * weight)
    average = AVERAGE * average + (1.0 - AVERAGE) * weight
    return (first, second, weight, average)


def update_kernel(*refs):
    grads, state, scalars, results = refs[:5], refs[5:25], refs[25:28], refs[28:]
    misc = grads[4]
    scale = misc[4:5, 0:1]
    for i in range(3):
        scalars[i][...] = misc[i : i + 1, 0:1]
    for group in range(5):
        weight, first, second, average = (state[group + 5 * i] for i in (0, 1, 2, 3))
        rate = RATE_SMALL if group in (2, 4) else RATE_MATRIX
        shape = weight.shape
        if group == 4:
            grad = misc[3:4, : shape[1]]
        elif group == 3:
            grad = grads[3][: shape[0], :]
        else:
            grad = grads[group][...]
        done = adamw(weight[...], first[...], second[...], average[...], grad * scale, rate)
        for ref, value in zip(results[4 * group : 4 * group + 4], done, strict=True):
            ref[...] = value


def local(
    nodes, cols, features, adjacency, node_mask, labels, label_mask, *state
):
    turn = (
        lambda a: a.T,
        lambda a: a.transpose(0, 2, 1),
        lambda a: a.transpose(1, 0, 2),
        lambda a: a.T,
        lambda a: a.reshape(1, -1),
    )
    back = turn[:4] + (lambda a: a.reshape(-1),)
    state = [turn[i % 5](a) for i, a in enumerate(state)]
    grads = gradients(
        nodes, cols, features[0].T, adjacency[0], node_mask, labels, label_mask, *state[:5]
    )
    outs = [jax.ShapeDtypeStruct((1, 1), F32)] * 3
    outs += [jax.ShapeDtypeStruct(a.shape, F32) for a in state[:5] for _ in range(4)]
    done = pl.pallas_call(update_kernel, out_shape=outs)(*grads, *state)
    return (
        *(a.reshape(()) for a in done[:3]),
        *(back[i // 4](a) for i, a in enumerate(done[3:])),
    )


def solution(mesh):
    rows, first, rest, all_of = P("cols", "nodes", None), P(None, "cols"), P(None, None, "cols"), P()
    state = [first, rest, all_of, all_of, all_of]
    return jax.shard_map(
        functools.partial(local, mesh.shape["nodes"], mesh.shape["cols"]),
        mesh=mesh,
        in_specs=(rows, rows) + (P("cols", "nodes"),) * 3 + tuple(state * 4),
        out_specs=(all_of,) * 3 + tuple(spec for spec in state for _ in range(4)),
        check_vma=False,
    )
```

```python
import functools
import types

import jax
import jax.numpy as jnp
from jax import lax
from jax.experimental import pallas as pl
from jax.experimental.pallas import tpu as pltpu
from jax.sharding import PartitionSpec as P

LAYERS = 3
ADAM_STEP = 10
CLIP = 0.02
RATE_MATRIX = 0.03
RATE_SMALL = 0.3
BETA_ONE = 0.9
BETA_TWO = 0.999
ADAM_EPS = 1e-08
DECAY = 0.01
AVERAGE = 0.9
NORM_EPS = 1e-05

MESH = pl.DeviceIdType.MESH
F32 = jnp.float32
BF16 = jnp.bfloat16
LANES = 128
GELU_OUT = 0.7978845608028654
GELU_CUBE = 0.044715


def cat(values, axis):
    return values[0] if len(values) == 1 else jnp.concatenate(values, axis=axis)


def split(value):
    high = value.astype(BF16)
    return high, (value - high.astype(F32)).astype(BF16)


def dot(left, right):
    return lax.dot_general(left, right, (((1,), (0,)), ((), ())), preferred_element_type=F32)


def dot_t(left, right):
    return lax.dot_general(left, right, (((1,), (1,)), ((), ())), preferred_element_type=F32)


def dot3(left, right):
    (lh, ll), (rh, rl) = left, right
    return dot(cat([lh, lh, ll], 1), cat([rh, rl, rh], 0))


def dot3_t(left, right):
    (lh, ll), (rh, rl) = left, right
    return dot_t(cat([lh, lh, ll], 1), cat([rh, rl, rh], 1))


def remote(src, dst, send, recv, device):
    return pltpu.make_async_remote_copy(
        src_ref=src, dst_ref=dst, send_sem=send, recv_sem=recv, device_id=device, device_id_type=MESH
    )


def wait_bytes(ref, sem):
    pltpu.make_async_copy(ref, ref, sem).wait()


def flip(index, distance):
    bit = 1
    while bit <= distance:
        if distance & bit:
            index = index + (1 - 2 * lax.rem(lax.div(index, bit), 2)) * bit
        bit *= 2
    return index


def step_kernel(d, *refs):
    v = types.SimpleNamespace(**dict(zip(d.names, refs, strict=True)))
    NN, NC, R, H, HC, CH, L = d.NN, d.NC, d.R, d.H, d.HC, d.CH, LAYERS
    NDEV, RPP, PPC, PH, HV, F, FR, CR = d.NDEV, d.RPP, d.PPC, d.PH, d.HV, d.F, d.FR, d.CR
    n, c = lax.axis_index("nodes"), lax.axis_index("cols")
    me = n * NC + c
    ch, k = lax.div(n, 2), lax.rem(n, 2)
    sib = (ch * 2 + 1 - k, c)
    drains = []

    def device(index):
        return lax.div(index, NC), lax.rem(index, NC)

    def peer(dd):
        return flip(ch, dd) * 2 + k, c

    def rows(i, size):
        return pl.ds(pl.multiple_of(i * size, size), size)

    def send(src, dst, ssem, rsem, dev):
        remote(src, dst, ssem, rsem, dev).start()
        drains.append(lambda: wait_bytes(src, ssem))

    def either(always, condition, fn, other=None):
        if always:
            fn()
            return

        @pl.when(condition)
        def _():
            fn()

        if other is not None:

            @pl.when(jnp.logical_not(condition))
            def _():
                other()

    barrier = pltpu.get_barrier_semaphore()

    def greet(i, carry):
        pl.semaphore_signal(
            barrier, inc=1, device_id=device(lax.rem(me + i, NDEV)), device_id_type=MESH
        )
        return carry

    lax.fori_loop(1, NDEV, greet, 0)

    def adj_cols(j, core):
        return v.adj.at[:, rows(j * 2 + core, R)]

    own_rows = rows(c, HC)
    w_loads = [
        pltpu.make_async_copy(v.wr.at[i], v.wtr.at[i, own_rows, :], v.ld.at[i]) for i in range(L - 1)
    ]
    small_loads = [
        pltpu.make_async_copy(
            v.feat.at[:, 0, :] if name == "feat" else getattr(v, name),
            getattr(v, name + "_in"),
            v.ld.at[L - 1 + i],
        )
        for i, name in enumerate(d.small)
    ]
    for copy in small_loads + w_loads:
        copy.start()
    base = L - 1 + len(d.small)
    for j in range(CH):
        pltpu.make_async_copy(adj_cols(j, k), v.adjb.at[0, j], v.ld.at[base + j]).start()
    for copy in small_loads:
        copy.wait()
    v.xown[:F, :] = v.feat_in[...]
    v.xown[F:, :] = jnp.ones((FR - F, R), F32)
    v.wt0[own_rows, :] = jnp.zeros((HC, 2 * FR), F32)
    v.wt0[own_rows, :F] = v.w0_in[:, :F]
    v.wt0[own_rows, FR : FR + F] = v.w0_in[:, F:]
    pl.semaphore_wait(barrier, NDEV - 1)

    def halves(ref):
        size = ref.shape[0]
        first = -(-size // 16) * 8
        return ref.at[:first], ref.at[first:]

    def ag_send(g, src, buf, part):
        s, r = v.s_ag.at[g], v.r_ag.at[g]
        mine = halves(src)
        slot = halves(buf.at[ch])
        if CH == 4:
            send(mine[part], slot[part], s.at[part], r.at[part], peer(1))
            if part == 1:
                send(mine[1], slot[1], s.at[3], r.at[3], peer(2))
                send(mine[0], slot[0], s.at[2], r.at[2], peer(2))
        elif part == 1:
            for dd in reversed(range(1, CH)):
                send(src, buf.at[ch], s.at[dd], r.at[dd], peer(dd))

    def ag_forward(g, buf):
        s, r = v.s_ag.at[g], v.r_ag.at[g]
        if CH == 4:
            x, y = (halves(buf.at[flip(ch, dd)]) for dd in (1, 2))
            wait_bytes(x[0], r.at[0])
            send(x[0], x[0], s.at[4], r.at[4], peer(2))
            wait_bytes(y[1], r.at[3])
            send(y[1], y[1], s.at[5], r.at[5], peer(1))

    def ag_blocks(g, buf, add):
        r = v.r_ag.at[g]
        if CH == 4:
            x, y, z = (halves(buf.at[flip(ch, dd)]) for dd in (1, 2, 3))
            add(flip(ch, 1), 0, x[0])
            add(flip(ch, 2), 1, y[1])
            wait_bytes(x[1], r.at[1])
            add(flip(ch, 1), 1, x[1])
            wait_bytes(y[0], r.at[2])
            add(flip(ch, 2), 0, y[0])
            wait_bytes(z[0], r.at[4])
            add(flip(ch, 3), 0, z[0])
            wait_bytes(z[1], r.at[5])
            add(flip(ch, 3), 1, z[1])
        else:
            for dd in range(1, CH):
                wait_bytes(buf.at[flip(ch, dd)], r.at[dd])
                for part in range(2):
                    add(flip(ch, dd), part, halves(buf.at[flip(ch, dd)])[part])

    def to_others(start, at_once=False):
        if at_once and NDEV <= 32:
            for dc in [*reversed(range(1, NC)), 0]:
                for dn in reversed(range(NN)):
                    if dn or dc:
                        tn, tc = lax.rem(n + dn, NN) if dn else n, lax.rem(c + dc, NC) if dc else c
                        start((tn, tc), tn * NC + tc)
            return

        def one(i, carry):
            t = lax.rem(me + i, NDEV)
            start(device(t), t)
            return carry

        lax.fori_loop(1, NDEV, one, 0)

    def ar_send(a, at_once=False):
        to_others(
            lambda dev, t: remote(
                v.arb.at[a, me], v.arb.at[a, me], v.s_ar.at[a], v.r_ar.at[a], dev
            ).start(),
            at_once,
        )
        drains.append(lambda: wait_bytes(v.arb.at[a, pl.ds(0, NDEV - 1)], v.s_ar.at[a]))

    def ar_put(a, vectors):
        at = 0
        for vec in vectors:
            for i in range(vec.shape[1] // LANES):
                v.arb[a, me, at : at + 1, :] = vec[:, i * LANES : (i + 1) * LANES]
                at += 1
        if at < 4:
            v.arb[a, me, at:, :] = jnp.zeros((4 - at, LANES), F32)

    def ar_wait(a):
        wait_bytes(v.arb.at[a, pl.ds(0, NDEV - 1)], v.r_ar.at[a])
        return jnp.sum(v.arb[a], axis=0)

    def vec(total, i):
        return cat([total[i * HV + j : i * HV + j + 1] for j in range(HV)], 1)

    for part in range(2):
        ag_send(0, v.xown, v.xg, part)

    def w_ref(l):
        return v.wt0 if l == 0 else v.wtr.at[l - 1]

    def w_half(l, dd, core):
        at = lax.rem(c + dd, NC) * HC + core * (HC // 2)
        return w_ref(l).at[pl.ds(pl.multiple_of(at, HC // 2), HC // 2), :]

    def w_send(l):
        block = w_half(l, 0, k)
        for dd in range(1, NC):
            send(block, block, v.s_w.at[l, dd], v.r_w.at[l, dd], (n, lax.rem(c + dd, NC)))

    def w_pass(l):
        for dd in range(1, NC):
            block = w_half(l, NC - dd, k)
            wait_bytes(block, v.r_w.at[l, dd])
            send(block, block, v.s_wp.at[l, dd], v.r_wp.at[l, dd], sib)

    def w_wait(l):
        for dd in range(1, NC):
            wait_bytes(w_half(l, NC - dd, 1 - k), v.r_wp.at[l, dd])

    w_send(0)
    for j in range(CH):
        send(adj_cols(j, 1 - k), v.adjb.at[1, j], v.s_adj.at[j], v.r_adj.at[j], sib)
    w_loads[0].wait()
    w_send(1)
    for copy in w_loads[1:]:
        copy.wait()

    def column(row):
        return jnp.broadcast_to(row.astype(F32), (LANES, R)).T

    v.valid[...] = column(v.nm_in[...])
    v.counted[...] = column(v.lm_in[...] * v.nm_in[...])
    v.label[...] = column(v.lb_in[...])
    v.whp[...] = jnp.zeros(v.whp.shape, F32)
    v.whp[: d.C, :] = v.whd_in[...]
    v.biasp[...] = jnp.zeros(v.biasp.shape, F32)
    v.biasp[:, : d.C] = v.bias_in[...]
    ar_put(
        8,
        [
            jnp.sum(v.valid[...], axis=0, keepdims=True),
            jnp.sum(v.counted[...], axis=0, keepdims=True),
        ],
    )
    ar_send(8)

    def adj_own(j, carry):
        pltpu.make_async_copy(adj_cols(j, k), v.adjb.at[0, j], v.ld.at[base + j]).wait()
        v.abf[j, :R, :] = v.adjb[0, j].astype(F32).astype(BF16)
        return carry

    def adj_sib(j, carry):
        wait_bytes(v.adjb.at[1, j], v.r_adj.at[j])
        v.abf[j, R:, :] = v.adjb[1, j].astype(F32).astype(BF16)
        return carry

    def adj_turn(j, carry):
        for side in range(2):
            v.at[side, j] = v.adjb[side, j].astype(F32).T.astype(BF16)
        return carry

    lax.fori_loop(0, CH, adj_own, 0)
    first_rows = len(drains)
    ag_forward(0, v.xg)
    lax.fori_loop(0, CH, adj_sib, 0)

    def wide(value):
        return cat([value] * HV, 1)

    RC = min(R // 2, 64)
    HALF = R // 2

    def activate(l, part):
        def chunk(i, carry):
            r = rows(i, RC)
            x = v.lin[r, :]
            square = x * x
            t = jnp.tanh(GELU_OUT * x * (1.0 + GELU_CUBE * square))
            half = 0.5 * (1.0 + t)
            act = x * half
            v.acts[l, r, :] = act
            v.gp[l, r, :] = half + (0.5 * GELU_OUT) * x * (1.0 - t * t) * (
                1.0 + (3.0 * GELU_CUBE) * square
            )
            masked = wide(v.valid[r, :]) * act
            return (
                carry[0] + jnp.sum(masked.reshape(RC // 8, 8, H), axis=0),
                carry[1] + jnp.sum((masked * act).reshape(RC // 8, 8, H), axis=0),
            )

        zero = jnp.zeros((8, H), F32)
        per = HALF // RC
        return lax.fori_loop(part * per, (part + 1) * per, chunk, (zero, zero))

    def over_rows(value):
        return jnp.sum(value, axis=0, keepdims=True)

    def keep_stats(l, total):
        count = jnp.max(v.count[0:1, :], axis=1, keepdims=True)
        mean = vec(total, 0) / count
        var = vec(total, 1) / count - mean * mean
        inverse = lax.rsqrt(var + NORM_EPS)
        gain, shift = v.npar_in[l, 0:1, :], v.npar_in[l, 1:2, :]
        v.vecs[l, 0:1, :] = mean
        v.vecs[l, 1:2, :] = inverse
        v.vecs[l, 2:3, :] = gain * inverse
        v.vecs[l, 3:4, :] = shift - mean * (gain * inverse)

    def finish(l, part_lin):
        sums = []
        for part in range(2):
            part_lin(part)
            sums.append(activate(l, part))
            if l < L - 1:
                ag_send(l + 1, v.acts.at[l], v.ag.at[l], part)
        ar_put(l, [over_rows(sums[0][i] + sums[1][i]) for i in range(2)])
        ar_send(l, l == L - 1)

    def add_first(chip, part, ref):
        high, low = split(ref[...])
        a = v.abf[chip]
        got = dot_t(cat([high, low], 1), cat([a, a], 1))
        first = -(-FR // 16) * 8
        r = slice(0, first) if part == 0 else slice(first, FR)
        seen = v.aggt[r, :]
        v.aggt[r, :] = seen + got

    v.aggt[...] = jnp.zeros((FR, 2 * R), F32)
    for part in range(2):
        add_first(ch, part, halves(v.xown)[part])
    w_pass(0)
    ag_blocks(0, v.xg, add_first)
    v.part0[...] = v.aggt[:, R:]
    send(v.part0, v.part0r, v.s_sib.at[0, 0], v.r_sib.at[0, 0], sib)
    w_wait(0)
    v.w0h[...], v.w0l[...] = split(v.wt0[...])
    feature = lax.broadcasted_iota(jnp.int32, (FR, R), 0) < F
    v.in0h[:FR, :], v.in0l[:FR, :] = split(jnp.where(feature, v.xown[...], 0.0))
    wait_bytes(v.part0r, v.r_sib.at[0, 0])
    total = v.aggt[:, :R] + v.part0r[...]
    degree = total[F : F + 1, :]
    v.in0h[FR:, :], v.in0l[FR:, :] = split(
        jnp.where(feature, total * (1.0 / jnp.maximum(degree, 1.0)), 0.0)
    )
    v.lin[...] = dot3((v.w0h[...], v.w0l[...]), (v.in0h[...], v.in0l[...])).T
    finish(0, lambda part: None)
    degree = column(degree)
    v.degree[...] = degree
    v.linked[...] = jnp.minimum(degree, 1.0)
    v.invdeg[...] = 1.0 / jnp.maximum(degree, 1.0)
    v.count[...] = ar_wait(8)[0:2]

    for l in range(1, L):
        if l == 1:
            lax.fori_loop(0, CH, adj_turn, 0)
        w_pass(l)
        ag_forward(l, v.ag.at[l - 1])
        w_wait(l)
        v.wh[l - 1], v.wl[l - 1] = split(v.wtr[l - 1])
        total = ar_wait(l - 1)
        if l < L - 1:
            w_send(l + 1)
        keep_stats(l - 1, total)
        scale, shift = v.vecs[l - 1, 2:3, :], v.vecs[l - 1, 3:4, :]
        v.inh[l - 1, :, :H], v.inl[l - 1, :, :H] = split(v.acts[l - 1] * scale + shift)
        v.lin[...] = dot3_t(
            (v.inh[l - 1, :, :H], v.inl[l - 1, :, :H]), (v.wh[l - 1, :, :H], v.wl[l - 1, :, :H])
        )

        def add(chip, part, ref):
            high, low = split(ref[...])
            a = v.abf[chip, :, part * HALF : (part + 1) * HALF]
            v.agg[...] += dot(cat([a, a], 1), cat([high, low], 0))

        high, low = split(v.acts[l - 1])
        a = v.abf[ch]
        v.agg[...] = dot(cat([a, a], 1), cat([high, low], 0))
        ag_blocks(l, v.ag.at[l - 1], add)
        parts, partr = halves(v.parts.at[l - 1]), halves(v.partr.at[l - 1])
        for part in range(2):
            parts[part][...] = v.agg[R + part * HALF : R + (part + 1) * HALF, :]
            send(parts[part], partr[part], v.s_sib.at[l, part], v.r_sib.at[l, part], sib)

        def part_lin(part):
            r = slice(part * HALF, (part + 1) * HALF)
            wait_bytes(partr[part], v.r_sib.at[l, part])
            agg = v.agg[r, :] + partr[part][...]
            v.kept[l - 1, r, :] = agg
            v.inh[l - 1, r, H:], v.inl[l - 1, r, H:] = split(
                agg * wide(v.invdeg[r, :]) * scale + wide(v.linked[r, :]) * shift
            )
            v.lin[r, :] += dot3_t(
                (v.inh[l - 1, r, H:], v.inl[l - 1, r, H:]), (v.wh[l - 1, :, H:], v.wl[l - 1, :, H:])
            )

        finish(l, part_lin)

    for drain in drains[first_rows:]:
        drain()
    del drains[first_rows:]

    head = split(v.whp[...])
    lane = lax.broadcasted_iota(jnp.int32, (R, LANES), 1)
    onehot = jnp.where(lane.astype(F32) == v.label[...], 1.0, 0.0)
    real = lane < d.C
    counted = v.counted[...]
    label_count = jnp.max(v.count[1:2, :], axis=1, keepdims=True)
    keep_stats(L - 1, ar_wait(L - 1))
    last = split(v.acts[L - 1] * v.vecs[L - 1, 2:3, :] + v.vecs[L - 1, 3:4, :])
    logits = dot3_t(last, head) + v.biasp[...]
    top = jnp.max(jnp.where(real, logits, -3.0e38), axis=1, keepdims=True)
    moved = logits - top
    power = jnp.where(real, jnp.exp(moved), 0.0)
    power_sum = jnp.sum(power, axis=1, keepdims=True)
    g_logits = counted * (power / power_sum - onehot) / label_count
    gl_split = split(g_logits)
    v.gout[...] = dot3(gl_split, head)

    def last_sums():
        mean, inverse = v.vecs[L - 1, 0:1, :], v.vecs[L - 1, 1:2, :]

        def chunk(i, carry):
            r = rows(i, RC)
            g = v.gout[r, :]
            normed = (v.acts[L - 1, r, :] - mean) * inverse
            return (
                carry[0] + jnp.sum((g * normed).reshape(RC // 8, 8, H), axis=0),
                carry[1] + jnp.sum(g.reshape(RC // 8, 8, H), axis=0),
            )

        zero = jnp.zeros((8, H), F32)
        return [over_rows(s) for s in lax.fori_loop(0, R // RC, chunk, (zero, zero))]

    ar_put(3, last_sums())
    ar_send(3, True)
    logp = moved - jnp.log(power_sum)
    rows_loss = jnp.sum(jnp.where(real, onehot * logp, 0.0), axis=1, keepdims=True) * counted
    ar_put(6, [-over_rows(rows_loss), over_rows(g_logits)])
    ar_send(6)
    head_grad = dot3(split(g_logits.T[:CR, :]), last)
    HT = d.HT
    for t in range(HT):
        i, j = t // HV, t % HV
        v.hg[t] = head_grad[8 * i : 8 * i + 8, j * LANES : (j + 1) * LANES]

    def others(index, size, ref_of, init):
        return lax.fori_loop(1, size, lambda i, s: s + ref_of(lax.rem(index + i, size)), init)

    def head_scatter(i, carry):
        t = lax.rem(me + i, NDEV)

        def go():
            remote(v.hg.at[t], v.hrecv.at[me], v.s_h.at[0], v.r_h.at[0], device(t)).start()

        either(HT == NDEV, t < HT, go)
        return carry

    lax.fori_loop(1, NDEV, head_scatter, 0)
    drains.append(
        lambda: either(
            HT == NDEV,
            me < HT,
            lambda: wait_bytes(v.hrecv.at[pl.ds(0, HT - 1)], v.s_h.at[0]),
            lambda: wait_bytes(v.hrecv.at[pl.ds(0, HT)], v.s_h.at[0]),
        )
    )

    def head_gather():
        def go():
            wait_bytes(v.hrecv.at[pl.ds(0, NDEV - 1)], v.r_h.at[0])
            v.hfin[me] = others(me, NDEV, lambda s: v.hrecv[s], v.hg[me])

            def one(i, carry):
                remote(
                    v.hfin.at[me], v.hfin.at[me], v.s_h.at[1], v.r_h.at[1],
                    device(lax.rem(me + i, NDEV)),
                ).start()
                return carry

            lax.fori_loop(1, NDEV, one, 0)

        either(HT == NDEV, me < HT, go)
        drains.append(
            lambda: either(
                HT == NDEV,
                me < HT,
                lambda: wait_bytes(v.hrecv.at[pl.ds(0, NDEV - 1)], v.s_h.at[1]),
            )
        )

    def sibling_send(i):
        send(v.dwb.at[i, 1 - k], v.dwr.at[i], v.s_d.at[i], v.r_d.at[i], sib)

    def cols_send(i):
        wait_bytes(v.dwr.at[i], v.r_d.at[i])
        v.dwb[i, k] += v.dwr[i]
        for dd in range(1, NC):
            t = lax.rem(c + dd, NC)
            remote(v.dwb.at[i, k, t], v.zrecv.at[i, c], v.s_z.at[i], v.r_z.at[i], (n, t)).start()
        drains.append(lambda: wait_bytes(v.zrecv.at[i, pl.ds(0, NC - 1)], v.s_z.at[i]))

    def nodes_send(i):
        wait_bytes(v.zrecv.at[i, pl.ds(0, NC - 1)], v.r_z.at[i])
        v.zs[i] = others(c, NC, lambda s: v.zrecv[i, s], v.dwb[i, k, c])

        def one(j, carry):
            t = lax.rem(ch + j, CH)
            either(
                PH == CH,
                t < PH,
                lambda: remote(
                    v.zs.at[i, rows(t, RPP), :], v.nrecv.at[i, ch], v.s_n.at[i], v.r_n.at[i],
                    (t * 2 + k, c),
                ).start(),
            )
            return carry

        lax.fori_loop(1, CH, one, 0)
        drains.append(
            lambda: either(
                PH == CH,
                ch < PH,
                lambda: wait_bytes(v.zs.at[i, pl.ds(0, (PH - 1) * RPP), :], v.s_n.at[i]),
                lambda: wait_bytes(v.zs.at[i, pl.ds(0, PH * RPP), :], v.s_n.at[i]),
            )
        )

    def pieces_out(i, fin, at, piece):
        mine = pl.ds(pl.multiple_of(at, RPP), RPP)
        fin[mine, :] = piece
        square = jnp.sum((piece * piece).reshape(RPP // 8, 8, piece.shape[1]), axis=0)
        v.sq[...] += jnp.sum(square, axis=1, keepdims=True)

        def one(j, carry):
            block = fin.at[mine, :]
            remote(block, block, v.s_f.at[i], v.r_f.at[i], (lax.rem(n + j, NN), c)).start()
            return carry

        lax.fori_loop(1, NN, one, 0)

    def pieces_drain(i, fin):
        drains.append(
            lambda: either(
                PPC == NN,
                n < PPC if i == L - 1 else ch < PH,
                lambda: lax.fori_loop(
                    1, NN, lambda j, carry: (wait_bytes(fin.at[pl.ds(0, RPP), :], v.s_f.at[i]), carry)[1], 0
                ),
            )
        )

    def nodes_gather(i):
        def go():
            wait_bytes(v.nrecv.at[i, pl.ds(0, CH - 1)], v.r_n.at[i])
            piece = others(ch, CH, lambda s: v.nrecv[i, s], v.zs[i, rows(ch, RPP), :])
            pieces_out(i, v.fin.at[i], k * (HC // 2) + ch * RPP, piece)

        either(PH == CH, ch < PH, go)
        pieces_drain(i, v.fin.at[i])

    v.sq[...] = jnp.zeros((8, LANES), F32)

    def fin_wait(i, fin):
        either(
            PPC == NN,
            n < PPC if i == L - 1 else ch < PH,
            lambda: wait_bytes(fin.at[pl.ds(0, (PPC - 1) * RPP), :], v.r_f.at[i]),
            lambda: wait_bytes(fin.at[pl.ds(0, PPC * RPP), :], v.r_f.at[i]),
        )

    def give(i, src, dst):
        copy = pltpu.make_async_copy(src, dst, v.s_out.at[i])
        copy.start()
        drains.append(copy.wait)

    def linear_grad(l, a):
        total = ar_wait(a)
        g_gain, g_shift = vec(total, 0), vec(total, 1)
        v.gn_o[l, 0:1, :] = g_gain
        v.gn_o[l, 1:2, :] = g_shift
        mean, inverse, scale = v.vecs[l, 0:1, :], v.vecs[l, 1:2, :], v.vecs[l, 2:3, :]
        count = jnp.max(v.count[0:1, :], axis=1, keepdims=True)
        by_one = scale * g_shift / count
        by_normed = scale * g_gain / count

        def chunk(i, carry):
            r = rows(i, RC)
            normed = (v.acts[l, r, :] - mean) * inverse
            g_active = scale * v.gout[r, :] - wide(v.valid[r, :]) * (by_one + normed * by_normed)
            g_linear = v.gp[l, r, :] * g_active
            v.lin[r, :] = g_linear
            v.glh[r, :], v.gll[r, :] = split(g_linear)
            return carry

        lax.fori_loop(0, R // RC, chunk, 0)

    for l in (2, 1):
        g = l - 1
        linear_grad(l, 5 - l)
        gl = (v.glh[...], v.gll[...])
        back = v.ag.at[2 - l]
        v.spread[...] = dot3(gl, (v.wh[g, :, H:], v.wl[g, :, H:])) * wide(v.invdeg[...])
        v.spreads[g] = v.spread[...]
        send(v.spreads.at[g], v.spreadr.at[g], v.s_sib.at[L + g, 0], v.r_sib.at[L + g, 0], sib)
        if g == 0:
            for drain in scatter_drains:
                drain()
        own = cat(list(split(v.spread[...])), 0)
        for dd in reversed(range(CH)):
            t = v.at[0, flip(ch, dd)]
            v.out[dd] = dot(cat([t, t], 1), own)
        wait_bytes(v.spreadr.at[g], v.r_sib.at[L + g, 0])
        other = cat(list(split(v.spreadr[g])), 0)

        def complete(dd):
            t = v.at[1, flip(ch, dd)]
            v.out[dd] += dot(cat([t, t], 1), other)

        s, r = v.s_rs.at[g], v.r_rs.at[g]
        kept_drains, drains = drains, []
        if CH == 4:
            x, y, z = (halves(v.out.at[dd]) for dd in (1, 2, 3))
            from_x, from_y, via = (halves(back.at[i]) for i in range(3))
            complete(3)
            send(z[0], via[0], s.at[0], r.at[0], peer(1))
            send(z[1], via[1], s.at[1], r.at[1], peer(2))
            complete(1)
            send(x[0], from_x[0], s.at[2], r.at[2], peer(1))
            complete(2)
            send(y[1], from_y[1], s.at[3], r.at[3], peer(2))
            complete(0)
            wait_bytes(via[0], r.at[0])
            y[0][...] += via[0][...]
            send(y[0], from_y[0], s.at[5], r.at[5], peer(2))
            wait_bytes(via[1], r.at[1])
            x[1][...] += via[1][...]
            send(x[1], from_x[1], s.at[4], r.at[4], peer(1))
        else:
            for dd in reversed(range(1, CH)):
                complete(dd)
                send(v.out.at[dd], back.at[dd], s.at[dd], r.at[dd], peer(dd))
            complete(0)
        scatter_drains, drains = drains, kept_drains

        v.gout[...] = dot3(gl, (v.wh[g, :, :H], v.wl[g, :, :H]))
        mean, inverse = v.vecs[g, 0:1, :], v.vecs[g, 1:2, :]

        def chunk(i, carry):
            r = rows(i, RC)
            self, spread, degree = v.gout[r, :], v.spread[r, :], wide(v.degree[r, :])
            normed = (v.acts[g, r, :] - mean) * inverse
            reached = (v.kept[g, r, :] - degree * mean) * inverse
            v.gout[r, :] = self + v.out[0, r, :]
            return (
                carry[0] + jnp.sum((self * normed + spread * reached).reshape(RC // 8, 8, H), axis=0),
                carry[1] + jnp.sum((self + spread * degree).reshape(RC // 8, 8, H), axis=0),
            )

        zero = jnp.zeros((8, H), F32)
        ar_put(6 - l, [over_rows(s) for s in lax.fori_loop(0, R // RC, chunk, (zero, zero))])
        ar_send(6 - l)
        grad = dot3(split(v.lin[...].T), (v.inh[g], v.inl[g]))
        for t in range(NC):
            for half in range(2):
                at = t * HC + half * (HC // 2)
                v.dwb[g, half, t] = grad[at : at + HC // 2, :]
        sibling_send(g)
        if l == 2:
            head_gather()
        else:
            nodes_send(1)
        cols_send(g)
        if l == 1:
            nodes_gather(1)
        if CH == 4:
            for half, i in ((from_x[0], 2), (from_y[1], 3), (from_y[0], 5), (from_x[1], 4)):
                wait_bytes(half, r.at[i])
            v.gout[...] += back[0] + back[1]
        else:
            for dd in range(1, CH):
                wait_bytes(back.at[dd], r.at[dd])
                v.gout[...] += back[dd]
    drains += scatter_drains

    linear_grad(0, 5)
    grad = dot3_t(split(v.lin[...].T), (v.in0h[...], v.in0l[...]))
    for t in range(NC):
        v.d0[t] = grad[t * HC : (t + 1) * HC, :]

    def first_scatter(dev, t):
        tn, tc = dev
        either(
            PPC == NN,
            tn < PPC,
            lambda: remote(
                v.d0.at[tc, rows(tn, RPP), :], v.recv0.at[me], v.s_0.at[0], v.r_0.at[0], dev
            ).start(),
        )

    to_others(first_scatter, True)
    drains.append(
        lambda: either(
            PPC == NN,
            n < PPC,
            lambda: wait_bytes(v.recv0.at[pl.ds(0, PPC * NC - 1)], v.s_0.at[0]),
            lambda: wait_bytes(v.recv0.at[pl.ds(0, PPC * NC)], v.s_0.at[0]),
        )
    )
    nodes_send(0)
    nodes_gather(0)

    def first_gather():
        wait_bytes(v.recv0.at[pl.ds(0, NDEV - 1)], v.r_0.at[0])
        piece = others(me, NDEV, lambda s: v.recv0[s], v.d0[c, rows(n, RPP), :])
        pieces_out(L - 1, v.fin0, n * RPP, piece)

    either(PPC == NN, n < PPC, first_gather)
    pieces_drain(L - 1, v.fin0)
    ar_put(7, [over_rows(v.sq[...])])
    ar_send(7, True)

    total = ar_wait(6)
    bias_grad = total[1:2]
    v.misc_o[...] = jnp.zeros((8, LANES), F32)
    v.misc_o[0:1, :] = total[0:1]
    v.misc_o[1:2, :] = v.count[1:2, :]
    v.misc_o[3:4, :] = bias_grad
    either(
        HT == NDEV,
        me < HT,
        lambda: wait_bytes(v.hfin.at[pl.ds(0, HT - 1)], v.r_h.at[1]),
        lambda: wait_bytes(v.hfin.at[pl.ds(0, HT)], v.r_h.at[1]),
    )
    give(2, v.gn_o, v.gn)
    give(3, v.hfin, v.gh)
    square = jnp.zeros((8, LANES), F32)
    for t in range(HT):
        square += v.hfin[t] * v.hfin[t]
    replicated = over_rows(square) + bias_grad * bias_grad
    small = jnp.zeros((1, H), F32)
    for l in range(L):
        small += over_rows(v.gn_o[l] * v.gn_o[l])
    for j in range(HV):
        replicated += small[:, j * LANES : (j + 1) * LANES]
    for i in range(L - 1):
        fin_wait(i, v.fin.at[i])
        give(5 + i, v.fin.at[i], v.gr.at[i])
    total = ar_wait(7)
    squares = total[0:1, 0:1] + jnp.sum(replicated, axis=1, keepdims=True)
    norm = jnp.sqrt(squares)
    v.misc_o[2:3, :] = jnp.broadcast_to(norm, (1, LANES))
    v.misc_o[4:5, :] = jnp.broadcast_to(CLIP / jnp.maximum(norm, CLIP), (1, LANES))
    give(4, v.misc_o, v.misc)
    fin_wait(L - 1, v.fin0)
    give(0, v.fin0, v.g0)

    for drain in drains:
        drain()


def gradients(NN, NC, feat, adj, nm, lb, lm, w0, wr, npar, whd, bias):
    F, _, R = feat.shape
    C, H = whd.shape
    HC = w0.shape[0]
    CH, NDEV = NN // 2, NN * NC
    up = lambda size: -(-size // 8) * 8
    FR, CR = up(F + 1), up(C)
    RPP = max(8, HC // NN)
    HV = H // LANES
    d = types.SimpleNamespace(
        NN=NN, NC=NC, R=R, F=F, H=H, C=C, HC=HC, CH=CH, NDEV=NDEV, FR=FR, CR=CR, RPP=RPP,
        PPC=HC // RPP, PH=HC // RPP // 2, HV=HV, HT=CR // 8 * HV,
    )
    dma = pltpu.SemaphoreType.DMA
    L = LAYERS
    inputs = {
        "feat": feat, "adj": adj, "nm": nm, "lb": lb, "lm": lm, "w0": w0, "wr": wr, "npar": npar,
        "whd": whd, "bias": bias,
    }
    small = [name for name in inputs if name not in ("adj", "wr")]
    d.small = small
    scratch = {
        "xown": pltpu.VMEM((FR, R), F32),
        "xg": pltpu.VMEM((CH, FR, R), F32),
        "ag": pltpu.VMEM((L - 1, CH, R, H), F32),
        "acts": pltpu.VMEM((L, R, H), F32),
        "gp": pltpu.VMEM((L, R, H), F32),
        "adjb": pltpu.VMEM((2, CH, R, R), jnp.int32),
        "abf": pltpu.VMEM((CH, 2 * R, R), BF16),
        "at": pltpu.VMEM((2, CH, R, R), BF16),
        "wt0": pltpu.VMEM((H, 2 * FR), F32),
        "wtr": pltpu.VMEM((L - 1, H, 2 * H), F32),
        "w0h": pltpu.VMEM((H, 2 * FR), BF16),
        "w0l": pltpu.VMEM((H, 2 * FR), BF16),
        "wh": pltpu.VMEM((L - 1, H, 2 * H), BF16),
        "wl": pltpu.VMEM((L - 1, H, 2 * H), BF16),
        "whp": pltpu.VMEM((LANES, H), F32),
        "biasp": pltpu.VMEM((1, LANES), F32),
        "in0h": pltpu.VMEM((2 * FR, R), BF16),
        "in0l": pltpu.VMEM((2 * FR, R), BF16),
        "inh": pltpu.VMEM((L - 1, R, 2 * H), BF16),
        "inl": pltpu.VMEM((L - 1, R, 2 * H), BF16),
        "aggt": pltpu.VMEM((FR, 2 * R), F32),
        "part0": pltpu.VMEM((FR, R), F32),
        "part0r": pltpu.VMEM((FR, R), F32),
        "agg": pltpu.VMEM((2 * R, H), F32),
        "parts": pltpu.VMEM((L - 1, R, H), F32),
        "partr": pltpu.VMEM((L - 1, R, H), F32),
        "kept": pltpu.VMEM((L - 1, R, H), F32),
        "lin": pltpu.VMEM((R, H), F32),
        "gout": pltpu.VMEM((R, H), F32),
        "glh": pltpu.VMEM((R, H), BF16),
        "gll": pltpu.VMEM((R, H), BF16),
        "spread": pltpu.VMEM((R, H), F32),
        "spreads": pltpu.VMEM((L - 1, R, H), F32),
        "spreadr": pltpu.VMEM((L - 1, R, H), F32),
        "out": pltpu.VMEM((CH, R, H), F32),
        "valid": pltpu.VMEM((R, LANES), F32),
        "counted": pltpu.VMEM((R, LANES), F32),
        "label": pltpu.VMEM((R, LANES), F32),
        "degree": pltpu.VMEM((R, LANES), F32),
        "invdeg": pltpu.VMEM((R, LANES), F32),
        "linked": pltpu.VMEM((R, LANES), F32),
        "count": pltpu.VMEM((2, LANES), F32),
        "vecs": pltpu.VMEM((L, 8, H), F32),
        "sq": pltpu.VMEM((8, LANES), F32),
        "arb": pltpu.VMEM((9, NDEV, 4, LANES), F32),
        "dwb": pltpu.VMEM((L - 1, 2, NC, HC // 2, 2 * H), F32),
        "dwr": pltpu.VMEM((L - 1, NC, HC // 2, 2 * H), F32),
        "zrecv": pltpu.VMEM((L - 1, NC, HC // 2, 2 * H), F32),
        "zs": pltpu.VMEM((L - 1, HC // 2, 2 * H), F32),
        "nrecv": pltpu.VMEM((L - 1, CH, RPP, 2 * H), F32),
        "fin": pltpu.VMEM((L - 1, HC, 2 * H), F32),
        "d0": pltpu.VMEM((NC, HC, 2 * FR), F32),
        "recv0": pltpu.VMEM((NDEV, RPP, 2 * FR), F32),
        "fin0": pltpu.VMEM((HC, 2 * FR), F32),
        "hg": pltpu.VMEM((d.HT, 8, LANES), F32),
        "hrecv": pltpu.VMEM((NDEV, 8, LANES), F32),
        "hfin": pltpu.VMEM((d.HT, 8, LANES), F32),
        "ld": dma((L - 1 + len(small) + CH,)),
        "s_adj": dma((CH,)),
        "r_adj": dma((CH,)),
        "s_ag": dma((L, max(CH, 6))),
        "r_ag": dma((L, max(CH, 6))),
        "s_sib": dma((2 * L - 1, 2)),
        "r_sib": dma((2 * L - 1, 2)),
        "s_w": dma((L, NC)),
        "r_w": dma((L, NC)),
        "s_wp": dma((L, NC)),
        "r_wp": dma((L, NC)),
        "s_d": dma((L - 1,)),
        "r_d": dma((L - 1,)),
        "s_ar": dma((9,)),
        "r_ar": dma((9,)),
        "s_rs": dma((L - 1, max(CH, 6))),
        "r_rs": dma((L - 1, max(CH, 6))),
        "s_z": dma((L - 1,)),
        "r_z": dma((L - 1,)),
        "s_n": dma((L - 1,)),
        "r_n": dma((L - 1,)),
        "s_f": dma((L,)),
        "r_f": dma((L,)),
        "s_0": dma((1,)),
        "r_0": dma((1,)),
        "s_h": dma((2,)),
        "r_h": dma((2,)),
        "gn_o": pltpu.VMEM(npar.shape, F32),
        "misc_o": pltpu.VMEM((8, LANES), F32),
        "s_out": dma((L + 4,)),
    }
    for name in small:
        shape = (F, R) if name == "feat" else inputs[name].shape
        scratch[name + "_in"] = pltpu.VMEM(shape, inputs[name].dtype)
    ins = list(inputs)
    outs = ["g0", "gr", "gn", "gh", "misc"]
    d.names = ins + outs + list(scratch)
    return pl.pallas_call(
        functools.partial(step_kernel, d),
        out_shape=[
            jax.ShapeDtypeStruct((HC, 2 * FR), F32),
            jax.ShapeDtypeStruct(wr.shape, F32),
            jax.ShapeDtypeStruct(npar.shape, F32),
            jax.ShapeDtypeStruct((d.HT, 8, LANES), F32),
            jax.ShapeDtypeStruct((8, LANES), F32),
        ],
        in_specs=[pl.BlockSpec(memory_space=pl.ANY)] * len(ins),
        out_specs=[pl.BlockSpec(memory_space=pl.ANY)] * len(outs),
        scratch_shapes=list(scratch.values()),
        compiler_params=pltpu.CompilerParams(
            collective_id=0, has_side_effects=True, vmem_limit_bytes=60 * 2**20
        ),
    )(*inputs.values())


def adamw(weight, first, second, average, grad, rate):
    first = BETA_ONE * first + (1.0 - BETA_ONE) * grad
    second = BETA_TWO * second + (1.0 - BETA_TWO) * grad * grad
    fix_one = 1.0 - BETA_ONE**ADAM_STEP
    fix_two = 1.0 - BETA_TWO**ADAM_STEP
    update = first / fix_one / (jnp.sqrt(second / fix_two) + ADAM_EPS)
    weight = weight - rate * (update + DECAY * weight)
    average = AVERAGE * average + (1.0 - AVERAGE) * weight
    return (first, second, weight, average)


ORDER = (1, 0, 3, 2, 4)


def update_kernel(*refs):
    far, scalars, far_out = refs[:25], refs[25:28], refs[28:48]
    near, near_out, loaded, stored = refs[48:73], refs[73:93], refs[93], refs[94]
    loads = [pltpu.make_async_copy(a, b, loaded.at[i]) for i, (a, b) in enumerate(zip(far, near, strict=True))]
    stores = [pltpu.make_async_copy(a, b, stored.at[i]) for i, (a, b) in enumerate(zip(near_out, far_out, strict=True))]
    loads[4].start()
    for group in ORDER:
        for i in ([] if group == 4 else [group]) + [5 + group + 5 * j for j in range(4)]:
            loads[i].start()
    loads[4].wait()
    misc = near[4]
    scale = misc[4:5, 0:1]
    for i in range(3):
        scalars[i][...] = misc[i : i + 1, 0:1]
    for group in ORDER:
        for i in ([] if group == 4 else [group]) + [5 + group + 5 * j for j in range(4)]:
            loads[i].wait()
        weight, first, second, average = (near[5 + group + 5 * j] for j in range(4))
        rate = RATE_SMALL if group in (2, 4) else RATE_MATRIX
        shape = weight.shape
        if group == 4:
            grad = misc[3:4, : shape[1]]
        elif group == 3:
            wide = shape[1] // LANES
            grad = cat(
                [cat([near[3][wide * i + j] for j in range(wide)], 1) for i in range(near[3].shape[0] // wide)], 0
            )[: shape[0]]
        elif group == 0:
            half = shape[1] // 2
            at = near[0].shape[1] // 2
            grad = cat([near[0][:, :half], near[0][:, at : at + half]], 1)
        else:
            grad = near[group][...]
        done = adamw(weight[...], first[...], second[...], average[...], grad * scale, rate)
        for i, value in enumerate(done):
            near_out[4 * group + i][...] = value
            stores[4 * group + i].start()
    for store in stores:
        store.wait()


def local(
    nodes, cols, features, adjacency, node_mask, labels, label_mask, *state
):
    turn = (
        lambda a: a.T,
        lambda a: a.transpose(0, 2, 1),
        lambda a: a.transpose(1, 0, 2),
        lambda a: a.T,
        lambda a: a.reshape(1, -1),
    )
    back = turn[:4] + (lambda a: a.reshape(-1),)
    state = [turn[i % 5](a) for i, a in enumerate(state)]
    grads = gradients(
        nodes, cols, features.transpose(2, 0, 1), adjacency[0], node_mask, labels, label_mask, *state[:5]
    )
    outs = [jax.ShapeDtypeStruct((1, 1), F32)] * 3
    outs += [jax.ShapeDtypeStruct(a.shape, F32) for a in state[:5] for _ in range(4)]
    far = pl.BlockSpec(memory_space=pl.ANY)
    given = [*grads, *state]
    done = pl.pallas_call(
        update_kernel,
        out_shape=outs,
        in_specs=[far] * len(given),
        out_specs=[pl.BlockSpec(memory_space=pltpu.VMEM)] * 3 + [far] * (len(outs) - 3),
        scratch_shapes=[pltpu.VMEM(a.shape, F32) for a in [*given, *outs[3:]]]
        + [pltpu.SemaphoreType.DMA((25,)), pltpu.SemaphoreType.DMA((20,))],
    )(*given)
    return (
        *(a.reshape(()) for a in done[:3]),
        *(back[i // 4](a) for i, a in enumerate(done[3:])),
    )


def solution(mesh):
    rows, first, rest, all_of = P("cols", "nodes", None), P(None, "cols"), P(None, None, "cols"), P()
    state = [first, rest, all_of, all_of, all_of]
    return jax.shard_map(
        functools.partial(local, mesh.shape["nodes"], mesh.shape["cols"]),
        mesh=mesh,
        in_specs=(rows, rows) + (P("cols", "nodes"),) * 3 + tuple(state * 4),
        out_specs=(all_of,) * 3 + tuple(spec for spec in state for _ in range(4)),
        check_vma=False,
    )
```

```python
import functools
import types

import jax
import jax.numpy as jnp
from jax import lax
from jax.experimental import pallas as pl
from jax.experimental.pallas import tpu as pltpu
from jax.sharding import PartitionSpec as P

LAYERS = 3
ADAM_STEP = 10
CLIP = 0.02
RATE_MATRIX = 0.03
RATE_SMALL = 0.3
BETA_ONE = 0.9
BETA_TWO = 0.999
ADAM_EPS = 1e-08
DECAY = 0.01
AVERAGE = 0.9
NORM_EPS = 1e-05

MESH = pl.DeviceIdType.MESH
F32 = jnp.float32
BF16 = jnp.bfloat16
LANES = 128
GELU_OUT = 0.7978845608028654
GELU_CUBE = 0.044715


def cat(values, axis):
    return values[0] if len(values) == 1 else jnp.concatenate(values, axis=axis)


def split(value):
    high = value.astype(BF16)
    return high, (value - high.astype(F32)).astype(BF16)


def dot(left, right):
    return lax.dot_general(left, right, (((1,), (0,)), ((), ())), preferred_element_type=F32)


def dot_t(left, right):
    return lax.dot_general(left, right, (((1,), (1,)), ((), ())), preferred_element_type=F32)


def dot3(left, right):
    (lh, ll), (rh, rl) = left, right
    return dot(cat([lh, lh, ll], 1), cat([rh, rl, rh], 0))


def dot3_t(left, right):
    (lh, ll), (rh, rl) = left, right
    return dot_t(cat([lh, lh, ll], 1), cat([rh, rl, rh], 1))


def remote(src, dst, send, recv, device):
    return pltpu.make_async_remote_copy(
        src_ref=src, dst_ref=dst, send_sem=send, recv_sem=recv, device_id=device, device_id_type=MESH
    )


def wait_bytes(ref, sem):
    pltpu.make_async_copy(ref, ref, sem).wait()


def flip(index, distance):
    bit = 1
    while bit <= distance:
        if distance & bit:
            index = index + (1 - 2 * lax.rem(lax.div(index, bit), 2)) * bit
        bit *= 2
    return index


def step_kernel(d, *refs):
    v = types.SimpleNamespace(**dict(zip(d.names, refs, strict=True)))
    NN, NC, R, H, HC, CH, L = d.NN, d.NC, d.R, d.H, d.HC, d.CH, LAYERS
    NDEV, RPP, PPC, PH, HV, F, FR, CR = d.NDEV, d.RPP, d.PPC, d.PH, d.HV, d.F, d.FR, d.CR
    n, c = lax.axis_index("nodes"), lax.axis_index("cols")
    me = n * NC + c
    ch, k = lax.div(n, 2), lax.rem(n, 2)
    sib = (ch * 2 + 1 - k, c)
    drains = []

    def device(index):
        return lax.div(index, NC), lax.rem(index, NC)

    def peer(dd):
        return flip(ch, dd) * 2 + k, c

    def rows(i, size):
        return pl.ds(pl.multiple_of(i * size, size), size)

    def send(src, dst, ssem, rsem, dev):
        remote(src, dst, ssem, rsem, dev).start()
        drains.append(lambda: wait_bytes(src, ssem))

    def either(always, condition, fn, other=None):
        if always:
            fn()
            return

        @pl.when(condition)
        def _():
            fn()

        if other is not None:

            @pl.when(jnp.logical_not(condition))
            def _():
                other()

    barrier = pltpu.get_barrier_semaphore()

    def adj_cols(j, core):
        return v.adj.at[:, rows(j * 2 + core, R)]

    own_rows = rows(c, HC)
    w_loads = [
        pltpu.make_async_copy(v.wr.at[i], v.wtr.at[i, own_rows, :], v.ld.at[i]) for i in range(L - 1)
    ]
    small_loads = [
        pltpu.make_async_copy(
            v.feat.at[:, 0, :] if name == "feat" else getattr(v, name),
            getattr(v, name + "_in"),
            v.ld.at[L - 1 + i],
        )
        for i, name in enumerate(d.small)
    ]
    for copy in small_loads + w_loads:
        copy.start()
    base = L - 1 + len(d.small)
    for j in range(CH):
        pltpu.make_async_copy(adj_cols(j, k), v.adjb.at[0, j], v.ld.at[base + j]).start()
    def greet(i, carry):
        pl.semaphore_signal(
            barrier, inc=1, device_id=device(lax.rem(me + i, NDEV)), device_id_type=MESH
        )
        return carry

    lax.fori_loop(1, NDEV, greet, 0)

    small_loads[0].wait()
    v.xown[:F, :] = v.feat_in[...]
    v.xown[F:, :] = jnp.ones((FR - F, R), F32)
    pl.semaphore_wait(barrier, NDEV - 1)

    def halves(ref):
        size = ref.shape[0]
        first = -(-size // 16) * 8
        return ref.at[:first], ref.at[first:]

    def ag_send(g, src, buf, part):
        s, r = v.s_ag.at[g], v.r_ag.at[g]
        mine = halves(src)
        slot = halves(buf.at[ch])
        if CH == 4:
            send(mine[part], slot[part], s.at[part], r.at[part], peer(1))
            if part == 1:
                send(mine[1], slot[1], s.at[3], r.at[3], peer(2))
                send(mine[0], slot[0], s.at[2], r.at[2], peer(2))
        elif part == 1:
            for dd in reversed(range(1, CH)):
                send(src, buf.at[ch], s.at[dd], r.at[dd], peer(dd))

    def ag_forward(g, buf):
        s, r = v.s_ag.at[g], v.r_ag.at[g]
        if CH == 4:
            x, y = (halves(buf.at[flip(ch, dd)]) for dd in (1, 2))
            wait_bytes(x[0], r.at[0])
            send(x[0], x[0], s.at[4], r.at[4], peer(2))
            wait_bytes(y[1], r.at[3])
            send(y[1], y[1], s.at[5], r.at[5], peer(1))

    def ag_blocks(g, buf, add):
        r = v.r_ag.at[g]
        if CH == 4:
            x, y, z = (halves(buf.at[flip(ch, dd)]) for dd in (1, 2, 3))
            add(flip(ch, 1), 0, x[0])
            add(flip(ch, 2), 1, y[1])
            wait_bytes(x[1], r.at[1])
            add(flip(ch, 1), 1, x[1])
            wait_bytes(y[0], r.at[2])
            add(flip(ch, 2), 0, y[0])
            wait_bytes(z[0], r.at[4])
            add(flip(ch, 3), 0, z[0])
            wait_bytes(z[1], r.at[5])
            add(flip(ch, 3), 1, z[1])
        else:
            for dd in range(1, CH):
                wait_bytes(buf.at[flip(ch, dd)], r.at[dd])
                for part in range(2):
                    add(flip(ch, dd), part, halves(buf.at[flip(ch, dd)])[part])

    def to_others(start, at_once=False):
        if at_once and NDEV <= 32:
            for dc in [*reversed(range(1, NC)), 0]:
                for dn in reversed(range(NN)):
                    if dn or dc:
                        tn, tc = lax.rem(n + dn, NN) if dn else n, lax.rem(c + dc, NC) if dc else c
                        start((tn, tc), tn * NC + tc)
            return

        def one(i, carry):
            t = lax.rem(me + i, NDEV)
            start(device(t), t)
            return carry

        lax.fori_loop(1, NDEV, one, 0)

    def ar_send(a, at_once=False):
        to_others(
            lambda dev, t: remote(
                v.arb.at[a, me], v.arb.at[a, me], v.s_ar.at[a], v.r_ar.at[a], dev
            ).start(),
            at_once,
        )
        drains.append(lambda: wait_bytes(v.arb.at[a, pl.ds(0, NDEV - 1)], v.s_ar.at[a]))

    def ar_put(a, vectors):
        at = 0
        for vec in vectors:
            for i in range(vec.shape[1] // LANES):
                v.arb[a, me, at : at + 1, :] = vec[:, i * LANES : (i + 1) * LANES]
                at += 1
        if at < 4:
            v.arb[a, me, at:, :] = jnp.zeros((4 - at, LANES), F32)

    def ar_wait(a):
        wait_bytes(v.arb.at[a, pl.ds(0, NDEV - 1)], v.r_ar.at[a])
        return jnp.sum(v.arb[a], axis=0)

    def vec(total, i):
        return cat([total[i * HV + j : i * HV + j + 1] for j in range(HV)], 1)

    for part in range(2):
        ag_send(0, v.xown, v.xg, part)

    def w_ref(l):
        return v.wt0 if l == 0 else v.wtr.at[l - 1]

    def w_half(l, dd, core):
        at = lax.rem(c + dd, NC) * HC + core * (HC // 2)
        return w_ref(l).at[pl.ds(pl.multiple_of(at, HC // 2), HC // 2), :]

    def w_send(l):
        block = w_half(l, 0, k)
        for dd in range(1, NC):
            send(block, block, v.s_w.at[l, dd], v.r_w.at[l, dd], (n, lax.rem(c + dd, NC)))

    def w_pass(l):
        for dd in range(1, NC):
            block = w_half(l, NC - dd, k)
            wait_bytes(block, v.r_w.at[l, dd])
            send(block, block, v.s_wp.at[l, dd], v.r_wp.at[l, dd], sib)

    def w_wait(l):
        for dd in range(1, NC):
            wait_bytes(w_half(l, NC - dd, 1 - k), v.r_wp.at[l, dd])

    for copy in small_loads[1:]:
        copy.wait()
    v.wt0[own_rows, :] = jnp.zeros((HC, 2 * FR), F32)
    v.wt0[own_rows, :F] = v.w0_in[:, :F]
    v.wt0[own_rows, FR : FR + F] = v.w0_in[:, F:]
    w_send(0)
    for j in range(CH):
        send(adj_cols(j, 1 - k), v.adjb.at[1, j], v.s_adj.at[j], v.r_adj.at[j], sib)
    w_loads[0].wait()
    w_send(1)
    for copy in w_loads[1:]:
        copy.wait()

    def column(row):
        return jnp.broadcast_to(row.astype(F32), (LANES, R)).T

    v.valid[...] = column(v.nm_in[...])
    v.counted[...] = column(v.lm_in[...] * v.nm_in[...])
    v.label[...] = column(v.lb_in[...])
    v.whp[...] = jnp.zeros(v.whp.shape, F32)
    v.whp[: d.C, :] = v.whd_in[...]
    v.biasp[...] = jnp.zeros(v.biasp.shape, F32)
    v.biasp[:, : d.C] = v.bias_in[...]
    ar_put(
        8,
        [
            jnp.sum(v.valid[...], axis=0, keepdims=True),
            jnp.sum(v.counted[...], axis=0, keepdims=True),
        ],
    )
    ar_send(8)

    def adj_own(j, carry):
        pltpu.make_async_copy(adj_cols(j, k), v.adjb.at[0, j], v.ld.at[base + j]).wait()
        v.abf[j, :R, :] = v.adjb[0, j].astype(F32).astype(BF16)
        return carry

    def adj_sib(j, carry):
        wait_bytes(v.adjb.at[1, j], v.r_adj.at[j])
        v.abf[j, R:, :] = v.adjb[1, j].astype(F32).astype(BF16)
        return carry

    def adj_turn(j, carry):
        for side in range(2):
            v.at[side, j] = v.adjb[side, j].astype(F32).T.astype(BF16)
        return carry

    lax.fori_loop(0, CH, adj_own, 0)
    first_rows = len(drains)
    ag_forward(0, v.xg)
    lax.fori_loop(0, CH, adj_sib, 0)

    def wide(value):
        return cat([value] * HV, 1)

    RC = min(R // 2, 64)
    HALF = R // 2

    def activate(l, part):
        def chunk(i, carry):
            r = rows(i, RC)
            x = v.lin[r, :]
            square = x * x
            t = jnp.tanh(GELU_OUT * x * (1.0 + GELU_CUBE * square))
            half = 0.5 * (1.0 + t)
            act = x * half
            v.acts[l, r, :] = act
            v.gp[l, r, :] = half + (0.5 * GELU_OUT) * x * (1.0 - t * t) * (
                1.0 + (3.0 * GELU_CUBE) * square
            )
            masked = wide(v.valid[r, :]) * act
            return (
                carry[0] + jnp.sum(masked.reshape(RC // 8, 8, H), axis=0),
                carry[1] + jnp.sum((masked * act).reshape(RC // 8, 8, H), axis=0),
            )

        zero = jnp.zeros((8, H), F32)
        per = HALF // RC
        return lax.fori_loop(part * per, (part + 1) * per, chunk, (zero, zero))

    def over_rows(value):
        return jnp.sum(value, axis=0, keepdims=True)

    def keep_stats(l, total):
        count = jnp.max(v.count[0:1, :], axis=1, keepdims=True)
        mean = vec(total, 0) / count
        var = vec(total, 1) / count - mean * mean
        inverse = lax.rsqrt(var + NORM_EPS)
        gain, shift = v.npar_in[l, 0:1, :], v.npar_in[l, 1:2, :]
        v.vecs[l, 0:1, :] = mean
        v.vecs[l, 1:2, :] = inverse
        v.vecs[l, 2:3, :] = gain * inverse
        v.vecs[l, 3:4, :] = shift - mean * (gain * inverse)

    def finish(l, part_lin):
        sums = []
        for part in range(2):
            part_lin(part)
            sums.append(activate(l, part))
            if l < L - 1:
                ag_send(l + 1, v.acts.at[l], v.ag.at[l], part)
        ar_put(l, [over_rows(sums[0][i] + sums[1][i]) for i in range(2)])
        ar_send(l, l == L - 1)

    def add_first(chip, part, ref):
        high, low = split(ref[...])
        a = v.abf[chip]
        got = dot_t(cat([high, low], 1), cat([a, a], 1))
        first = -(-FR // 16) * 8
        r = slice(0, first) if part == 0 else slice(first, FR)
        seen = v.aggt[r, :]
        v.aggt[r, :] = seen + got

    v.aggt[...] = jnp.zeros((FR, 2 * R), F32)
    for part in range(2):
        add_first(ch, part, halves(v.xown)[part])
    w_pass(0)
    ag_blocks(0, v.xg, add_first)
    v.part0[...] = v.aggt[:, R:]
    send(v.part0, v.part0r, v.s_sib.at[0, 0], v.r_sib.at[0, 0], sib)
    w_wait(0)
    v.w0h[...], v.w0l[...] = split(v.wt0[...])
    feature = lax.broadcasted_iota(jnp.int32, (FR, R), 0) < F
    v.in0h[:FR, :], v.in0l[:FR, :] = split(jnp.where(feature, v.xown[...], 0.0))
    wait_bytes(v.part0r, v.r_sib.at[0, 0])
    total = v.aggt[:, :R] + v.part0r[...]
    degree = total[F : F + 1, :]
    v.in0h[FR:, :], v.in0l[FR:, :] = split(
        jnp.where(feature, total * (1.0 / jnp.maximum(degree, 1.0)), 0.0)
    )
    v.lin[...] = dot3((v.w0h[...], v.w0l[...]), (v.in0h[...], v.in0l[...])).T
    finish(0, lambda part: None)
    degree = column(degree)
    v.degree[...] = degree
    v.linked[...] = jnp.minimum(degree, 1.0)
    v.invdeg[...] = 1.0 / jnp.maximum(degree, 1.0)
    v.count[...] = ar_wait(8)[0:2]

    for l in range(1, L):
        if l == 1:
            lax.fori_loop(0, CH, adj_turn, 0)
        w_pass(l)
        ag_forward(l, v.ag.at[l - 1])
        w_wait(l)
        v.wh[l - 1], v.wl[l - 1] = split(v.wtr[l - 1])
        total = ar_wait(l - 1)
        if l < L - 1:
            w_send(l + 1)
        keep_stats(l - 1, total)
        scale, shift = v.vecs[l - 1, 2:3, :], v.vecs[l - 1, 3:4, :]
        v.inh[l - 1, :, :H], v.inl[l - 1, :, :H] = split(v.acts[l - 1] * scale + shift)
        v.lin[...] = dot3_t(
            (v.inh[l - 1, :, :H], v.inl[l - 1, :, :H]), (v.wh[l - 1, :, :H], v.wl[l - 1, :, :H])
        )

        def add(chip, part, ref):
            high, low = split(ref[...])
            a = v.abf[chip, :, part * HALF : (part + 1) * HALF]
            v.agg[...] += dot(cat([a, a], 1), cat([high, low], 0))

        high, low = split(v.acts[l - 1])
        a = v.abf[ch]
        v.agg[...] = dot(cat([a, a], 1), cat([high, low], 0))
        ag_blocks(l, v.ag.at[l - 1], add)
        parts, partr = halves(v.parts.at[l - 1]), halves(v.partr.at[l - 1])
        for part in range(2):
            parts[part][...] = v.agg[R + part * HALF : R + (part + 1) * HALF, :]
            send(parts[part], partr[part], v.s_sib.at[l, part], v.r_sib.at[l, part], sib)

        def part_lin(part):
            r = slice(part * HALF, (part + 1) * HALF)
            wait_bytes(partr[part], v.r_sib.at[l, part])
            agg = v.agg[r, :] + partr[part][...]
            v.kept[l - 1, r, :] = agg
            v.inh[l - 1, r, H:], v.inl[l - 1, r, H:] = split(
                agg * wide(v.invdeg[r, :]) * scale + wide(v.linked[r, :]) * shift
            )
            v.lin[r, :] += dot3_t(
                (v.inh[l - 1, r, H:], v.inl[l - 1, r, H:]), (v.wh[l - 1, :, H:], v.wl[l - 1, :, H:])
            )

        finish(l, part_lin)

    for drain in drains[first_rows:]:
        drain()
    del drains[first_rows:]

    head = split(v.whp[...])
    lane = lax.broadcasted_iota(jnp.int32, (R, LANES), 1)
    onehot = jnp.where(lane.astype(F32) == v.label[...], 1.0, 0.0)
    real = lane < d.C
    counted = v.counted[...]
    label_count = jnp.max(v.count[1:2, :], axis=1, keepdims=True)
    keep_stats(L - 1, ar_wait(L - 1))
    last = split(v.acts[L - 1] * v.vecs[L - 1, 2:3, :] + v.vecs[L - 1, 3:4, :])
    logits = dot3_t(last, head) + v.biasp[...]
    top = jnp.max(jnp.where(real, logits, -3.0e38), axis=1, keepdims=True)
    moved = logits - top
    power = jnp.where(real, jnp.exp(moved), 0.0)
    power_sum = jnp.sum(power, axis=1, keepdims=True)
    g_logits = counted * (power / power_sum - onehot) / label_count
    gl_split = split(g_logits)
    v.gout[...] = dot3(gl_split, head)

    def last_sums():
        mean, inverse = v.vecs[L - 1, 0:1, :], v.vecs[L - 1, 1:2, :]

        def chunk(i, carry):
            r = rows(i, RC)
            g = v.gout[r, :]
            normed = (v.acts[L - 1, r, :] - mean) * inverse
            return (
                carry[0] + jnp.sum((g * normed).reshape(RC // 8, 8, H), axis=0),
                carry[1] + jnp.sum(g.reshape(RC // 8, 8, H), axis=0),
            )

        zero = jnp.zeros((8, H), F32)
        return [over_rows(s) for s in lax.fori_loop(0, R // RC, chunk, (zero, zero))]

    ar_put(3, last_sums())
    ar_send(3, True)
    logp = moved - jnp.log(power_sum)
    rows_loss = jnp.sum(jnp.where(real, onehot * logp, 0.0), axis=1, keepdims=True) * counted
    ar_put(6, [-over_rows(rows_loss), over_rows(g_logits)])
    ar_send(6)
    head_grad = dot3(split(g_logits.T[:CR, :]), last)
    HT = d.HT
    for t in range(HT):
        i, j = t // HV, t % HV
        v.hg[t] = head_grad[8 * i : 8 * i + 8, j * LANES : (j + 1) * LANES]

    def others(index, size, ref_of, init):
        return lax.fori_loop(1, size, lambda i, s: s + ref_of(lax.rem(index + i, size)), init)

    def head_scatter(i, carry):
        t = lax.rem(me + i, NDEV)

        def go():
            remote(v.hg.at[t], v.hrecv.at[me], v.s_h.at[0], v.r_h.at[0], device(t)).start()

        either(HT == NDEV, t < HT, go)
        return carry

    lax.fori_loop(1, NDEV, head_scatter, 0)
    drains.append(
        lambda: either(
            HT == NDEV,
            me < HT,
            lambda: wait_bytes(v.hrecv.at[pl.ds(0, HT - 1)], v.s_h.at[0]),
            lambda: wait_bytes(v.hrecv.at[pl.ds(0, HT)], v.s_h.at[0]),
        )
    )

    def head_gather():
        def go():
            wait_bytes(v.hrecv.at[pl.ds(0, NDEV - 1)], v.r_h.at[0])
            v.hfin[me] = others(me, NDEV, lambda s: v.hrecv[s], v.hg[me])

            def one(i, carry):
                remote(
                    v.hfin.at[me], v.hfin.at[me], v.s_h.at[1], v.r_h.at[1],
                    device(lax.rem(me + i, NDEV)),
                ).start()
                return carry

            lax.fori_loop(1, NDEV, one, 0)

        either(HT == NDEV, me < HT, go)
        drains.append(
            lambda: either(
                HT == NDEV,
                me < HT,
                lambda: wait_bytes(v.hrecv.at[pl.ds(0, NDEV - 1)], v.s_h.at[1]),
            )
        )

    def sibling_send(i):
        send(v.dwb.at[i, 1 - k], v.dwr.at[i], v.s_d.at[i], v.r_d.at[i], sib)

    def cols_send(i):
        wait_bytes(v.dwr.at[i], v.r_d.at[i])
        v.dwb[i, k] += v.dwr[i]
        for dd in range(1, NC):
            t = lax.rem(c + dd, NC)
            remote(v.dwb.at[i, k, t], v.zrecv.at[i, c], v.s_z.at[i], v.r_z.at[i], (n, t)).start()
        drains.append(lambda: wait_bytes(v.zrecv.at[i, pl.ds(0, NC - 1)], v.s_z.at[i]))

    def nodes_send(i):
        wait_bytes(v.zrecv.at[i, pl.ds(0, NC - 1)], v.r_z.at[i])
        v.zs[i] = others(c, NC, lambda s: v.zrecv[i, s], v.dwb[i, k, c])

        def one(j, carry):
            t = lax.rem(ch + j, CH)
            either(
                PH == CH,
                t < PH,
                lambda: remote(
                    v.zs.at[i, rows(t, RPP), :], v.nrecv.at[i, ch], v.s_n.at[i], v.r_n.at[i],
                    (t * 2 + k, c),
                ).start(),
            )
            return carry

        lax.fori_loop(1, CH, one, 0)
        drains.append(
            lambda: either(
                PH == CH,
                ch < PH,
                lambda: wait_bytes(v.zs.at[i, pl.ds(0, (PH - 1) * RPP), :], v.s_n.at[i]),
                lambda: wait_bytes(v.zs.at[i, pl.ds(0, PH * RPP), :], v.s_n.at[i]),
            )
        )

    def pieces_out(i, fin, at, piece):
        mine = pl.ds(pl.multiple_of(at, RPP), RPP)
        fin[mine, :] = piece
        square = jnp.sum((piece * piece).reshape(RPP // 8, 8, piece.shape[1]), axis=0)
        v.sq[...] += jnp.sum(square, axis=1, keepdims=True)

        def one(j, carry):
            block = fin.at[mine, :]
            remote(block, block, v.s_f.at[i], v.r_f.at[i], (lax.rem(n + j, NN), c)).start()
            return carry

        lax.fori_loop(1, NN, one, 0)

    def pieces_drain(i, fin):
        drains.append(
            lambda: either(
                PPC == NN,
                n < PPC if i == L - 1 else ch < PH,
                lambda: lax.fori_loop(
                    1, NN, lambda j, carry: (wait_bytes(fin.at[pl.ds(0, RPP), :], v.s_f.at[i]), carry)[1], 0
                ),
            )
        )

    def nodes_gather(i):
        def go():
            wait_bytes(v.nrecv.at[i, pl.ds(0, CH - 1)], v.r_n.at[i])
            piece = others(ch, CH, lambda s: v.nrecv[i, s], v.zs[i, rows(ch, RPP), :])
            pieces_out(i, v.fin.at[i], k * (HC // 2) + ch * RPP, piece)

        either(PH == CH, ch < PH, go)
        pieces_drain(i, v.fin.at[i])

    v.sq[...] = jnp.zeros((8, LANES), F32)

    def fin_wait(i, fin):
        either(
            PPC == NN,
            n < PPC if i == L - 1 else ch < PH,
            lambda: wait_bytes(fin.at[pl.ds(0, (PPC - 1) * RPP), :], v.r_f.at[i]),
            lambda: wait_bytes(fin.at[pl.ds(0, PPC * RPP), :], v.r_f.at[i]),
        )

    def give(i, src, dst):
        copy = pltpu.make_async_copy(src, dst, v.s_out.at[i])
        copy.start()
        drains.append(copy.wait)

    def linear_grad(l, a):
        total = ar_wait(a)
        g_gain, g_shift = vec(total, 0), vec(total, 1)
        v.gn_o[l, 0:1, :] = g_gain
        v.gn_o[l, 1:2, :] = g_shift
        mean, inverse, scale = v.vecs[l, 0:1, :], v.vecs[l, 1:2, :], v.vecs[l, 2:3, :]
        count = jnp.max(v.count[0:1, :], axis=1, keepdims=True)
        by_one = scale * g_shift / count
        by_normed = scale * g_gain / count

        def chunk(i, carry):
            r = rows(i, RC)
            normed = (v.acts[l, r, :] - mean) * inverse
            g_active = scale * v.gout[r, :] - wide(v.valid[r, :]) * (by_one + normed * by_normed)
            g_linear = v.gp[l, r, :] * g_active
            v.lin[r, :] = g_linear
            v.glh[r, :], v.gll[r, :] = split(g_linear)
            return carry

        lax.fori_loop(0, R // RC, chunk, 0)

    for l in (2, 1):
        g = l - 1
        linear_grad(l, 5 - l)
        gl = (v.glh[...], v.gll[...])
        back = v.ag.at[2 - l]
        v.spread[...] = dot3(gl, (v.wh[g, :, H:], v.wl[g, :, H:])) * wide(v.invdeg[...])
        v.spreads[g] = v.spread[...]
        send(v.spreads.at[g], v.spreadr.at[g], v.s_sib.at[L + g, 0], v.r_sib.at[L + g, 0], sib)
        if g == 0:
            for drain in scatter_drains:
                drain()
        own = cat(list(split(v.spread[...])), 0)
        for dd in reversed(range(CH)):
            t = v.at[0, flip(ch, dd)]
            v.out[dd] = dot(cat([t, t], 1), own)
        wait_bytes(v.spreadr.at[g], v.r_sib.at[L + g, 0])
        other = cat(list(split(v.spreadr[g])), 0)

        def complete(dd):
            t = v.at[1, flip(ch, dd)]
            v.out[dd] += dot(cat([t, t], 1), other)

        s, r = v.s_rs.at[g], v.r_rs.at[g]
        kept_drains, drains = drains, []
        if CH == 4:
            x, y, z = (halves(v.out.at[dd]) for dd in (1, 2, 3))
            from_x, from_y, via = (halves(back.at[i]) for i in range(3))
            complete(3)
            send(z[0], via[0], s.at[0], r.at[0], peer(1))
            send(z[1], via[1], s.at[1], r.at[1], peer(2))
            complete(1)
            send(x[0], from_x[0], s.at[2], r.at[2], peer(1))
            complete(2)
            send(y[1], from_y[1], s.at[3], r.at[3], peer(2))
            complete(0)
        else:
            for dd in reversed(range(1, CH)):
                complete(dd)
                send(v.out.at[dd], back.at[dd], s.at[dd], r.at[dd], peer(dd))
            complete(0)
        v.gout[...] = dot3(gl, (v.wh[g, :, :H], v.wl[g, :, :H]))
        mean, inverse = v.vecs[g, 0:1, :], v.vecs[g, 1:2, :]

        def chunk(i, carry):
            r = rows(i, RC)
            self, spread, degree = v.gout[r, :], v.spread[r, :], wide(v.degree[r, :])
            normed = (v.acts[g, r, :] - mean) * inverse
            reached = (v.kept[g, r, :] - degree * mean) * inverse
            v.gout[r, :] = self + v.out[0, r, :]
            return (
                carry[0] + jnp.sum((self * normed + spread * reached).reshape(RC // 8, 8, H), axis=0),
                carry[1] + jnp.sum((self + spread * degree).reshape(RC // 8, 8, H), axis=0),
            )

        zero = jnp.zeros((8, H), F32)
        ar_put(6 - l, [over_rows(t) for t in lax.fori_loop(0, R // RC, chunk, (zero, zero))])
        ar_send(6 - l, True)
        if CH == 4:
            wait_bytes(via[0], r.at[0])
            y[0][...] += via[0][...]
            send(y[0], from_y[0], s.at[5], r.at[5], peer(2))
            wait_bytes(via[1], r.at[1])
            x[1][...] += via[1][...]
            send(x[1], from_x[1], s.at[4], r.at[4], peer(1))
        scatter_drains, drains = drains, kept_drains
        grad = dot3(split(v.lin[...].T), (v.inh[g], v.inl[g]))
        for t in range(NC):
            for half in range(2):
                at = t * HC + half * (HC // 2)
                v.dwb[g, half, t] = grad[at : at + HC // 2, :]
        sibling_send(g)
        if l == 2:
            head_gather()
        else:
            nodes_send(1)
        cols_send(g)
        if l == 1:
            nodes_gather(1)
        if CH == 4:
            for half, i in ((from_x[0], 2), (from_y[1], 3), (from_y[0], 5), (from_x[1], 4)):
                wait_bytes(half, r.at[i])
            v.gout[...] += back[0] + back[1]
        else:
            for dd in range(1, CH):
                wait_bytes(back.at[dd], r.at[dd])
                v.gout[...] += back[dd]
    drains += scatter_drains

    linear_grad(0, 5)
    grad = dot3_t(split(v.lin[...].T), (v.in0h[...], v.in0l[...]))
    for t in range(NC):
        v.d0[t] = grad[t * HC : (t + 1) * HC, :]

    def first_scatter(dev, t):
        tn, tc = dev
        either(
            PPC == NN,
            tn < PPC,
            lambda: remote(
                v.d0.at[tc, rows(tn, RPP), :], v.recv0.at[me], v.s_0.at[0], v.r_0.at[0], dev
            ).start(),
        )

    to_others(first_scatter, True)
    drains.append(
        lambda: either(
            PPC == NN,
            n < PPC,
            lambda: wait_bytes(v.recv0.at[pl.ds(0, PPC * NC - 1)], v.s_0.at[0]),
            lambda: wait_bytes(v.recv0.at[pl.ds(0, PPC * NC)], v.s_0.at[0]),
        )
    )
    nodes_send(0)
    nodes_gather(0)

    def first_gather():
        wait_bytes(v.recv0.at[pl.ds(0, NDEV - 1)], v.r_0.at[0])
        piece = others(me, NDEV, lambda s: v.recv0[s], v.d0[c, rows(n, RPP), :])
        pieces_out(L - 1, v.fin0, n * RPP, piece)

    either(PPC == NN, n < PPC, first_gather)
    pieces_drain(L - 1, v.fin0)
    ar_put(7, [over_rows(v.sq[...])])
    ar_send(7, True)

    total = ar_wait(6)
    bias_grad = total[1:2]
    v.misc_o[...] = jnp.zeros((8, LANES), F32)
    v.misc_o[0:1, :] = total[0:1]
    v.misc_o[1:2, :] = v.count[1:2, :]
    v.misc_o[3:4, :] = bias_grad
    either(
        HT == NDEV,
        me < HT,
        lambda: wait_bytes(v.hfin.at[pl.ds(0, HT - 1)], v.r_h.at[1]),
        lambda: wait_bytes(v.hfin.at[pl.ds(0, HT)], v.r_h.at[1]),
    )
    give(2, v.gn_o, v.gn)
    give(3, v.hfin, v.gh)
    square = jnp.zeros((8, LANES), F32)
    for t in range(HT):
        square += v.hfin[t] * v.hfin[t]
    replicated = over_rows(square) + bias_grad * bias_grad
    small = jnp.zeros((1, H), F32)
    for l in range(L):
        small += over_rows(v.gn_o[l] * v.gn_o[l])
    for j in range(HV):
        replicated += small[:, j * LANES : (j + 1) * LANES]
    for i in range(L - 1):
        fin_wait(i, v.fin.at[i])
        give(5 + i, v.fin.at[i], v.gr.at[i])
    total = ar_wait(7)
    squares = total[0:1, 0:1] + jnp.sum(replicated, axis=1, keepdims=True)
    norm = jnp.sqrt(squares)
    v.misc_o[2:3, :] = jnp.broadcast_to(norm, (1, LANES))
    v.misc_o[4:5, :] = jnp.broadcast_to(CLIP / jnp.maximum(norm, CLIP), (1, LANES))
    give(4, v.misc_o, v.misc)
    fin_wait(L - 1, v.fin0)
    give(0, v.fin0, v.g0)

    for drain in drains:
        drain()


def gradients(NN, NC, feat, adj, nm, lb, lm, w0, wr, npar, whd, bias):
    F, _, R = feat.shape
    C, H = whd.shape
    HC = w0.shape[0]
    CH, NDEV = NN // 2, NN * NC
    up = lambda size: -(-size // 8) * 8
    FR, CR = up(F + 1), up(C)
    RPP = max(8, HC // NN)
    HV = H // LANES
    d = types.SimpleNamespace(
        NN=NN, NC=NC, R=R, F=F, H=H, C=C, HC=HC, CH=CH, NDEV=NDEV, FR=FR, CR=CR, RPP=RPP,
        PPC=HC // RPP, PH=HC // RPP // 2, HV=HV, HT=CR // 8 * HV,
    )
    dma = pltpu.SemaphoreType.DMA
    L = LAYERS
    inputs = {
        "feat": feat, "adj": adj, "nm": nm, "lb": lb, "lm": lm, "w0": w0, "wr": wr, "npar": npar,
        "whd": whd, "bias": bias,
    }
    small = [name for name in inputs if name not in ("adj", "wr")]
    d.small = small
    scratch = {
        "xown": pltpu.VMEM((FR, R), F32),
        "xg": pltpu.VMEM((CH, FR, R), F32),
        "ag": pltpu.VMEM((L - 1, CH, R, H), F32),
        "acts": pltpu.VMEM((L, R, H), F32),
        "gp": pltpu.VMEM((L, R, H), F32),
        "adjb": pltpu.VMEM((2, CH, R, R), jnp.int32),
        "abf": pltpu.VMEM((CH, 2 * R, R), BF16),
        "at": pltpu.VMEM((2, CH, R, R), BF16),
        "wt0": pltpu.VMEM((H, 2 * FR), F32),
        "wtr": pltpu.VMEM((L - 1, H, 2 * H), F32),
        "w0h": pltpu.VMEM((H, 2 * FR), BF16),
        "w0l": pltpu.VMEM((H, 2 * FR), BF16),
        "wh": pltpu.VMEM((L - 1, H, 2 * H), BF16),
        "wl": pltpu.VMEM((L - 1, H, 2 * H), BF16),
        "whp": pltpu.VMEM((LANES, H), F32),
        "biasp": pltpu.VMEM((1, LANES), F32),
        "in0h": pltpu.VMEM((2 * FR, R), BF16),
        "in0l": pltpu.VMEM((2 * FR, R), BF16),
        "inh": pltpu.VMEM((L - 1, R, 2 * H), BF16),
        "inl": pltpu.VMEM((L - 1, R, 2 * H), BF16),
        "aggt": pltpu.VMEM((FR, 2 * R), F32),
        "part0": pltpu.VMEM((FR, R), F32),
        "part0r": pltpu.VMEM((FR, R), F32),
        "agg": pltpu.VMEM((2 * R, H), F32),
        "parts": pltpu.VMEM((L - 1, R, H), F32),
        "partr": pltpu.VMEM((L - 1, R, H), F32),
        "kept": pltpu.VMEM((L - 1, R, H), F32),
        "lin": pltpu.VMEM((R, H), F32),
        "gout": pltpu.VMEM((R, H), F32),
        "glh": pltpu.VMEM((R, H), BF16),
        "gll": pltpu.VMEM((R, H), BF16),
        "spread": pltpu.VMEM((R, H), F32),
        "spreads": pltpu.VMEM((L - 1, R, H), F32),
        "spreadr": pltpu.VMEM((L - 1, R, H), F32),
        "out": pltpu.VMEM((CH, R, H), F32),
        "valid": pltpu.VMEM((R, LANES), F32),
        "counted": pltpu.VMEM((R, LANES), F32),
        "label": pltpu.VMEM((R, LANES), F32),
        "degree": pltpu.VMEM((R, LANES), F32),
        "invdeg": pltpu.VMEM((R, LANES), F32),
        "linked": pltpu.VMEM((R, LANES), F32),
        "count": pltpu.VMEM((2, LANES), F32),
        "vecs": pltpu.VMEM((L, 8, H), F32),
        "sq": pltpu.VMEM((8, LANES), F32),
        "arb": pltpu.VMEM((9, NDEV, 4, LANES), F32),
        "dwb": pltpu.VMEM((L - 1, 2, NC, HC // 2, 2 * H), F32),
        "dwr": pltpu.VMEM((L - 1, NC, HC // 2, 2 * H), F32),
        "zrecv": pltpu.VMEM((L - 1, NC, HC // 2, 2 * H), F32),
        "zs": pltpu.VMEM((L - 1, HC // 2, 2 * H), F32),
        "nrecv": pltpu.VMEM((L - 1, CH, RPP, 2 * H), F32),
        "fin": pltpu.VMEM((L - 1, HC, 2 * H), F32),
        "d0": pltpu.VMEM((NC, HC, 2 * FR), F32),
        "recv0": pltpu.VMEM((NDEV, RPP, 2 * FR), F32),
        "fin0": pltpu.VMEM((HC, 2 * FR), F32),
        "hg": pltpu.VMEM((d.HT, 8, LANES), F32),
        "hrecv": pltpu.VMEM((NDEV, 8, LANES), F32),
        "hfin": pltpu.VMEM((d.HT, 8, LANES), F32),
        "ld": dma((L - 1 + len(small) + CH,)),
        "s_adj": dma((CH,)),
        "r_adj": dma((CH,)),
        "s_ag": dma((L, max(CH, 6))),
        "r_ag": dma((L, max(CH, 6))),
        "s_sib": dma((2 * L - 1, 2)),
        "r_sib": dma((2 * L - 1, 2)),
        "s_w": dma((L, NC)),
        "r_w": dma((L, NC)),
        "s_wp": dma((L, NC)),
        "r_wp": dma((L, NC)),
        "s_d": dma((L - 1,)),
        "r_d": dma((L - 1,)),
        "s_ar": dma((9,)),
        "r_ar": dma((9,)),
        "s_rs": dma((L - 1, max(CH, 6))),
        "r_rs": dma((L - 1, max(CH, 6))),
        "s_z": dma((L - 1,)),
        "r_z": dma((L - 1,)),
        "s_n": dma((L - 1,)),
        "r_n": dma((L - 1,)),
        "s_f": dma((L,)),
        "r_f": dma((L,)),
        "s_0": dma((1,)),
        "r_0": dma((1,)),
        "s_h": dma((2,)),
        "r_h": dma((2,)),
        "gn_o": pltpu.VMEM(npar.shape, F32),
        "misc_o": pltpu.VMEM((8, LANES), F32),
        "s_out": dma((L + 4,)),
    }
    for name in small:
        shape = (F, R) if name == "feat" else inputs[name].shape
        scratch[name + "_in"] = pltpu.VMEM(shape, inputs[name].dtype)
    ins = list(inputs)
    outs = ["g0", "gr", "gn", "gh", "misc"]
    d.names = ins + outs + list(scratch)
    return pl.pallas_call(
        functools.partial(step_kernel, d),
        out_shape=[
            jax.ShapeDtypeStruct((HC, 2 * FR), F32),
            jax.ShapeDtypeStruct(wr.shape, F32),
            jax.ShapeDtypeStruct(npar.shape, F32),
            jax.ShapeDtypeStruct((d.HT, 8, LANES), F32),
            jax.ShapeDtypeStruct((8, LANES), F32),
        ],
        in_specs=[pl.BlockSpec(memory_space=pl.ANY)] * len(ins),
        out_specs=[pl.BlockSpec(memory_space=pl.ANY)] * len(outs),
        scratch_shapes=list(scratch.values()),
        compiler_params=pltpu.CompilerParams(
            collective_id=0, has_side_effects=True, vmem_limit_bytes=60 * 2**20
        ),
    )(*inputs.values())


def adamw(weight, first, second, average, grad, rate):
    first = BETA_ONE * first + (1.0 - BETA_ONE) * grad
    second = BETA_TWO * second + (1.0 - BETA_TWO) * grad * grad
    fix_one = 1.0 - BETA_ONE**ADAM_STEP
    fix_two = 1.0 - BETA_TWO**ADAM_STEP
    update = first / fix_one / (jnp.sqrt(second / fix_two) + ADAM_EPS)
    weight = weight - rate * (update + DECAY * weight)
    average = AVERAGE * average + (1.0 - AVERAGE) * weight
    return (first, second, weight, average)


def update_kernel(*refs):
    grads, state, scalars, results = refs[:5], refs[5:25], refs[25:28], refs[28:]
    misc = grads[4]
    scale = misc[4:5, 0:1]
    for i in range(3):
        scalars[i][...] = misc[i : i + 1, 0:1]
    for group in range(5):
        weight, first, second, average = (state[group + 5 * j] for j in range(4))
        rate = RATE_SMALL if group in (2, 4) else RATE_MATRIX
        shape = weight.shape
        if group == 4:
            grad = misc[3:4, : shape[1]]
        elif group == 3:
            wide = shape[1] // LANES
            grad = cat(
                [
                    cat([grads[3][wide * i + j] for j in range(wide)], 1)
                    for i in range(grads[3].shape[0] // wide)
                ],
                0,
            )[: shape[0]]
        elif group == 0:
            half = shape[1] // 2
            at = grads[0].shape[1] // 2
            grad = cat([grads[0][:, :half], grads[0][:, at : at + half]], 1)
        else:
            grad = grads[group][...]
        done = adamw(weight[...], first[...], second[...], average[...], grad * scale, rate)
        for ref, value in zip(results[4 * group : 4 * group + 4], done, strict=True):
            ref[...] = value


def local(
    nodes, cols, features, adjacency, node_mask, labels, label_mask, *state
):
    turn = (
        lambda a: a.T,
        lambda a: a.transpose(0, 2, 1),
        lambda a: a.transpose(1, 0, 2),
        lambda a: a.T,
        lambda a: a.reshape(1, -1),
    )
    back = turn[:4] + (lambda a: a.reshape(-1),)
    state = [turn[i % 5](a) for i, a in enumerate(state)]
    grads = gradients(
        nodes, cols, features.transpose(2, 0, 1), adjacency[0], node_mask, labels, label_mask, *state[:5]
    )
    outs = [jax.ShapeDtypeStruct((1, 1), F32)] * 3
    outs += [jax.ShapeDtypeStruct(a.shape, F32) for a in state[:5] for _ in range(4)]
    done = pl.pallas_call(update_kernel, out_shape=outs)(*grads, *state)
    return (
        *(a.reshape(()) for a in done[:3]),
        *(back[i // 4](a) for i, a in enumerate(done[3:])),
    )


def solution(mesh):
    rows, first, rest, all_of = P("cols", "nodes", None), P(None, "cols"), P(None, None, "cols"), P()
    state = [first, rest, all_of, all_of, all_of]
    return jax.shard_map(
        functools.partial(local, mesh.shape["nodes"], mesh.shape["cols"]),
        mesh=mesh,
        in_specs=(rows, rows) + (P("cols", "nodes"),) * 3 + tuple(state * 4),
        out_specs=(all_of,) * 3 + tuple(spec for spec in state for _ in range(4)),
        check_vma=False,
    )
```

```python
import functools
import types

import jax
import jax.numpy as jnp
from jax import lax
from jax.experimental import pallas as pl
from jax.experimental.pallas import tpu as pltpu
from jax.sharding import PartitionSpec as P

LAYERS = 3
ADAM_STEP = 10
CLIP = 0.02
RATE_MATRIX = 0.03
RATE_SMALL = 0.3
BETA_ONE = 0.9
BETA_TWO = 0.999
ADAM_EPS = 1e-08
DECAY = 0.01
AVERAGE = 0.9
NORM_EPS = 1e-05

MESH = pl.DeviceIdType.MESH
F32 = jnp.float32
BF16 = jnp.bfloat16
LANES = 128
GELU_OUT = 0.7978845608028654
GELU_CUBE = 0.044715


def cat(values, axis):
    return values[0] if len(values) == 1 else jnp.concatenate(values, axis=axis)


def split(value):
    high = value.astype(BF16)
    return high, (value - high.astype(F32)).astype(BF16)


def dot(left, right):
    return lax.dot_general(left, right, (((1,), (0,)), ((), ())), preferred_element_type=F32)


def dot_t(left, right):
    return lax.dot_general(left, right, (((1,), (1,)), ((), ())), preferred_element_type=F32)


def dot3(left, right):
    (lh, ll), (rh, rl) = left, right
    return dot(cat([lh, lh, ll], 1), cat([rh, rl, rh], 0))


def dot3_t(left, right):
    (lh, ll), (rh, rl) = left, right
    return dot_t(cat([lh, lh, ll], 1), cat([rh, rl, rh], 1))


def remote(src, dst, send, recv, device):
    return pltpu.make_async_remote_copy(
        src_ref=src, dst_ref=dst, send_sem=send, recv_sem=recv, device_id=device, device_id_type=MESH
    )


def wait_bytes(ref, sem):
    pltpu.make_async_copy(ref, ref, sem).wait()


def flip(index, distance):
    bit = 1
    while bit <= distance:
        if distance & bit:
            index = index + (1 - 2 * lax.rem(lax.div(index, bit), 2)) * bit
        bit *= 2
    return index


def step_kernel(d, *refs):
    v = types.SimpleNamespace(**dict(zip(d.names, refs, strict=True)))
    NN, NC, R, H, HC, CH, L = d.NN, d.NC, d.R, d.H, d.HC, d.CH, LAYERS
    NDEV, RPP, PPC, PH, HV, F, FR, CR = d.NDEV, d.RPP, d.PPC, d.PH, d.HV, d.F, d.FR, d.CR
    n, c = lax.axis_index("nodes"), lax.axis_index("cols")
    me = n * NC + c
    ch, k = lax.div(n, 2), lax.rem(n, 2)
    sib = (ch * 2 + 1 - k, c)
    drains = []

    def device(index):
        return lax.div(index, NC), lax.rem(index, NC)

    def peer(dd):
        return flip(ch, dd) * 2 + k, c

    def rows(i, size):
        return pl.ds(pl.multiple_of(i * size, size), size)

    def send(src, dst, ssem, rsem, dev):
        remote(src, dst, ssem, rsem, dev).start()
        drains.append(lambda: wait_bytes(src, ssem))

    def either(always, condition, fn, other=None):
        if always:
            fn()
            return

        @pl.when(condition)
        def _():
            fn()

        if other is not None:

            @pl.when(jnp.logical_not(condition))
            def _():
                other()

    barrier = pltpu.get_barrier_semaphore()

    def adj_cols(j, core):
        return v.adj.at[:, rows(j * 2 + core, R)]

    own_rows = rows(c, HC)
    w_loads = [
        pltpu.make_async_copy(v.wr.at[i], v.wtr.at[i, own_rows, :], v.ld.at[i]) for i in range(L - 1)
    ]
    small_loads = [
        pltpu.make_async_copy(
            v.feat.at[:, 0, :] if name == "feat" else getattr(v, name),
            getattr(v, name + "_in"),
            v.ld.at[L - 1 + i],
        )
        for i, name in enumerate(d.small)
    ]
    for copy in small_loads + w_loads:
        copy.start()
    base = L - 1 + len(d.small)
    for j in range(CH):
        pltpu.make_async_copy(adj_cols(j, k), v.adjb.at[0, j], v.ld.at[base + j]).start()
    def greet(i, carry):
        pl.semaphore_signal(
            barrier, inc=1, device_id=device(lax.rem(me + i, NDEV)), device_id_type=MESH
        )
        return carry

    lax.fori_loop(1, NDEV, greet, 0)

    small_loads[0].wait()
    v.xown[:F, :] = v.feat_in[...]
    v.xown[F:, :] = jnp.ones((FR - F, R), F32)
    pl.semaphore_wait(barrier, NDEV - 1)

    def halves(ref):
        size = ref.shape[0]
        first = -(-size // 16) * 8
        return ref.at[:first], ref.at[first:]

    def ag_send(g, src, buf, part):
        s, r = v.s_ag.at[g], v.r_ag.at[g]
        mine = halves(src)
        slot = halves(buf.at[ch])
        if CH == 4:
            send(mine[part], slot[part], s.at[part], r.at[part], peer(1))
            if part == 1:
                send(mine[1], slot[1], s.at[3], r.at[3], peer(2))
                send(mine[0], slot[0], s.at[2], r.at[2], peer(2))
        elif part == 1:
            for dd in reversed(range(1, CH)):
                send(src, buf.at[ch], s.at[dd], r.at[dd], peer(dd))

    def ag_forward(g, buf):
        s, r = v.s_ag.at[g], v.r_ag.at[g]
        if CH == 4:
            x, y = (halves(buf.at[flip(ch, dd)]) for dd in (1, 2))
            wait_bytes(x[0], r.at[0])
            send(x[0], x[0], s.at[4], r.at[4], peer(2))
            wait_bytes(y[1], r.at[3])
            send(y[1], y[1], s.at[5], r.at[5], peer(1))

    def ag_blocks(g, buf, add):
        r = v.r_ag.at[g]
        if CH == 4:
            x, y, z = (halves(buf.at[flip(ch, dd)]) for dd in (1, 2, 3))
            add(flip(ch, 1), 0, x[0])
            add(flip(ch, 2), 1, y[1])
            wait_bytes(x[1], r.at[1])
            add(flip(ch, 1), 1, x[1])
            wait_bytes(y[0], r.at[2])
            add(flip(ch, 2), 0, y[0])
            wait_bytes(z[0], r.at[4])
            add(flip(ch, 3), 0, z[0])
            wait_bytes(z[1], r.at[5])
            add(flip(ch, 3), 1, z[1], True)
        else:
            for dd in range(1, CH):
                wait_bytes(buf.at[flip(ch, dd)], r.at[dd])
                for part in range(2):
                    add(flip(ch, dd), part, halves(buf.at[flip(ch, dd)])[part], dd == CH - 1 and part == 1)

    def to_others(start, at_once=False):
        if at_once and NDEV <= 32:
            for dc in [*reversed(range(1, NC)), 0]:
                for dn in reversed(range(NN)):
                    if dn or dc:
                        tn, tc = lax.rem(n + dn, NN) if dn else n, lax.rem(c + dc, NC) if dc else c
                        start((tn, tc), tn * NC + tc)
            return

        def one(i, carry):
            t = lax.rem(me + i, NDEV)
            start(device(t), t)
            return carry

        lax.fori_loop(1, NDEV, one, 0)

    def ar_send(a, at_once=False):
        to_others(
            lambda dev, t: remote(
                v.arb.at[a, me], v.arb.at[a, me], v.s_ar.at[a], v.r_ar.at[a], dev
            ).start(),
            at_once,
        )
        drains.append(lambda: wait_bytes(v.arb.at[a, pl.ds(0, NDEV - 1)], v.s_ar.at[a]))

    def ar_put(a, vectors):
        at = 0
        for vec in vectors:
            for i in range(vec.shape[1] // LANES):
                v.arb[a, me, at : at + 1, :] = vec[:, i * LANES : (i + 1) * LANES]
                at += 1
        if at < 4:
            v.arb[a, me, at:, :] = jnp.zeros((4 - at, LANES), F32)

    def ar_wait(a):
        wait_bytes(v.arb.at[a, pl.ds(0, NDEV - 1)], v.r_ar.at[a])
        return jnp.sum(v.arb[a], axis=0)

    def vec(total, i):
        return cat([total[i * HV + j : i * HV + j + 1] for j in range(HV)], 1)

    for part in range(2):
        ag_send(0, v.xown, v.xg, part)

    def w_ref(l):
        return v.wt0 if l == 0 else v.wtr.at[l - 1]

    def w_half(l, dd, core):
        at = lax.rem(c + dd, NC) * HC + core * (HC // 2)
        return w_ref(l).at[pl.ds(pl.multiple_of(at, HC // 2), HC // 2), :]

    def w_send(l):
        block = w_half(l, 0, k)
        for dd in range(1, NC):
            send(block, block, v.s_w.at[l, dd], v.r_w.at[l, dd], (n, lax.rem(c + dd, NC)))

    def w_pass(l):
        for dd in range(1, NC):
            block = w_half(l, NC - dd, k)
            wait_bytes(block, v.r_w.at[l, dd])
            send(block, block, v.s_wp.at[l, dd], v.r_wp.at[l, dd], sib)

    def w_wait(l):
        for dd in range(1, NC):
            wait_bytes(w_half(l, NC - dd, 1 - k), v.r_wp.at[l, dd])

    for copy in small_loads[1:]:
        copy.wait()
    v.wt0[own_rows, :] = jnp.zeros((HC, 2 * FR), F32)
    v.wt0[own_rows, :F] = v.w0_in[:, :F]
    v.wt0[own_rows, FR : FR + F] = v.w0_in[:, F:]
    w_send(0)
    for j in range(CH):
        send(adj_cols(j, 1 - k), v.adjb.at[1, j], v.s_adj.at[j], v.r_adj.at[j], sib)
    w_loads[0].wait()
    w_send(1)
    for copy in w_loads[1:]:
        copy.wait()

    def column(row):
        return jnp.broadcast_to(row.astype(F32), (LANES, R)).T

    v.valid[...] = column(v.nm_in[...])
    v.counted[...] = column(v.lm_in[...] * v.nm_in[...])
    v.label[...] = column(v.lb_in[...])
    v.whp[...] = jnp.zeros(v.whp.shape, F32)
    v.whp[: d.C, :] = v.whd_in[...]
    v.biasp[...] = jnp.zeros(v.biasp.shape, F32)
    v.biasp[:, : d.C] = v.bias_in[...]
    ar_put(
        8,
        [
            jnp.sum(v.valid[...], axis=0, keepdims=True),
            jnp.sum(v.counted[...], axis=0, keepdims=True),
        ],
    )
    ar_send(8)

    def adj_own(j, carry):
        pltpu.make_async_copy(adj_cols(j, k), v.adjb.at[0, j], v.ld.at[base + j]).wait()
        v.abf[j, :R, :] = v.adjb[0, j].astype(F32).astype(BF16)
        return carry

    def adj_sib(j, carry):
        wait_bytes(v.adjb.at[1, j], v.r_adj.at[j])
        v.abf[j, R:, :] = v.adjb[1, j].astype(F32).astype(BF16)
        return carry

    def adj_turn(j, carry):
        for side in range(2):
            v.at[side, j] = v.adjb[side, j].astype(F32).T.astype(BF16)
        return carry

    lax.fori_loop(0, CH, adj_own, 0)
    first_rows = len(drains)
    ag_forward(0, v.xg)
    lax.fori_loop(0, CH, adj_sib, 0)

    def wide(value):
        return cat([value] * HV, 1)

    RC = min(R // 2, 64)
    HALF = R // 2

    def activate(l, part):
        def chunk(i, carry):
            r = rows(i, RC)
            x = v.lin[r, :]
            square = x * x
            t = jnp.tanh(GELU_OUT * x * (1.0 + GELU_CUBE * square))
            half = 0.5 * (1.0 + t)
            act = x * half
            v.acts[l, r, :] = act
            v.gp[l, r, :] = half + (0.5 * GELU_OUT) * x * (1.0 - t * t) * (
                1.0 + (3.0 * GELU_CUBE) * square
            )
            masked = wide(v.valid[r, :]) * act
            return (
                carry[0] + jnp.sum(masked.reshape(RC // 8, 8, H), axis=0),
                carry[1] + jnp.sum((masked * act).reshape(RC // 8, 8, H), axis=0),
            )

        zero = jnp.zeros((8, H), F32)
        per = HALF // RC
        return lax.fori_loop(part * per, (part + 1) * per, chunk, (zero, zero))

    def over_rows(value):
        return jnp.sum(value, axis=0, keepdims=True)

    def keep_stats(l, total):
        count = jnp.max(v.count[0:1, :], axis=1, keepdims=True)
        mean = vec(total, 0) / count
        var = vec(total, 1) / count - mean * mean
        inverse = lax.rsqrt(var + NORM_EPS)
        gain, shift = v.npar_in[l, 0:1, :], v.npar_in[l, 1:2, :]
        v.vecs[l, 0:1, :] = mean
        v.vecs[l, 1:2, :] = inverse
        v.vecs[l, 2:3, :] = gain * inverse
        v.vecs[l, 3:4, :] = shift - mean * (gain * inverse)

    def finish(l, part_lin):
        sums = []
        for part in range(2):
            part_lin(part)
            sums.append(activate(l, part))
            if l < L - 1:
                ag_send(l + 1, v.acts.at[l], v.ag.at[l], part)
        ar_put(l, [over_rows(sums[0][i] + sums[1][i]) for i in range(2)])
        ar_send(l, l == L - 1)

    def add_first(chip, part, ref, last=False):
        high, low = split(ref[...])
        a = v.abf[chip]
        got = dot_t(cat([high, low], 1), cat([a, a], 1))
        first = -(-FR // 16) * 8
        r = slice(0, first) if part == 0 else slice(first, FR)
        seen = v.aggt[r, :]
        v.aggt[r, :] = seen + got

    v.aggt[...] = jnp.zeros((FR, 2 * R), F32)
    for part in range(2):
        add_first(ch, part, halves(v.xown)[part])
    w_pass(0)
    ag_blocks(0, v.xg, add_first)
    v.part0[...] = v.aggt[:, R:]
    send(v.part0, v.part0r, v.s_sib.at[0, 0], v.r_sib.at[0, 0], sib)
    w_wait(0)
    v.w0h[...], v.w0l[...] = split(v.wt0[...])
    feature = lax.broadcasted_iota(jnp.int32, (FR, R), 0) < F
    v.in0h[:FR, :], v.in0l[:FR, :] = split(jnp.where(feature, v.xown[...], 0.0))
    wait_bytes(v.part0r, v.r_sib.at[0, 0])
    total = v.aggt[:, :R] + v.part0r[...]
    degree = total[F : F + 1, :]
    v.in0h[FR:, :], v.in0l[FR:, :] = split(
        jnp.where(feature, total * (1.0 / jnp.maximum(degree, 1.0)), 0.0)
    )
    v.lin[...] = dot3((v.w0h[...], v.w0l[...]), (v.in0h[...], v.in0l[...])).T
    finish(0, lambda part: None)
    degree = column(degree)
    v.degree[...] = degree
    v.linked[...] = jnp.minimum(degree, 1.0)
    v.invdeg[...] = 1.0 / jnp.maximum(degree, 1.0)
    v.count[...] = ar_wait(8)[0:2]

    for l in range(1, L):
        if l == 1:
            lax.fori_loop(0, CH, adj_turn, 0)
        w_pass(l)
        ag_forward(l, v.ag.at[l - 1])
        w_wait(l)
        v.wh[l - 1], v.wl[l - 1] = split(v.wtr[l - 1])
        total = ar_wait(l - 1)
        if l < L - 1:
            w_send(l + 1)
        keep_stats(l - 1, total)
        scale, shift = v.vecs[l - 1, 2:3, :], v.vecs[l - 1, 3:4, :]
        v.inh[l - 1, :, :H], v.inl[l - 1, :, :H] = split(v.acts[l - 1] * scale + shift)
        v.lin[...] = dot3_t(
            (v.inh[l - 1, :, :H], v.inl[l - 1, :, :H]), (v.wh[l - 1, :, :H], v.wl[l - 1, :, :H])
        )

        parts, partr = v.parts.at[l - 1], v.partr.at[l - 1]

        def share(a, both, first=False):
            for at, total in ((R, parts), (0, v.agg)):
                got = dot(cat([a[at : at + R]] * 2, 1), both)
                total[...] = got if first else total[...] + got
                if at and a is v.last_columns:
                    for part in range(2):
                        send(
                            halves(parts)[part], halves(partr)[part], v.s_sib.at[l, part],
                            v.r_sib.at[l, part], sib,
                        )

        def add(chip, part, ref, last=False):
            columns = v.abf[chip, :, part * HALF : (part + 1) * HALF]
            v.last_columns = columns if last else None
            share(columns, cat(list(split(ref[...])), 0))

        v.last_columns = None
        share(v.abf[ch], cat(list(split(v.acts[l - 1])), 0), True)
        ag_blocks(l, v.ag.at[l - 1], add)

        def part_lin(part):
            r = slice(part * HALF, (part + 1) * HALF)
            wait_bytes(halves(partr)[part], v.r_sib.at[l, part])
            agg = v.agg[r, :] + partr[r, :]
            v.kept[l - 1, r, :] = agg
            v.inh[l - 1, r, H:], v.inl[l - 1, r, H:] = split(
                agg * wide(v.invdeg[r, :]) * scale + wide(v.linked[r, :]) * shift
            )
            v.lin[r, :] += dot3_t(
                (v.inh[l - 1, r, H:], v.inl[l - 1, r, H:]), (v.wh[l - 1, :, H:], v.wl[l - 1, :, H:])
            )

        finish(l, part_lin)

    for drain in drains[first_rows:]:
        drain()
    del drains[first_rows:]

    head = split(v.whp[...])
    lane = lax.broadcasted_iota(jnp.int32, (R, LANES), 1)
    onehot = jnp.where(lane.astype(F32) == v.label[...], 1.0, 0.0)
    real = lane < d.C
    counted = v.counted[...]
    label_count = jnp.max(v.count[1:2, :], axis=1, keepdims=True)
    keep_stats(L - 1, ar_wait(L - 1))
    last = split(v.acts[L - 1] * v.vecs[L - 1, 2:3, :] + v.vecs[L - 1, 3:4, :])
    logits = dot3_t(last, head) + v.biasp[...]
    top = jnp.max(jnp.where(real, logits, -3.0e38), axis=1, keepdims=True)
    moved = logits - top
    power = jnp.where(real, jnp.exp(moved), 0.0)
    power_sum = jnp.sum(power, axis=1, keepdims=True)
    g_logits = counted * (power / power_sum - onehot) / label_count
    gl_split = split(g_logits)
    v.gout[...] = dot3(gl_split, head)

    def last_sums():
        mean, inverse = v.vecs[L - 1, 0:1, :], v.vecs[L - 1, 1:2, :]

        def chunk(i, carry):
            r = rows(i, RC)
            g = v.gout[r, :]
            normed = (v.acts[L - 1, r, :] - mean) * inverse
            return (
                carry[0] + jnp.sum((g * normed).reshape(RC // 8, 8, H), axis=0),
                carry[1] + jnp.sum(g.reshape(RC // 8, 8, H), axis=0),
            )

        zero = jnp.zeros((8, H), F32)
        return [over_rows(s) for s in lax.fori_loop(0, R // RC, chunk, (zero, zero))]

    ar_put(3, last_sums())
    ar_send(3, True)
    logp = moved - jnp.log(power_sum)
    rows_loss = jnp.sum(jnp.where(real, onehot * logp, 0.0), axis=1, keepdims=True) * counted
    ar_put(6, [-over_rows(rows_loss), over_rows(g_logits)])
    ar_send(6)
    head_grad = dot3(split(g_logits.T[:CR, :]), last)
    HT = d.HT
    for t in range(HT):
        i, j = t // HV, t % HV
        v.hg[t] = head_grad[8 * i : 8 * i + 8, j * LANES : (j + 1) * LANES]

    def others(index, size, ref_of, init):
        return lax.fori_loop(1, size, lambda i, s: s + ref_of(lax.rem(index + i, size)), init)

    def head_scatter(i, carry):
        t = lax.rem(me + i, NDEV)

        def go():
            remote(v.hg.at[t], v.hrecv.at[me], v.s_h.at[0], v.r_h.at[0], device(t)).start()

        either(HT == NDEV, t < HT, go)
        return carry

    lax.fori_loop(1, NDEV, head_scatter, 0)
    drains.append(
        lambda: either(
            HT == NDEV,
            me < HT,
            lambda: wait_bytes(v.hrecv.at[pl.ds(0, HT - 1)], v.s_h.at[0]),
            lambda: wait_bytes(v.hrecv.at[pl.ds(0, HT)], v.s_h.at[0]),
        )
    )

    def head_gather():
        def go():
            wait_bytes(v.hrecv.at[pl.ds(0, NDEV - 1)], v.r_h.at[0])
            v.hfin[me] = others(me, NDEV, lambda s: v.hrecv[s], v.hg[me])

            def one(i, carry):
                remote(
                    v.hfin.at[me], v.hfin.at[me], v.s_h.at[1], v.r_h.at[1],
                    device(lax.rem(me + i, NDEV)),
                ).start()
                return carry

            lax.fori_loop(1, NDEV, one, 0)

        either(HT == NDEV, me < HT, go)
        drains.append(
            lambda: either(
                HT == NDEV,
                me < HT,
                lambda: wait_bytes(v.hrecv.at[pl.ds(0, NDEV - 1)], v.s_h.at[1]),
            )
        )

    def sibling_send(i):
        send(v.dwb.at[i, 1 - k], v.dwr.at[i], v.s_d.at[i], v.r_d.at[i], sib)

    def cols_send(i):
        wait_bytes(v.dwr.at[i], v.r_d.at[i])
        v.dwb[i, k] += v.dwr[i]
        for dd in range(1, NC):
            t = lax.rem(c + dd, NC)
            remote(v.dwb.at[i, k, t], v.zrecv.at[i, c], v.s_z.at[i], v.r_z.at[i], (n, t)).start()
        drains.append(lambda: wait_bytes(v.zrecv.at[i, pl.ds(0, NC - 1)], v.s_z.at[i]))

    def nodes_send(i):
        wait_bytes(v.zrecv.at[i, pl.ds(0, NC - 1)], v.r_z.at[i])
        v.zs[i] = others(c, NC, lambda s: v.zrecv[i, s], v.dwb[i, k, c])

        def one(j, carry):
            t = lax.rem(ch + j, CH)
            either(
                PH == CH,
                t < PH,
                lambda: remote(
                    v.zs.at[i, rows(t, RPP), :], v.nrecv.at[i, ch], v.s_n.at[i], v.r_n.at[i],
                    (t * 2 + k, c),
                ).start(),
            )
            return carry

        lax.fori_loop(1, CH, one, 0)
        drains.append(
            lambda: either(
                PH == CH,
                ch < PH,
                lambda: wait_bytes(v.zs.at[i, pl.ds(0, (PH - 1) * RPP), :], v.s_n.at[i]),
                lambda: wait_bytes(v.zs.at[i, pl.ds(0, PH * RPP), :], v.s_n.at[i]),
            )
        )

    def pieces_out(i, fin, at, piece):
        mine = pl.ds(pl.multiple_of(at, RPP), RPP)
        fin[mine, :] = piece
        square = jnp.sum((piece * piece).reshape(RPP // 8, 8, piece.shape[1]), axis=0)
        v.sq[...] += jnp.sum(square, axis=1, keepdims=True)

        def one(j, carry):
            block = fin.at[mine, :]
            remote(block, block, v.s_f.at[i], v.r_f.at[i], (lax.rem(n + j, NN), c)).start()
            return carry

        lax.fori_loop(1, NN, one, 0)

    def pieces_drain(i, fin):
        drains.append(
            lambda: either(
                PPC == NN,
                n < PPC if i == L - 1 else ch < PH,
                lambda: lax.fori_loop(
                    1, NN, lambda j, carry: (wait_bytes(fin.at[pl.ds(0, RPP), :], v.s_f.at[i]), carry)[1], 0
                ),
            )
        )

    def nodes_gather(i):
        def go():
            wait_bytes(v.nrecv.at[i, pl.ds(0, CH - 1)], v.r_n.at[i])
            piece = others(ch, CH, lambda s: v.nrecv[i, s], v.zs[i, rows(ch, RPP), :])
            pieces_out(i, v.fin.at[i], k * (HC // 2) + ch * RPP, piece)

        either(PH == CH, ch < PH, go)
        pieces_drain(i, v.fin.at[i])

    v.sq[...] = jnp.zeros((8, LANES), F32)

    def fin_wait(i, fin):
        either(
            PPC == NN,
            n < PPC if i == L - 1 else ch < PH,
            lambda: wait_bytes(fin.at[pl.ds(0, (PPC - 1) * RPP), :], v.r_f.at[i]),
            lambda: wait_bytes(fin.at[pl.ds(0, PPC * RPP), :], v.r_f.at[i]),
        )

    def give(i, src, dst):
        copy = pltpu.make_async_copy(src, dst, v.s_out.at[i])
        copy.start()
        drains.append(copy.wait)

    def linear_grad(l, a):
        total = ar_wait(a)
        g_gain, g_shift = vec(total, 0), vec(total, 1)
        v.gn_o[l, 0:1, :] = g_gain
        v.gn_o[l, 1:2, :] = g_shift
        mean, inverse, scale = v.vecs[l, 0:1, :], v.vecs[l, 1:2, :], v.vecs[l, 2:3, :]
        count = jnp.max(v.count[0:1, :], axis=1, keepdims=True)
        by_one = scale * g_shift / count
        by_normed = scale * g_gain / count

        def chunk(i, carry):
            r = rows(i, RC)
            normed = (v.acts[l, r, :] - mean) * inverse
            g_active = scale * v.gout[r, :] - wide(v.valid[r, :]) * (by_one + normed * by_normed)
            g_linear = v.gp[l, r, :] * g_active
            v.lin[r, :] = g_linear
            v.glh[r, :], v.gll[r, :] = split(g_linear)
            return carry

        lax.fori_loop(0, R // RC, chunk, 0)

    for l in (2, 1):
        g = l - 1
        linear_grad(l, 5 - l)
        gl = (v.glh[...], v.gll[...])
        back = v.ag.at[2 - l]
        for part in range(2):
            r = slice(part * HALF, (part + 1) * HALF)
            spread = dot3((v.glh[r, :], v.gll[r, :]), (v.wh[g, :, H:], v.wl[g, :, H:]))
            v.spreads[g, r, :] = spread * wide(v.invdeg[r, :])
            send(
                halves(v.spreads.at[g])[part], halves(v.spreadr.at[g])[part],
                v.s_sib.at[L + g, part], v.r_sib.at[L + g, part], sib,
            )
        if g == 0:
            for drain in scatter_drains:
                drain()
        own = cat(list(split(v.spreads[g])), 0)
        for dd in reversed(range(CH)):
            t = v.at[0, flip(ch, dd)]
            v.out[dd] = dot(cat([t, t], 1), own)
        for part in range(2):
            wait_bytes(halves(v.spreadr.at[g])[part], v.r_sib.at[L + g, part])
        other = cat(list(split(v.spreadr[g])), 0)

        def complete(dd):
            t = v.at[1, flip(ch, dd)]
            v.out[dd] += dot(cat([t, t], 1), other)

        s, r = v.s_rs.at[g], v.r_rs.at[g]
        kept_drains, drains = drains, []
        if CH == 4:
            x, y, z = (halves(v.out.at[dd]) for dd in (1, 2, 3))
            from_x, from_y, via = (halves(back.at[i]) for i in range(3))
            complete(3)
            send(z[0], via[0], s.at[0], r.at[0], peer(1))
            send(z[1], via[1], s.at[1], r.at[1], peer(2))
            complete(1)
            send(x[0], from_x[0], s.at[2], r.at[2], peer(1))
            complete(2)
            send(y[1], from_y[1], s.at[3], r.at[3], peer(2))
            complete(0)
        else:
            for dd in reversed(range(1, CH)):
                complete(dd)
                send(v.out.at[dd], back.at[dd], s.at[dd], r.at[dd], peer(dd))
            complete(0)
        v.gout[...] = dot3(gl, (v.wh[g, :, :H], v.wl[g, :, :H]))
        mean, inverse = v.vecs[g, 0:1, :], v.vecs[g, 1:2, :]

        def chunk(i, carry):
            r = rows(i, RC)
            self, spread, degree = v.gout[r, :], v.spreads[g, r, :], wide(v.degree[r, :])
            normed = (v.acts[g, r, :] - mean) * inverse
            reached = (v.kept[g, r, :] - degree * mean) * inverse
            v.gout[r, :] = self + v.out[0, r, :]
            return (
                carry[0] + jnp.sum((self * normed + spread * reached).reshape(RC // 8, 8, H), axis=0),
                carry[1] + jnp.sum((self + spread * degree).reshape(RC // 8, 8, H), axis=0),
            )

        zero = jnp.zeros((8, H), F32)
        ar_put(6 - l, [over_rows(t) for t in lax.fori_loop(0, R // RC, chunk, (zero, zero))])
        ar_send(6 - l, True)
        if CH == 4:
            wait_bytes(via[0], r.at[0])
            y[0][...] += via[0][...]
            send(y[0], from_y[0], s.at[5], r.at[5], peer(2))
            wait_bytes(via[1], r.at[1])
            x[1][...] += via[1][...]
            send(x[1], from_x[1], s.at[4], r.at[4], peer(1))
        scatter_drains, drains = drains, kept_drains
        grad = dot3(split(v.lin[...].T), (v.inh[g], v.inl[g]))
        for t in range(NC):
            for half in range(2):
                at = t * HC + half * (HC // 2)
                v.dwb[g, half, t] = grad[at : at + HC // 2, :]
        sibling_send(g)
        if l == 2:
            head_gather()
        else:
            nodes_send(1)
        cols_send(g)
        if l == 1:
            nodes_gather(1)
        if CH == 4:
            for half, i in ((from_x[0], 2), (from_y[1], 3), (from_y[0], 5), (from_x[1], 4)):
                wait_bytes(half, r.at[i])
            v.gout[...] += back[0] + back[1]
        else:
            for dd in range(1, CH):
                wait_bytes(back.at[dd], r.at[dd])
                v.gout[...] += back[dd]
    drains += scatter_drains

    linear_grad(0, 5)
    grad = dot3_t(split(v.lin[...].T), (v.in0h[...], v.in0l[...]))
    for t in range(NC):
        v.d0[t] = grad[t * HC : (t + 1) * HC, :]

    def first_scatter(dev, t):
        tn, tc = dev
        either(
            PPC == NN,
            tn < PPC,
            lambda: remote(
                v.d0.at[tc, rows(tn, RPP), :], v.recv0.at[me], v.s_0.at[0], v.r_0.at[0], dev
            ).start(),
        )

    to_others(first_scatter, True)
    drains.append(
        lambda: either(
            PPC == NN,
            n < PPC,
            lambda: wait_bytes(v.recv0.at[pl.ds(0, PPC * NC - 1)], v.s_0.at[0]),
            lambda: wait_bytes(v.recv0.at[pl.ds(0, PPC * NC)], v.s_0.at[0]),
        )
    )
    nodes_send(0)
    nodes_gather(0)

    def first_gather():
        wait_bytes(v.recv0.at[pl.ds(0, NDEV - 1)], v.r_0.at[0])
        piece = others(me, NDEV, lambda s: v.recv0[s], v.d0[c, rows(n, RPP), :])
        pieces_out(L - 1, v.fin0, n * RPP, piece)

    either(PPC == NN, n < PPC, first_gather)
    pieces_drain(L - 1, v.fin0)
    ar_put(7, [over_rows(v.sq[...])])
    ar_send(7, True)

    total = ar_wait(6)
    bias_grad = total[1:2]
    v.misc_o[...] = jnp.zeros((8, LANES), F32)
    v.misc_o[0:1, :] = total[0:1]
    v.misc_o[1:2, :] = v.count[1:2, :]
    v.misc_o[3:4, :] = bias_grad
    either(
        HT == NDEV,
        me < HT,
        lambda: wait_bytes(v.hfin.at[pl.ds(0, HT - 1)], v.r_h.at[1]),
        lambda: wait_bytes(v.hfin.at[pl.ds(0, HT)], v.r_h.at[1]),
    )
    give(2, v.gn_o, v.gn)
    give(3, v.hfin, v.gh)
    square = jnp.zeros((8, LANES), F32)
    for t in range(HT):
        square += v.hfin[t] * v.hfin[t]
    replicated = over_rows(square) + bias_grad * bias_grad
    small = jnp.zeros((1, H), F32)
    for l in range(L):
        small += over_rows(v.gn_o[l] * v.gn_o[l])
    for j in range(HV):
        replicated += small[:, j * LANES : (j + 1) * LANES]
    for i in range(L - 1):
        fin_wait(i, v.fin.at[i])
        give(5 + i, v.fin.at[i], v.gr.at[i])
    total = ar_wait(7)
    squares = total[0:1, 0:1] + jnp.sum(replicated, axis=1, keepdims=True)
    norm = jnp.sqrt(squares)
    v.misc_o[2:3, :] = jnp.broadcast_to(norm, (1, LANES))
    v.misc_o[4:5, :] = jnp.broadcast_to(CLIP / jnp.maximum(norm, CLIP), (1, LANES))
    give(4, v.misc_o, v.misc)
    fin_wait(L - 1, v.fin0)
    give(0, v.fin0, v.g0)

    for drain in drains:
        drain()


def gradients(NN, NC, feat, adj, nm, lb, lm, w0, wr, npar, whd, bias):
    F, _, R = feat.shape
    C, H = whd.shape
    HC = w0.shape[0]
    CH, NDEV = NN // 2, NN * NC
    up = lambda size: -(-size // 8) * 8
    FR, CR = up(F + 1), up(C)
    RPP = max(8, HC // NN)
    HV = H // LANES
    d = types.SimpleNamespace(
        NN=NN, NC=NC, R=R, F=F, H=H, C=C, HC=HC, CH=CH, NDEV=NDEV, FR=FR, CR=CR, RPP=RPP,
        PPC=HC // RPP, PH=HC // RPP // 2, HV=HV, HT=CR // 8 * HV,
    )
    dma = pltpu.SemaphoreType.DMA
    L = LAYERS
    inputs = {
        "feat": feat, "adj": adj, "nm": nm, "lb": lb, "lm": lm, "w0": w0, "wr": wr, "npar": npar,
        "whd": whd, "bias": bias,
    }
    small = [name for name in inputs if name not in ("adj", "wr")]
    d.small = small
    scratch = {
        "xown": pltpu.VMEM((FR, R), F32),
        "xg": pltpu.VMEM((CH, FR, R), F32),
        "ag": pltpu.VMEM((L - 1, CH, R, H), F32),
        "acts": pltpu.VMEM((L, R, H), F32),
        "gp": pltpu.VMEM((L, R, H), F32),
        "adjb": pltpu.VMEM((2, CH, R, R), jnp.int32),
        "abf": pltpu.VMEM((CH, 2 * R, R), BF16),
        "at": pltpu.VMEM((2, CH, R, R), BF16),
        "wt0": pltpu.VMEM((H, 2 * FR), F32),
        "wtr": pltpu.VMEM((L - 1, H, 2 * H), F32),
        "w0h": pltpu.VMEM((H, 2 * FR), BF16),
        "w0l": pltpu.VMEM((H, 2 * FR), BF16),
        "wh": pltpu.VMEM((L - 1, H, 2 * H), BF16),
        "wl": pltpu.VMEM((L - 1, H, 2 * H), BF16),
        "whp": pltpu.VMEM((LANES, H), F32),
        "biasp": pltpu.VMEM((1, LANES), F32),
        "in0h": pltpu.VMEM((2 * FR, R), BF16),
        "in0l": pltpu.VMEM((2 * FR, R), BF16),
        "inh": pltpu.VMEM((L - 1, R, 2 * H), BF16),
        "inl": pltpu.VMEM((L - 1, R, 2 * H), BF16),
        "aggt": pltpu.VMEM((FR, 2 * R), F32),
        "part0": pltpu.VMEM((FR, R), F32),
        "part0r": pltpu.VMEM((FR, R), F32),
        "agg": pltpu.VMEM((R, H), F32),
        "parts": pltpu.VMEM((L - 1, R, H), F32),
        "partr": pltpu.VMEM((L - 1, R, H), F32),
        "kept": pltpu.VMEM((L - 1, R, H), F32),
        "lin": pltpu.VMEM((R, H), F32),
        "gout": pltpu.VMEM((R, H), F32),
        "glh": pltpu.VMEM((R, H), BF16),
        "gll": pltpu.VMEM((R, H), BF16),
        "spreads": pltpu.VMEM((L - 1, R, H), F32),
        "spreadr": pltpu.VMEM((L - 1, R, H), F32),
        "out": pltpu.VMEM((CH, R, H), F32),
        "valid": pltpu.VMEM((R, LANES), F32),
        "counted": pltpu.VMEM((R, LANES), F32),
        "label": pltpu.VMEM((R, LANES), F32),
        "degree": pltpu.VMEM((R, LANES), F32),
        "invdeg": pltpu.VMEM((R, LANES), F32),
        "linked": pltpu.VMEM((R, LANES), F32),
        "count": pltpu.VMEM((2, LANES), F32),
        "vecs": pltpu.VMEM((L, 8, H), F32),
        "sq": pltpu.VMEM((8, LANES), F32),
        "arb": pltpu.VMEM((9, NDEV, 4, LANES), F32),
        "dwb": pltpu.VMEM((L - 1, 2, NC, HC // 2, 2 * H), F32),
        "dwr": pltpu.VMEM((L - 1, NC, HC // 2, 2 * H), F32),
        "zrecv": pltpu.VMEM((L - 1, NC, HC // 2, 2 * H), F32),
        "zs": pltpu.VMEM((L - 1, HC // 2, 2 * H), F32),
        "nrecv": pltpu.VMEM((L - 1, CH, RPP, 2 * H), F32),
        "fin": pltpu.VMEM((L - 1, HC, 2 * H), F32),
        "d0": pltpu.VMEM((NC, HC, 2 * FR), F32),
        "recv0": pltpu.VMEM((NDEV, RPP, 2 * FR), F32),
        "fin0": pltpu.VMEM((HC, 2 * FR), F32),
        "hg": pltpu.VMEM((d.HT, 8, LANES), F32),
        "hrecv": pltpu.VMEM((NDEV, 8, LANES), F32),
        "hfin": pltpu.VMEM((d.HT, 8, LANES), F32),
        "ld": dma((L - 1 + len(small) + CH,)),
        "s_adj": dma((CH,)),
        "r_adj": dma((CH,)),
        "s_ag": dma((L, max(CH, 6))),
        "r_ag": dma((L, max(CH, 6))),
        "s_sib": dma((2 * L - 1, 2)),
        "r_sib": dma((2 * L - 1, 2)),
        "s_w": dma((L, NC)),
        "r_w": dma((L, NC)),
        "s_wp": dma((L, NC)),
        "r_wp": dma((L, NC)),
        "s_d": dma((L - 1,)),
        "r_d": dma((L - 1,)),
        "s_ar": dma((9,)),
        "r_ar": dma((9,)),
        "s_rs": dma((L - 1, max(CH, 6))),
        "r_rs": dma((L - 1, max(CH, 6))),
        "s_z": dma((L - 1,)),
        "r_z": dma((L - 1,)),
        "s_n": dma((L - 1,)),
        "r_n": dma((L - 1,)),
        "s_f": dma((L,)),
        "r_f": dma((L,)),
        "s_0": dma((1,)),
        "r_0": dma((1,)),
        "s_h": dma((2,)),
        "r_h": dma((2,)),
        "gn_o": pltpu.VMEM(npar.shape, F32),
        "misc_o": pltpu.VMEM((8, LANES), F32),
        "s_out": dma((L + 4,)),
    }
    for name in small:
        shape = (F, R) if name == "feat" else inputs[name].shape
        scratch[name + "_in"] = pltpu.VMEM(shape, inputs[name].dtype)
    ins = list(inputs)
    room = 6 * 2**20
    for ref in scratch.values():
        if ref.memory_space == pltpu.VMEM:
            size = jnp.dtype(ref.dtype).itemsize
            for i, length in enumerate(reversed(ref.shape)):
                size *= -(-length // LANES) * LANES if i == 0 else -(-length // 8) * 8 if i == 1 else length
            room += size
    outs = ["g0", "gr", "gn", "gh", "misc"]
    d.names = ins + outs + list(scratch)
    return pl.pallas_call(
        functools.partial(step_kernel, d),
        out_shape=[
            jax.ShapeDtypeStruct((HC, 2 * FR), F32),
            jax.ShapeDtypeStruct(wr.shape, F32),
            jax.ShapeDtypeStruct(npar.shape, F32),
            jax.ShapeDtypeStruct((d.HT, 8, LANES), F32),
            jax.ShapeDtypeStruct((8, LANES), F32),
        ],
        in_specs=[pl.BlockSpec(memory_space=pltpu.HBM)] * len(ins),
        out_specs=[pl.BlockSpec(memory_space=pl.ANY)] * len(outs),
        scratch_shapes=list(scratch.values()),
        compiler_params=pltpu.CompilerParams(
            collective_id=0, has_side_effects=True, vmem_limit_bytes=min(room, 60 * 2**20)
        ),
    )(*(pltpu.with_memory_space_constraint(a, pltpu.HBM) for a in inputs.values()))


def adamw(weight, first, second, average, grad, rate):
    first = BETA_ONE * first + (1.0 - BETA_ONE) * grad
    second = BETA_TWO * second + (1.0 - BETA_TWO) * grad * grad
    fix_one = 1.0 - BETA_ONE**ADAM_STEP
    fix_two = 1.0 - BETA_TWO**ADAM_STEP
    update = first / fix_one / (jnp.sqrt(second / fix_two) + ADAM_EPS)
    weight = weight - rate * (update + DECAY * weight)
    average = AVERAGE * average + (1.0 - AVERAGE) * weight
    return (first, second, weight, average)


def update_kernel(*refs):
    grads, state, scalars, results = refs[:5], refs[5:25], refs[25:28], refs[28:]
    misc = grads[4]
    scale = misc[4:5, 0:1]
    for i in range(3):
        scalars[i][...] = misc[i : i + 1, 0:1]
    for group in range(5):
        weight, first, second, average = (state[group + 5 * j] for j in range(4))
        rate = RATE_SMALL if group in (2, 4) else RATE_MATRIX
        shape = weight.shape
        if group == 4:
            grad = misc[3:4, : shape[1]]
        elif group == 3:
            wide = shape[1] // LANES
            grad = cat(
                [
                    cat([grads[3][wide * i + j] for j in range(wide)], 1)
                    for i in range(grads[3].shape[0] // wide)
                ],
                0,
            )[: shape[0]]
        elif group == 0:
            half = shape[1] // 2
            at = grads[0].shape[1] // 2
            grad = cat([grads[0][:, :half], grads[0][:, at : at + half]], 1)
        else:
            grad = grads[group][...]
        done = adamw(weight[...], first[...], second[...], average[...], grad * scale, rate)
        for ref, value in zip(results[4 * group : 4 * group + 4], done, strict=True):
            ref[...] = value


def local(
    nodes, cols, features, adjacency, node_mask, labels, label_mask, *state
):
    turn = (
        lambda a: a.T,
        lambda a: a.transpose(0, 2, 1),
        lambda a: a.transpose(1, 0, 2),
        lambda a: a.T,
        lambda a: a.reshape(1, -1),
    )
    back = turn[:4] + (lambda a: a.reshape(-1),)
    state = [turn[i % 5](a) for i, a in enumerate(state)]
    grads = gradients(
        nodes, cols, features.transpose(2, 0, 1), adjacency[0], node_mask, labels, label_mask, *state[:5]
    )
    outs = [jax.ShapeDtypeStruct((1, 1), F32)] * 3
    outs += [jax.ShapeDtypeStruct(a.shape, F32) for a in state[:5] for _ in range(4)]
    grads = [pltpu.with_memory_space_constraint(a, pltpu.VMEM) for a in grads]
    state = [pltpu.with_memory_space_constraint(a, pltpu.HBM) for a in state]
    done = pl.pallas_call(update_kernel, out_shape=outs)(*grads, *state)
    return (
        *(a.reshape(()) for a in done[:3]),
        *(back[i // 4](a) for i, a in enumerate(done[3:])),
    )


def solution(mesh):
    rows, first, rest, all_of = P("cols", "nodes", None), P(None, "cols"), P(None, None, "cols"), P()
    state = [first, rest, all_of, all_of, all_of]
    return jax.shard_map(
        functools.partial(local, mesh.shape["nodes"], mesh.shape["cols"]),
        mesh=mesh,
        in_specs=(rows, rows) + (P("cols", "nodes"),) * 3 + tuple(state * 4),
        out_specs=(all_of,) * 3 + tuple(spec for spec in state for _ in range(4)),
        check_vma=False,
    )
```

```python
import functools
import types

import jax
import jax.numpy as jnp
from jax import lax
from jax.experimental import pallas as pl
from jax.experimental.pallas import tpu as pltpu
from jax.sharding import PartitionSpec as P

LAYERS = 3
ADAM_STEP = 10
CLIP = 0.02
RATE_MATRIX = 0.03
RATE_SMALL = 0.3
BETA_ONE = 0.9
BETA_TWO = 0.999
ADAM_EPS = 1e-08
DECAY = 0.01
AVERAGE = 0.9
NORM_EPS = 1e-05

MESH = pl.DeviceIdType.MESH
F32 = jnp.float32
BF16 = jnp.bfloat16
LANES = 128
GELU_OUT = 0.7978845608028654
GELU_CUBE = 0.044715


def cat(values, axis):
    return values[0] if len(values) == 1 else jnp.concatenate(values, axis=axis)


def split(value):
    high = value.astype(BF16)
    return high, (value - high.astype(F32)).astype(BF16)


def dot(left, right):
    return lax.dot_general(left, right, (((1,), (0,)), ((), ())), preferred_element_type=F32)


def dot_t(left, right):
    return lax.dot_general(left, right, (((1,), (1,)), ((), ())), preferred_element_type=F32)


def dot3(left, right):
    (lh, ll), (rh, rl) = left, right
    return dot(cat([lh, lh, ll], 1), cat([rh, rl, rh], 0))


def dot3_t(left, right):
    (lh, ll), (rh, rl) = left, right
    return dot_t(cat([lh, lh, ll], 1), cat([rh, rl, rh], 1))


def remote(src, dst, send, recv, device):
    return pltpu.make_async_remote_copy(
        src_ref=src, dst_ref=dst, send_sem=send, recv_sem=recv, device_id=device, device_id_type=MESH
    )


def wait_bytes(ref, sem):
    pltpu.make_async_copy(ref, ref, sem).wait()


def flip(index, distance):
    bit = 1
    while bit <= distance:
        if distance & bit:
            index = index + (1 - 2 * lax.rem(lax.div(index, bit), 2)) * bit
        bit *= 2
    return index


def step_kernel(d, *refs):
    v = types.SimpleNamespace(**dict(zip(d.names, refs, strict=True)))
    NN, NC, R, H, HC, CH, L = d.NN, d.NC, d.R, d.H, d.HC, d.CH, LAYERS
    NDEV, RPP, PPC, PH, HV, F, FR, CR = d.NDEV, d.RPP, d.PPC, d.PH, d.HV, d.F, d.FR, d.CR
    n, c = lax.axis_index("nodes"), lax.axis_index("cols")
    me = n * NC + c
    ch, k = lax.div(n, 2), lax.rem(n, 2)
    sib = (ch * 2 + 1 - k, c)
    drains = []

    def device(index):
        return lax.div(index, NC), lax.rem(index, NC)

    def peer(dd):
        return flip(ch, dd) * 2 + k, c

    def rows(i, size):
        return pl.ds(pl.multiple_of(i * size, size), size)

    def send(src, dst, ssem, rsem, dev):
        remote(src, dst, ssem, rsem, dev).start()
        drains.append(lambda: wait_bytes(src, ssem))

    def either(always, condition, fn, other=None):
        if always:
            fn()
            return

        @pl.when(condition)
        def _():
            fn()

        if other is not None:

            @pl.when(jnp.logical_not(condition))
            def _():
                other()

    barrier = pltpu.get_barrier_semaphore()

    def adj_cols(j, core):
        return v.adj.at[:, rows(j * 2 + core, R)]

    own_rows = rows(c, HC)
    w_loads = [
        pltpu.make_async_copy(v.wr.at[i], v.wtr.at[i, own_rows, :], v.ld.at[i]) for i in range(L - 1)
    ]
    small_loads = [
        pltpu.make_async_copy(
            v.feat.at[:, 0, :] if name == "feat" else getattr(v, name),
            getattr(v, name + "_in"),
            v.ld.at[L - 1 + i],
        )
        for i, name in enumerate(d.small)
    ]
    for copy in small_loads + w_loads:
        copy.start()
    base = L - 1 + len(d.small)
    for j in range(CH):
        pltpu.make_async_copy(adj_cols(j, k), v.adjb.at[0, j], v.ld.at[base + j]).start()
    def greet(i, carry):
        pl.semaphore_signal(
            barrier, inc=1, device_id=device(lax.rem(me + i, NDEV)), device_id_type=MESH
        )
        return carry

    lax.fori_loop(1, NDEV, greet, 0)

    small_loads[0].wait()
    v.xown[:F, :] = v.feat_in[...]
    v.xown[F:, :] = jnp.ones((FR - F, R), F32)
    pl.semaphore_wait(barrier, NDEV - 1)

    def halves(ref):
        size = ref.shape[0]
        first = -(-size // 16) * 8
        return ref.at[:first], ref.at[first:]

    def ag_send(g, src, buf, part):
        s, r = v.s_ag.at[g], v.r_ag.at[g]
        mine = halves(src)
        slot = halves(buf.at[ch])
        if CH == 4:
            send(mine[part], slot[part], s.at[part], r.at[part], peer(1))
            if part == 1:
                send(mine[1], slot[1], s.at[3], r.at[3], peer(2))
                send(mine[0], slot[0], s.at[2], r.at[2], peer(2))
        elif part == 1:
            for dd in reversed(range(1, CH)):
                send(src, buf.at[ch], s.at[dd], r.at[dd], peer(dd))

    def ag_forward(g, buf):
        s, r = v.s_ag.at[g], v.r_ag.at[g]
        if CH == 4:
            x, y = (halves(buf.at[flip(ch, dd)]) for dd in (1, 2))
            wait_bytes(x[0], r.at[0])
            send(x[0], x[0], s.at[4], r.at[4], peer(2))
            wait_bytes(y[1], r.at[3])
            send(y[1], y[1], s.at[5], r.at[5], peer(1))

    def ag_blocks(g, buf, add):
        r = v.r_ag.at[g]
        if CH == 4:
            x, y, z = (halves(buf.at[flip(ch, dd)]) for dd in (1, 2, 3))
            add(flip(ch, 1), 0, x[0])
            add(flip(ch, 2), 1, y[1])
            wait_bytes(x[1], r.at[1])
            add(flip(ch, 1), 1, x[1])
            wait_bytes(y[0], r.at[2])
            add(flip(ch, 2), 0, y[0])
            wait_bytes(z[0], r.at[4])
            add(flip(ch, 3), 0, z[0])
            wait_bytes(z[1], r.at[5])
            add(flip(ch, 3), 1, z[1], True)
        else:
            for dd in range(1, CH):
                wait_bytes(buf.at[flip(ch, dd)], r.at[dd])
                for part in range(2):
                    add(flip(ch, dd), part, halves(buf.at[flip(ch, dd)])[part], dd == CH - 1 and part == 1)

    def to_others(start, at_once=False):
        if at_once and NDEV <= 32:
            for dc in [*reversed(range(1, NC)), 0]:
                for dn in reversed(range(NN)):
                    if dn or dc:
                        tn, tc = lax.rem(n + dn, NN) if dn else n, lax.rem(c + dc, NC) if dc else c
                        start((tn, tc), tn * NC + tc)
            return

        def one(i, carry):
            t = lax.rem(me + i, NDEV)
            start(device(t), t)
            return carry

        lax.fori_loop(1, NDEV, one, 0)

    def ar_send(a, at_once=False):
        to_others(
            lambda dev, t: remote(
                v.arb.at[a, me], v.arb.at[a, me], v.s_ar.at[a], v.r_ar.at[a], dev
            ).start(),
            at_once,
        )
        drains.append(lambda: wait_bytes(v.arb.at[a, pl.ds(0, NDEV - 1)], v.s_ar.at[a]))

    def ar_put(a, vectors):
        at = 0
        for vec in vectors:
            for i in range(vec.shape[1] // LANES):
                v.arb[a, me, at : at + 1, :] = vec[:, i * LANES : (i + 1) * LANES]
                at += 1
        if at < 4:
            v.arb[a, me, at:, :] = jnp.zeros((4 - at, LANES), F32)

    def ar_wait(a):
        wait_bytes(v.arb.at[a, pl.ds(0, NDEV - 1)], v.r_ar.at[a])
        return jnp.sum(v.arb[a], axis=0)

    def vec(total, i):
        return cat([total[i * HV + j : i * HV + j + 1] for j in range(HV)], 1)

    for part in range(2):
        ag_send(0, v.xown, v.xg, part)

    def w_ref(l):
        return v.wt0 if l == 0 else v.wtr.at[l - 1]

    def w_half(l, dd, core):
        at = lax.rem(c + dd, NC) * HC + core * (HC // 2)
        return w_ref(l).at[pl.ds(pl.multiple_of(at, HC // 2), HC // 2), :]

    def w_send(l):
        block = w_half(l, 0, k)
        for dd in range(1, NC):
            send(block, block, v.s_w.at[l, dd], v.r_w.at[l, dd], (n, lax.rem(c + dd, NC)))

    def w_pass(l):
        for dd in range(1, NC):
            block = w_half(l, NC - dd, k)
            wait_bytes(block, v.r_w.at[l, dd])
            send(block, block, v.s_wp.at[l, dd], v.r_wp.at[l, dd], sib)

    def w_wait(l):
        for dd in range(1, NC):
            wait_bytes(w_half(l, NC - dd, 1 - k), v.r_wp.at[l, dd])

    for copy in small_loads[1:]:
        copy.wait()
    v.wt0[own_rows, :] = jnp.zeros((HC, 2 * FR), F32)
    v.wt0[own_rows, :F] = v.w0_in[:, :F]
    v.wt0[own_rows, FR : FR + F] = v.w0_in[:, F:]
    w_send(0)
    for j in range(CH):
        send(adj_cols(j, 1 - k), v.adjb.at[1, j], v.s_adj.at[j], v.r_adj.at[j], sib)
    w_loads[0].wait()
    w_send(1)
    for copy in w_loads[1:]:
        copy.wait()

    def column(row):
        return jnp.broadcast_to(row.astype(F32), (LANES, R)).T

    v.valid[...] = column(v.nm_in[...])
    v.counted[...] = column(v.lm_in[...] * v.nm_in[...])
    v.label[...] = column(v.lb_in[...])
    v.whp[...] = jnp.zeros(v.whp.shape, F32)
    v.whp[: d.C, :] = v.whd_in[...]
    v.biasp[...] = jnp.zeros(v.biasp.shape, F32)
    v.biasp[:, : d.C] = v.bias_in[...]
    ar_put(
        8,
        [
            jnp.sum(v.valid[...], axis=0, keepdims=True),
            jnp.sum(v.counted[...], axis=0, keepdims=True),
        ],
    )
    ar_send(8)

    def adj_own(j, carry):
        pltpu.make_async_copy(adj_cols(j, k), v.adjb.at[0, j], v.ld.at[base + j]).wait()
        v.abf[j, :R, :] = v.adjb[0, j].astype(F32).astype(BF16)
        return carry

    def adj_sib(j, carry):
        wait_bytes(v.adjb.at[1, j], v.r_adj.at[j])
        v.abf[j, R:, :] = v.adjb[1, j].astype(F32).astype(BF16)
        return carry

    def adj_turn(j, carry):
        for side in range(2):
            v.at[side, j] = v.adjb[side, j].astype(F32).T.astype(BF16)
        return carry

    lax.fori_loop(0, CH, adj_own, 0)
    first_rows = len(drains)
    ag_forward(0, v.xg)
    lax.fori_loop(0, CH, adj_sib, 0)

    def wide(value):
        return cat([value] * HV, 1)

    RC = min(R // 2, 64)
    HALF = R // 2

    def activate(l, part):
        def chunk(i, carry):
            r = rows(i, RC)
            x = v.lin[r, :]
            square = x * x
            t = jnp.tanh(GELU_OUT * x * (1.0 + GELU_CUBE * square))
            half = 0.5 * (1.0 + t)
            act = x * half
            v.acts[l, r, :] = act
            v.gp[l, r, :] = half + (0.5 * GELU_OUT) * x * (1.0 - t * t) * (
                1.0 + (3.0 * GELU_CUBE) * square
            )
            masked = wide(v.valid[r, :]) * act
            return (
                carry[0] + jnp.sum(masked.reshape(RC // 8, 8, H), axis=0),
                carry[1] + jnp.sum((masked * act).reshape(RC // 8, 8, H), axis=0),
            )

        zero = jnp.zeros((8, H), F32)
        per = HALF // RC
        return lax.fori_loop(part * per, (part + 1) * per, chunk, (zero, zero))

    def over_rows(value):
        return jnp.sum(value, axis=0, keepdims=True)

    def keep_stats(l, total):
        count = jnp.max(v.count[0:1, :], axis=1, keepdims=True)
        mean = vec(total, 0) / count
        var = vec(total, 1) / count - mean * mean
        inverse = lax.rsqrt(var + NORM_EPS)
        gain, shift = v.npar_in[l, 0:1, :], v.npar_in[l, 1:2, :]
        v.vecs[l, 0:1, :] = mean
        v.vecs[l, 1:2, :] = inverse
        v.vecs[l, 2:3, :] = gain * inverse
        v.vecs[l, 3:4, :] = shift - mean * (gain * inverse)

    def finish(l, part_lin):
        sums = []
        for part in range(2):
            part_lin(part)
            sums.append(activate(l, part))
            if l < L - 1:
                ag_send(l + 1, v.acts.at[l], v.ag.at[l], part)
        ar_put(l, [over_rows(sums[0][i] + sums[1][i]) for i in range(2)])
        ar_send(l, l == L - 1)

    def add_first(chip, part, ref, last=False):
        high, low = split(ref[...])
        a = v.abf[chip]
        got = dot_t(cat([high, low], 1), cat([a, a], 1))
        first = -(-FR // 16) * 8
        r = slice(0, first) if part == 0 else slice(first, FR)
        seen = v.aggt[r, :]
        v.aggt[r, :] = seen + got

    v.aggt[...] = jnp.zeros((FR, 2 * R), F32)
    for part in range(2):
        add_first(ch, part, halves(v.xown)[part])
    w_pass(0)
    ag_blocks(0, v.xg, add_first)
    v.part0[...] = v.aggt[:, R:]
    send(v.part0, v.part0r, v.s_sib.at[0, 0], v.r_sib.at[0, 0], sib)
    w_wait(0)
    v.w0h[...], v.w0l[...] = split(v.wt0[...])
    feature = lax.broadcasted_iota(jnp.int32, (FR, R), 0) < F
    v.in0h[:FR, :], v.in0l[:FR, :] = split(jnp.where(feature, v.xown[...], 0.0))
    wait_bytes(v.part0r, v.r_sib.at[0, 0])
    total = v.aggt[:, :R] + v.part0r[...]
    degree = total[F : F + 1, :]
    v.in0h[FR:, :], v.in0l[FR:, :] = split(
        jnp.where(feature, total * (1.0 / jnp.maximum(degree, 1.0)), 0.0)
    )
    v.lin[...] = dot3((v.w0h[...], v.w0l[...]), (v.in0h[...], v.in0l[...])).T
    finish(0, lambda part: None)
    degree = column(degree)
    v.degree[...] = degree
    v.linked[...] = jnp.minimum(degree, 1.0)
    v.invdeg[...] = 1.0 / jnp.maximum(degree, 1.0)
    v.count[...] = ar_wait(8)[0:2]

    for l in range(1, L):
        if l == 1:
            lax.fori_loop(0, CH, adj_turn, 0)
        w_pass(l)
        ag_forward(l, v.ag.at[l - 1])
        w_wait(l)
        v.wh[l - 1], v.wl[l - 1] = split(v.wtr[l - 1])
        total = ar_wait(l - 1)
        if l < L - 1:
            w_send(l + 1)
        keep_stats(l - 1, total)
        scale, shift = v.vecs[l - 1, 2:3, :], v.vecs[l - 1, 3:4, :]
        v.inh[l - 1, :, :H], v.inl[l - 1, :, :H] = split(v.acts[l - 1] * scale + shift)
        v.lin[...] = dot3_t(
            (v.inh[l - 1, :, :H], v.inl[l - 1, :, :H]), (v.wh[l - 1, :, :H], v.wl[l - 1, :, :H])
        )

        parts, partr = v.parts.at[l - 1], v.partr.at[l - 1]

        def share(a, both, first=False):
            for at, total in ((R, parts), (0, v.agg)):
                got = dot(cat([a[at : at + R]] * 2, 1), both)
                total[...] = got if first else total[...] + got
                if at and a is v.last_columns:
                    for part in range(2):
                        send(
                            halves(parts)[part], halves(partr)[part], v.s_sib.at[l, part],
                            v.r_sib.at[l, part], sib,
                        )

        def add(chip, part, ref, last=False):
            columns = v.abf[chip, :, part * HALF : (part + 1) * HALF]
            v.last_columns = columns if last else None
            share(columns, cat(list(split(ref[...])), 0))

        v.last_columns = None
        share(v.abf[ch], cat(list(split(v.acts[l - 1])), 0), True)
        ag_blocks(l, v.ag.at[l - 1], add)

        def part_lin(part):
            r = slice(part * HALF, (part + 1) * HALF)
            wait_bytes(halves(partr)[part], v.r_sib.at[l, part])
            agg = v.agg[r, :] + partr[r, :]
            v.kept[l - 1, r, :] = agg
            v.inh[l - 1, r, H:], v.inl[l - 1, r, H:] = split(
                agg * wide(v.invdeg[r, :]) * scale + wide(v.linked[r, :]) * shift
            )
            v.lin[r, :] += dot3_t(
                (v.inh[l - 1, r, H:], v.inl[l - 1, r, H:]), (v.wh[l - 1, :, H:], v.wl[l - 1, :, H:])
            )

        finish(l, part_lin)

    for drain in drains[first_rows:]:
        drain()
    del drains[first_rows:]

    head = split(v.whp[...])
    lane = lax.broadcasted_iota(jnp.int32, (R, LANES), 1)
    onehot = jnp.where(lane.astype(F32) == v.label[...], 1.0, 0.0)
    real = lane < d.C
    counted = v.counted[...]
    label_count = jnp.max(v.count[1:2, :], axis=1, keepdims=True)
    keep_stats(L - 1, ar_wait(L - 1))
    last = split(v.acts[L - 1] * v.vecs[L - 1, 2:3, :] + v.vecs[L - 1, 3:4, :])
    logits = dot3_t(last, head) + v.biasp[...]
    top = jnp.max(jnp.where(real, logits, -3.0e38), axis=1, keepdims=True)
    moved = logits - top
    power = jnp.where(real, jnp.exp(moved), 0.0)
    power_sum = jnp.sum(power, axis=1, keepdims=True)
    g_logits = counted * (power / power_sum - onehot) / label_count
    gl_split = split(g_logits)
    v.gout[...] = dot3(gl_split, head)

    def last_sums():
        mean, inverse = v.vecs[L - 1, 0:1, :], v.vecs[L - 1, 1:2, :]

        def chunk(i, carry):
            r = rows(i, RC)
            g = v.gout[r, :]
            normed = (v.acts[L - 1, r, :] - mean) * inverse
            return (
                carry[0] + jnp.sum((g * normed).reshape(RC // 8, 8, H), axis=0),
                carry[1] + jnp.sum(g.reshape(RC // 8, 8, H), axis=0),
            )

        zero = jnp.zeros((8, H), F32)
        return [over_rows(s) for s in lax.fori_loop(0, R // RC, chunk, (zero, zero))]

    ar_put(3, last_sums())
    ar_send(3, True)
    logp = moved - jnp.log(power_sum)
    rows_loss = jnp.sum(jnp.where(real, onehot * logp, 0.0), axis=1, keepdims=True) * counted
    ar_put(6, [-over_rows(rows_loss), over_rows(g_logits)])
    ar_send(6)
    head_grad = dot3(split(g_logits.T[:CR, :]), last)
    HT = d.HT
    for t in range(HT):
        i, j = t // HV, t % HV
        v.hg[t] = head_grad[8 * i : 8 * i + 8, j * LANES : (j + 1) * LANES]

    def others(index, size, ref_of, init):
        return lax.fori_loop(1, size, lambda i, s: s + ref_of(lax.rem(index + i, size)), init)

    owners = [t * NDEV // HT for t in range(HT)]
    tile = lax.div(me * HT + NDEV - 1, NDEV)
    adds_tile = jnp.logical_and(tile < HT, lax.div(tile * NDEV, HT) == me)
    tile = jnp.minimum(tile, HT - 1)
    for t, owner in enumerate(owners):

        def go(t=t, owner=owner):
            remote(
                v.hg.at[t], v.hrecv.at[me], v.s_h.at[0], v.r_h.at[0], (owner // NC, owner % NC)
            ).start()

        either(False, me != owner, go)
    drains.append(
        lambda: either(
            HT == NDEV,
            adds_tile,
            lambda: wait_bytes(v.hrecv.at[pl.ds(0, HT - 1)], v.s_h.at[0]),
            lambda: wait_bytes(v.hrecv.at[pl.ds(0, HT)], v.s_h.at[0]),
        )
    )

    def head_gather():
        def go():
            wait_bytes(v.hrecv.at[pl.ds(0, NDEV - 1)], v.r_h.at[0])
            v.hfin[tile] = others(me, NDEV, lambda s: v.hrecv[s], v.hg[tile])

            def one(i, carry):
                remote(
                    v.hfin.at[tile], v.hfin.at[tile], v.s_h.at[1], v.r_h.at[1],
                    device(lax.rem(me + i, NDEV)),
                ).start()
                return carry

            lax.fori_loop(1, NDEV, one, 0)

        either(HT == NDEV, adds_tile, go)
        drains.append(
            lambda: either(
                HT == NDEV,
                adds_tile,
                lambda: wait_bytes(v.hrecv.at[pl.ds(0, NDEV - 1)], v.s_h.at[1]),
            )
        )

    def sibling_send(i):
        send(v.dwb.at[i, 1 - k], v.dwr.at[i], v.s_d.at[i], v.r_d.at[i], sib)

    def cols_send(i):
        wait_bytes(v.dwr.at[i], v.r_d.at[i])
        v.dwb[i, k] += v.dwr[i]
        for dd in range(1, NC):
            t = lax.rem(c + dd, NC)
            remote(v.dwb.at[i, k, t], v.zrecv.at[i, c], v.s_z.at[i], v.r_z.at[i], (n, t)).start()
        drains.append(lambda: wait_bytes(v.zrecv.at[i, pl.ds(0, NC - 1)], v.s_z.at[i]))

    def nodes_send(i):
        wait_bytes(v.zrecv.at[i, pl.ds(0, NC - 1)], v.r_z.at[i])
        v.zs[i] = others(c, NC, lambda s: v.zrecv[i, s], v.dwb[i, k, c])

        def one(j, carry):
            t = lax.rem(ch + j, CH)
            either(
                PH == CH,
                t < PH,
                lambda: remote(
                    v.zs.at[i, rows(t, RPP), :], v.nrecv.at[i, ch], v.s_n.at[i], v.r_n.at[i],
                    (t * 2 + k, c),
                ).start(),
            )
            return carry

        lax.fori_loop(1, CH, one, 0)
        drains.append(
            lambda: either(
                PH == CH,
                ch < PH,
                lambda: wait_bytes(v.zs.at[i, pl.ds(0, (PH - 1) * RPP), :], v.s_n.at[i]),
                lambda: wait_bytes(v.zs.at[i, pl.ds(0, PH * RPP), :], v.s_n.at[i]),
            )
        )

    def pieces_out(i, fin, at, piece):
        mine = pl.ds(pl.multiple_of(at, RPP), RPP)
        fin[mine, :] = piece
        square = jnp.sum((piece * piece).reshape(RPP // 8, 8, piece.shape[1]), axis=0)
        v.sq[...] += jnp.sum(square, axis=1, keepdims=True)

        def one(j, carry):
            block = fin.at[mine, :]
            remote(block, block, v.s_f.at[i], v.r_f.at[i], (lax.rem(n + j, NN), c)).start()
            return carry

        lax.fori_loop(1, NN, one, 0)

    def pieces_drain(i, fin):
        drains.append(
            lambda: either(
                PPC == NN,
                n < PPC if i == L - 1 else ch < PH,
                lambda: lax.fori_loop(
                    1, NN, lambda j, carry: (wait_bytes(fin.at[pl.ds(0, RPP), :], v.s_f.at[i]), carry)[1], 0
                ),
            )
        )

    def nodes_gather(i):
        def go():
            wait_bytes(v.nrecv.at[i, pl.ds(0, CH - 1)], v.r_n.at[i])
            piece = others(ch, CH, lambda s: v.nrecv[i, s], v.zs[i, rows(ch, RPP), :])
            pieces_out(i, v.fin.at[i], k * (HC // 2) + ch * RPP, piece)

        either(PH == CH, ch < PH, go)
        pieces_drain(i, v.fin.at[i])

    v.sq[...] = jnp.zeros((8, LANES), F32)

    def fin_wait(i, fin):
        either(
            PPC == NN,
            n < PPC if i == L - 1 else ch < PH,
            lambda: wait_bytes(fin.at[pl.ds(0, (PPC - 1) * RPP), :], v.r_f.at[i]),
            lambda: wait_bytes(fin.at[pl.ds(0, PPC * RPP), :], v.r_f.at[i]),
        )

    def give(i, src, dst):
        copy = pltpu.make_async_copy(src, dst, v.s_out.at[i])
        copy.start()
        drains.append(copy.wait)

    def linear_grad(l, a):
        total = ar_wait(a)
        g_gain, g_shift = vec(total, 0), vec(total, 1)
        v.gn_o[l, 0:1, :] = g_gain
        v.gn_o[l, 1:2, :] = g_shift
        mean, inverse, scale = v.vecs[l, 0:1, :], v.vecs[l, 1:2, :], v.vecs[l, 2:3, :]
        count = jnp.max(v.count[0:1, :], axis=1, keepdims=True)
        by_one = scale * g_shift / count
        by_normed = scale * g_gain / count

        def chunk(i, carry):
            r = rows(i, RC)
            normed = (v.acts[l, r, :] - mean) * inverse
            g_active = scale * v.gout[r, :] - wide(v.valid[r, :]) * (by_one + normed * by_normed)
            g_linear = v.gp[l, r, :] * g_active
            v.lin[r, :] = g_linear
            v.glh[r, :], v.gll[r, :] = split(g_linear)
            return carry

        lax.fori_loop(0, R // RC, chunk, 0)

    for l in (2, 1):
        g = l - 1
        linear_grad(l, 5 - l)
        gl = (v.glh[...], v.gll[...])
        back = v.ag.at[2 - l]
        for part in range(2):
            r = slice(part * HALF, (part + 1) * HALF)
            spread = dot3((v.glh[r, :], v.gll[r, :]), (v.wh[g, :, H:], v.wl[g, :, H:]))
            v.spreads[g, r, :] = spread * wide(v.invdeg[r, :])
            send(
                halves(v.spreads.at[g])[part], halves(v.spreadr.at[g])[part],
                v.s_sib.at[L + g, part], v.r_sib.at[L + g, part], sib,
            )
        if g == 0:
            for drain in scatter_drains:
                drain()
        own = cat(list(split(v.spreads[g])), 0)
        for dd in reversed(range(CH)):
            t = v.at[0, flip(ch, dd)]
            v.out[dd] = dot(cat([t, t], 1), own)
        for part in range(2):
            wait_bytes(halves(v.spreadr.at[g])[part], v.r_sib.at[L + g, part])
        other = cat(list(split(v.spreadr[g])), 0)

        def complete(dd):
            t = v.at[1, flip(ch, dd)]
            v.out[dd] += dot(cat([t, t], 1), other)

        s, r = v.s_rs.at[g], v.r_rs.at[g]
        kept_drains, drains = drains, []
        if CH == 4:
            x, y, z = (halves(v.out.at[dd]) for dd in (1, 2, 3))
            from_x, from_y, via = (halves(back.at[i]) for i in range(3))
            complete(3)
            send(z[0], via[0], s.at[0], r.at[0], peer(1))
            send(z[1], via[1], s.at[1], r.at[1], peer(2))
            complete(1)
            send(x[0], from_x[0], s.at[2], r.at[2], peer(1))
            complete(2)
            send(y[1], from_y[1], s.at[3], r.at[3], peer(2))
            complete(0)
        else:
            for dd in reversed(range(1, CH)):
                complete(dd)
                send(v.out.at[dd], back.at[dd], s.at[dd], r.at[dd], peer(dd))
            complete(0)
        v.gout[...] = dot3(gl, (v.wh[g, :, :H], v.wl[g, :, :H]))
        mean, inverse = v.vecs[g, 0:1, :], v.vecs[g, 1:2, :]

        def chunk(i, carry):
            r = rows(i, RC)
            self, spread, degree = v.gout[r, :], v.spreads[g, r, :], wide(v.degree[r, :])
            normed = (v.acts[g, r, :] - mean) * inverse
            reached = (v.kept[g, r, :] - degree * mean) * inverse
            v.gout[r, :] = self + v.out[0, r, :]
            return (
                carry[0] + jnp.sum((self * normed + spread * reached).reshape(RC // 8, 8, H), axis=0),
                carry[1] + jnp.sum((self + spread * degree).reshape(RC // 8, 8, H), axis=0),
            )

        zero = jnp.zeros((8, H), F32)
        ar_put(6 - l, [over_rows(t) for t in lax.fori_loop(0, R // RC, chunk, (zero, zero))])
        ar_send(6 - l, True)
        grad = dot3(split(v.lin[...].T), (v.inh[g], v.inl[g]))
        for t in range(NC):
            for half in range(2):
                at = t * HC + half * (HC // 2)
                v.dwb[g, half, t] = grad[at : at + HC // 2, :]
        sibling_send(g)
        if CH == 4:
            wait_bytes(via[0], r.at[0])
            y[0][...] += via[0][...]
            send(y[0], from_y[0], s.at[5], r.at[5], peer(2))
            wait_bytes(via[1], r.at[1])
            x[1][...] += via[1][...]
            send(x[1], from_x[1], s.at[4], r.at[4], peer(1))
        scatter_drains, drains = drains, kept_drains
        if l == 2:
            head_gather()
        else:
            nodes_send(1)
        cols_send(g)
        if l == 1:
            nodes_gather(1)
        if CH == 4:
            for half, i in ((from_x[0], 2), (from_y[1], 3), (from_y[0], 5), (from_x[1], 4)):
                wait_bytes(half, r.at[i])
            v.gout[...] += back[0] + back[1]
        else:
            for dd in range(1, CH):
                wait_bytes(back.at[dd], r.at[dd])
                v.gout[...] += back[dd]
    drains += scatter_drains

    linear_grad(0, 5)
    grad = dot3_t(split(v.lin[...].T), (v.in0h[...], v.in0l[...]))
    for t in range(NC):
        v.d0[t] = grad[t * HC : (t + 1) * HC, :]

    def first_scatter(dev, t):
        tn, tc = dev
        either(
            PPC == NN,
            tn < PPC,
            lambda: remote(
                v.d0.at[tc, rows(tn, RPP), :], v.recv0.at[me], v.s_0.at[0], v.r_0.at[0], dev
            ).start(),
        )

    to_others(first_scatter, True)
    drains.append(
        lambda: either(
            PPC == NN,
            n < PPC,
            lambda: wait_bytes(v.recv0.at[pl.ds(0, PPC * NC - 1)], v.s_0.at[0]),
            lambda: wait_bytes(v.recv0.at[pl.ds(0, PPC * NC)], v.s_0.at[0]),
        )
    )
    nodes_send(0)
    nodes_gather(0)

    def first_gather():
        wait_bytes(v.recv0.at[pl.ds(0, NDEV - 1)], v.r_0.at[0])
        piece = others(me, NDEV, lambda s: v.recv0[s], v.d0[c, rows(n, RPP), :])
        pieces_out(L - 1, v.fin0, n * RPP, piece)

    either(PPC == NN, n < PPC, first_gather)
    pieces_drain(L - 1, v.fin0)
    ar_put(7, [over_rows(v.sq[...])])
    ar_send(7, True)

    total = ar_wait(6)
    bias_grad = total[1:2]
    v.misc_o[...] = jnp.zeros((8, LANES), F32)
    v.misc_o[0:1, :] = total[0:1]
    v.misc_o[1:2, :] = v.count[1:2, :]
    v.misc_o[3:4, :] = bias_grad
    either(
        HT == NDEV,
        adds_tile,
        lambda: wait_bytes(v.hfin.at[pl.ds(0, HT - 1)], v.r_h.at[1]),
        lambda: wait_bytes(v.hfin.at[pl.ds(0, HT)], v.r_h.at[1]),
    )
    give(2, v.gn_o, v.gn)
    give(3, v.hfin, v.gh)
    square = jnp.zeros((8, LANES), F32)
    for t in range(HT):
        square += v.hfin[t] * v.hfin[t]
    replicated = over_rows(square) + bias_grad * bias_grad
    small = jnp.zeros((1, H), F32)
    for l in range(L):
        small += over_rows(v.gn_o[l] * v.gn_o[l])
    for j in range(HV):
        replicated += small[:, j * LANES : (j + 1) * LANES]
    for i in range(L - 1):
        fin_wait(i, v.fin.at[i])
        give(5 + i, v.fin.at[i], v.gr.at[i])
    total = ar_wait(7)
    squares = total[0:1, 0:1] + jnp.sum(replicated, axis=1, keepdims=True)
    norm = jnp.sqrt(squares)
    v.misc_o[2:3, :] = jnp.broadcast_to(norm, (1, LANES))
    v.misc_o[4:5, :] = jnp.broadcast_to(CLIP / jnp.maximum(norm, CLIP), (1, LANES))
    give(4, v.misc_o, v.misc)
    fin_wait(L - 1, v.fin0)
    give(0, v.fin0, v.g0)

    for drain in drains:
        drain()


def gradients(NN, NC, feat, adj, nm, lb, lm, w0, wr, npar, whd, bias):
    F, _, R = feat.shape
    C, H = whd.shape
    HC = w0.shape[0]
    CH, NDEV = NN // 2, NN * NC
    up = lambda size: -(-size // 8) * 8
    FR, CR = up(F + 1), up(C)
    RPP = max(8, HC // NN)
    HV = H // LANES
    d = types.SimpleNamespace(
        NN=NN, NC=NC, R=R, F=F, H=H, C=C, HC=HC, CH=CH, NDEV=NDEV, FR=FR, CR=CR, RPP=RPP,
        PPC=HC // RPP, PH=HC // RPP // 2, HV=HV, HT=CR // 8 * HV,
    )
    dma = pltpu.SemaphoreType.DMA
    L = LAYERS
    inputs = {
        "feat": feat, "adj": adj, "nm": nm, "lb": lb, "lm": lm, "w0": w0, "wr": wr, "npar": npar,
        "whd": whd, "bias": bias,
    }
    small = [name for name in inputs if name not in ("adj", "wr")]
    d.small = small
    scratch = {
        "xown": pltpu.VMEM((FR, R), F32),
        "xg": pltpu.VMEM((CH, FR, R), F32),
        "ag": pltpu.VMEM((L - 1, CH, R, H), F32),
        "acts": pltpu.VMEM((L, R, H), F32),
        "gp": pltpu.VMEM((L, R, H), F32),
        "adjb": pltpu.VMEM((2, CH, R, R), jnp.int32),
        "abf": pltpu.VMEM((CH, 2 * R, R), BF16),
        "at": pltpu.VMEM((2, CH, R, R), BF16),
        "wt0": pltpu.VMEM((H, 2 * FR), F32),
        "wtr": pltpu.VMEM((L - 1, H, 2 * H), F32),
        "w0h": pltpu.VMEM((H, 2 * FR), BF16),
        "w0l": pltpu.VMEM((H, 2 * FR), BF16),
        "wh": pltpu.VMEM((L - 1, H, 2 * H), BF16),
        "wl": pltpu.VMEM((L - 1, H, 2 * H), BF16),
        "whp": pltpu.VMEM((LANES, H), F32),
        "biasp": pltpu.VMEM((1, LANES), F32),
        "in0h": pltpu.VMEM((2 * FR, R), BF16),
        "in0l": pltpu.VMEM((2 * FR, R), BF16),
        "inh": pltpu.VMEM((L - 1, R, 2 * H), BF16),
        "inl": pltpu.VMEM((L - 1, R, 2 * H), BF16),
        "aggt": pltpu.VMEM((FR, 2 * R), F32),
        "part0": pltpu.VMEM((FR, R), F32),
        "part0r": pltpu.VMEM((FR, R), F32),
        "agg": pltpu.VMEM((R, H), F32),
        "parts": pltpu.VMEM((L - 1, R, H), F32),
        "partr": pltpu.VMEM((L - 1, R, H), F32),
        "kept": pltpu.VMEM((L - 1, R, H), F32),
        "lin": pltpu.VMEM((R, H), F32),
        "gout": pltpu.VMEM((R, H), F32),
        "glh": pltpu.VMEM((R, H), BF16),
        "gll": pltpu.VMEM((R, H), BF16),
        "spreads": pltpu.VMEM((L - 1, R, H), F32),
        "spreadr": pltpu.VMEM((L - 1, R, H), F32),
        "out": pltpu.VMEM((CH, R, H), F32),
        "valid": pltpu.VMEM((R, LANES), F32),
        "counted": pltpu.VMEM((R, LANES), F32),
        "label": pltpu.VMEM((R, LANES), F32),
        "degree": pltpu.VMEM((R, LANES), F32),
        "invdeg": pltpu.VMEM((R, LANES), F32),
        "linked": pltpu.VMEM((R, LANES), F32),
        "count": pltpu.VMEM((2, LANES), F32),
        "vecs": pltpu.VMEM((L, 8, H), F32),
        "sq": pltpu.VMEM((8, LANES), F32),
        "arb": pltpu.VMEM((9, NDEV, 4, LANES), F32),
        "dwb": pltpu.VMEM((L - 1, 2, NC, HC // 2, 2 * H), F32),
        "dwr": pltpu.VMEM((L - 1, NC, HC // 2, 2 * H), F32),
        "zrecv": pltpu.VMEM((L - 1, NC, HC // 2, 2 * H), F32),
        "zs": pltpu.VMEM((L - 1, HC // 2, 2 * H), F32),
        "nrecv": pltpu.VMEM((L - 1, CH, RPP, 2 * H), F32),
        "fin": pltpu.VMEM((L - 1, HC, 2 * H), F32),
        "d0": pltpu.VMEM((NC, HC, 2 * FR), F32),
        "recv0": pltpu.VMEM((NDEV, RPP, 2 * FR), F32),
        "fin0": pltpu.VMEM((HC, 2 * FR), F32),
        "hg": pltpu.VMEM((d.HT, 8, LANES), F32),
        "hrecv": pltpu.VMEM((NDEV, 8, LANES), F32),
        "hfin": pltpu.VMEM((d.HT, 8, LANES), F32),
        "ld": dma((L - 1 + len(small) + CH,)),
        "s_adj": dma((CH,)),
        "r_adj": dma((CH,)),
        "s_ag": dma((L, max(CH, 6))),
        "r_ag": dma((L, max(CH, 6))),
        "s_sib": dma((2 * L - 1, 2)),
        "r_sib": dma((2 * L - 1, 2)),
        "s_w": dma((L, NC)),
        "r_w": dma((L, NC)),
        "s_wp": dma((L, NC)),
        "r_wp": dma((L, NC)),
        "s_d": dma((L - 1,)),
        "r_d": dma((L - 1,)),
        "s_ar": dma((9,)),
        "r_ar": dma((9,)),
        "s_rs": dma((L - 1, max(CH, 6))),
        "r_rs": dma((L - 1, max(CH, 6))),
        "s_z": dma((L - 1,)),
        "r_z": dma((L - 1,)),
        "s_n": dma((L - 1,)),
        "r_n": dma((L - 1,)),
        "s_f": dma((L,)),
        "r_f": dma((L,)),
        "s_0": dma((1,)),
        "r_0": dma((1,)),
        "s_h": dma((2,)),
        "r_h": dma((2,)),
        "gn_o": pltpu.VMEM(npar.shape, F32),
        "misc_o": pltpu.VMEM((8, LANES), F32),
        "s_out": dma((L + 4,)),
    }
    for name in small:
        shape = (F, R) if name == "feat" else inputs[name].shape
        scratch[name + "_in"] = pltpu.VMEM(shape, inputs[name].dtype)
    ins = list(inputs)
    room = 6 * 2**20
    for ref in scratch.values():
        if ref.memory_space == pltpu.VMEM:
            size = jnp.dtype(ref.dtype).itemsize
            for i, length in enumerate(reversed(ref.shape)):
                size *= -(-length // LANES) * LANES if i == 0 else -(-length // 8) * 8 if i == 1 else length
            room += size
    outs = ["g0", "gr", "gn", "gh", "misc"]
    d.names = ins + outs + list(scratch)
    return pl.pallas_call(
        functools.partial(step_kernel, d),
        out_shape=[
            jax.ShapeDtypeStruct((HC, 2 * FR), F32),
            jax.ShapeDtypeStruct(wr.shape, F32),
            jax.ShapeDtypeStruct(npar.shape, F32),
            jax.ShapeDtypeStruct((d.HT, 8, LANES), F32),
            jax.ShapeDtypeStruct((8, LANES), F32),
        ],
        in_specs=[pl.BlockSpec(memory_space=pltpu.HBM)] * len(ins),
        out_specs=[pl.BlockSpec(memory_space=pl.ANY)] * len(outs),
        scratch_shapes=list(scratch.values()),
        compiler_params=pltpu.CompilerParams(
            collective_id=0, has_side_effects=True, vmem_limit_bytes=min(room, 60 * 2**20)
        ),
    )(*(pltpu.with_memory_space_constraint(a, pltpu.HBM) for a in inputs.values()))


def adamw(weight, first, second, average, grad, rate):
    first = BETA_ONE * first + (1.0 - BETA_ONE) * grad
    second = BETA_TWO * second + (1.0 - BETA_TWO) * grad * grad
    fix_one = 1.0 - BETA_ONE**ADAM_STEP
    fix_two = 1.0 - BETA_TWO**ADAM_STEP
    update = first / fix_one / (jnp.sqrt(second / fix_two) + ADAM_EPS)
    weight = weight - rate * (update + DECAY * weight)
    average = AVERAGE * average + (1.0 - AVERAGE) * weight
    return (first, second, weight, average)


def update_kernel(*refs):
    grads, state, scalars, results = refs[:5], refs[5:25], refs[25:28], refs[28:]
    misc = grads[4]
    scale = misc[4:5, 0:1]
    for i in range(3):
        scalars[i][...] = misc[i : i + 1, 0:1]
    for group in range(5):
        weight, first, second, average = (state[group + 5 * j] for j in range(4))
        rate = RATE_SMALL if group in (2, 4) else RATE_MATRIX
        shape = weight.shape
        if group == 4:
            grad = misc[3:4, : shape[1]]
        elif group == 3:
            wide = shape[1] // LANES
            grad = cat(
                [
                    cat([grads[3][wide * i + j] for j in range(wide)], 1)
                    for i in range(grads[3].shape[0] // wide)
                ],
                0,
            )[: shape[0]]
        elif group == 0:
            half = shape[1] // 2
            at = grads[0].shape[1] // 2
            grad = cat([grads[0][:, :half], grads[0][:, at : at + half]], 1)
        else:
            grad = grads[group][...]
        done = adamw(weight[...], first[...], second[...], average[...], grad * scale, rate)
        for ref, value in zip(results[4 * group : 4 * group + 4], done, strict=True):
            ref[...] = value


def local(
    nodes, cols, features, adjacency, node_mask, labels, label_mask, *state
):
    turn = (
        lambda a: a.T,
        lambda a: a.transpose(0, 2, 1),
        lambda a: a.transpose(1, 0, 2),
        lambda a: a.T,
        lambda a: a.reshape(1, -1),
    )
    back = turn[:4] + (lambda a: a.reshape(-1),)
    state = [turn[i % 5](a) for i, a in enumerate(state)]
    grads = gradients(
        nodes, cols, features.transpose(2, 0, 1), adjacency[0], node_mask, labels, label_mask, *state[:5]
    )
    outs = [jax.ShapeDtypeStruct((1, 1), F32)] * 3
    outs += [jax.ShapeDtypeStruct(a.shape, F32) for a in state[:5] for _ in range(4)]
    grads = [pltpu.with_memory_space_constraint(a, pltpu.VMEM) for a in grads]
    state = [pltpu.with_memory_space_constraint(a, pltpu.HBM) for a in state]
    done = pl.pallas_call(update_kernel, out_shape=outs)(*grads, *state)
    return (
        *(a.reshape(()) for a in done[:3]),
        *(back[i // 4](a) for i, a in enumerate(done[3:])),
    )


def solution(mesh):
    rows, first, rest, all_of = P("cols", "nodes", None), P(None, "cols"), P(None, None, "cols"), P()
    state = [first, rest, all_of, all_of, all_of]
    return jax.shard_map(
        functools.partial(local, mesh.shape["nodes"], mesh.shape["cols"]),
        mesh=mesh,
        in_specs=(rows, rows) + (P("cols", "nodes"),) * 3 + tuple(state * 4),
        out_specs=(all_of,) * 3 + tuple(spec for spec in state for _ in range(4)),
        check_vma=False,
    )
```

```python
import functools
import types

import jax
import jax.numpy as jnp
from jax import lax
from jax.experimental import pallas as pl
from jax.experimental.pallas import tpu as pltpu
from jax.sharding import PartitionSpec as P

LAYERS = 3
ADAM_STEP = 10
CLIP = 0.02
RATE_MATRIX = 0.03
RATE_SMALL = 0.3
BETA_ONE = 0.9
BETA_TWO = 0.999
ADAM_EPS = 1e-08
DECAY = 0.01
AVERAGE = 0.9
NORM_EPS = 1e-05

MESH = pl.DeviceIdType.MESH
F32 = jnp.float32
BF16 = jnp.bfloat16
LANES = 128
GELU_OUT = 0.7978845608028654
GELU_CUBE = 0.044715


def cat(values, axis):
    return values[0] if len(values) == 1 else jnp.concatenate(values, axis=axis)


def split(value):
    high = value.astype(BF16)
    return high, (value - high.astype(F32)).astype(BF16)


def dot(left, right):
    return lax.dot_general(left, right, (((1,), (0,)), ((), ())), preferred_element_type=F32)


def dot_t(left, right):
    return lax.dot_general(left, right, (((1,), (1,)), ((), ())), preferred_element_type=F32)


def dot3(left, right):
    (lh, ll), (rh, rl) = left, right
    return dot(cat([lh, lh, ll], 1), cat([rh, rl, rh], 0))


def dot3_t(left, right):
    (lh, ll), (rh, rl) = left, right
    return dot_t(cat([lh, lh, ll], 1), cat([rh, rl, rh], 1))


def remote(src, dst, send, recv, device):
    return pltpu.make_async_remote_copy(
        src_ref=src, dst_ref=dst, send_sem=send, recv_sem=recv, device_id=device, device_id_type=MESH
    )


def wait_bytes(ref, sem):
    pltpu.make_async_copy(ref, ref, sem).wait()


def flip(index, distance):
    bit = 1
    while bit <= distance:
        if distance & bit:
            index = index + (1 - 2 * lax.rem(lax.div(index, bit), 2)) * bit
        bit *= 2
    return index


def step_kernel(d, *refs):
    v = types.SimpleNamespace(**dict(zip(d.names, refs, strict=True)))
    NN, NC, R, H, HC, CH, L = d.NN, d.NC, d.R, d.H, d.HC, d.CH, LAYERS
    NDEV, RPP, PPC, PH, HV, F, FR, CR = d.NDEV, d.RPP, d.PPC, d.PH, d.HV, d.F, d.FR, d.CR
    n, c = lax.axis_index("nodes"), lax.axis_index("cols")
    me = n * NC + c
    ch, k = lax.div(n, 2), lax.rem(n, 2)
    sib = (ch * 2 + 1 - k, c)
    drains = []

    def device(index):
        return lax.div(index, NC), lax.rem(index, NC)

    def peer(dd):
        return flip(ch, dd) * 2 + k, c

    def rows(i, size):
        return pl.ds(pl.multiple_of(i * size, size), size)

    def send(src, dst, ssem, rsem, dev):
        remote(src, dst, ssem, rsem, dev).start()
        drains.append(lambda: wait_bytes(src, ssem))

    def either(always, condition, fn, other=None):
        if always:
            fn()
            return

        @pl.when(condition)
        def _():
            fn()

        if other is not None:

            @pl.when(jnp.logical_not(condition))
            def _():
                other()

    barrier = pltpu.get_barrier_semaphore()

    def adj_cols(j, core):
        return v.adj.at[:, rows(j * 2 + core, R)]

    own_rows = rows(c, HC)
    w_loads = [
        pltpu.make_async_copy(v.wr.at[i], v.wtr.at[i, own_rows, :], v.ld.at[i]) for i in range(L - 1)
    ]
    small_loads = [
        pltpu.make_async_copy(
            v.feat.at[:, 0, :] if name == "feat" else getattr(v, name),
            getattr(v, name + "_in"),
            v.ld.at[L - 1 + i],
        )
        for i, name in enumerate(d.small)
    ]
    for copy in small_loads + w_loads:
        copy.start()
    base = L - 1 + len(d.small)
    for j in range(CH):
        pltpu.make_async_copy(adj_cols(j, k), v.adjb.at[0, j], v.ld.at[base + j]).start()
    def greet(i, carry):
        pl.semaphore_signal(
            barrier, inc=1, device_id=device(lax.rem(me + i, NDEV)), device_id_type=MESH
        )
        return carry

    lax.fori_loop(1, NDEV, greet, 0)

    small_loads[0].wait()
    v.xown[:F, :] = v.feat_in[...]
    v.xown[F:, :] = jnp.ones((FR - F, R), F32)
    pl.semaphore_wait(barrier, NDEV - 1)

    def halves(ref):
        size = ref.shape[0]
        first = -(-size // 16) * 8
        return ref.at[:first], ref.at[first:]

    def ag_send(g, src, buf, part):
        s, r = v.s_ag.at[g], v.r_ag.at[g]
        mine = halves(src)
        slot = halves(buf.at[ch])
        if CH == 4:
            send(mine[part], slot[part], s.at[part], r.at[part], peer(1))
            if part == 1:
                send(mine[1], slot[1], s.at[3], r.at[3], peer(2))
                send(mine[0], slot[0], s.at[2], r.at[2], peer(2))
        elif part == 1:
            for dd in reversed(range(1, CH)):
                send(src, buf.at[ch], s.at[dd], r.at[dd], peer(dd))

    def ag_forward(g, buf):
        s, r = v.s_ag.at[g], v.r_ag.at[g]
        if CH == 4:
            x, y = (halves(buf.at[flip(ch, dd)]) for dd in (1, 2))
            wait_bytes(x[0], r.at[0])
            send(x[0], x[0], s.at[4], r.at[4], peer(2))
            wait_bytes(y[1], r.at[3])
            send(y[1], y[1], s.at[5], r.at[5], peer(1))

    def ag_blocks(g, buf, add):
        r = v.r_ag.at[g]
        if CH == 4:
            x, y, z = (halves(buf.at[flip(ch, dd)]) for dd in (1, 2, 3))
            add(flip(ch, 1), 0, x[0])
            add(flip(ch, 2), 1, y[1])
            wait_bytes(x[1], r.at[1])
            add(flip(ch, 1), 1, x[1])
            wait_bytes(y[0], r.at[2])
            add(flip(ch, 2), 0, y[0])
            wait_bytes(z[0], r.at[4])
            add(flip(ch, 3), 0, z[0])
            wait_bytes(z[1], r.at[5])
            add(flip(ch, 3), 1, z[1], True)
        else:
            for dd in range(1, CH):
                wait_bytes(buf.at[flip(ch, dd)], r.at[dd])
                for part in range(2):
                    add(flip(ch, dd), part, halves(buf.at[flip(ch, dd)])[part], dd == CH - 1 and part == 1)

    def to_others(start, at_once=False):
        if at_once and NDEV <= 32:
            for dc in [*reversed(range(1, NC)), 0]:
                for dn in reversed(range(NN)):
                    if dn or dc:
                        tn, tc = lax.rem(n + dn, NN) if dn else n, lax.rem(c + dc, NC) if dc else c
                        start((tn, tc), tn * NC + tc)
            return

        def one(i, carry):
            t = lax.rem(me + i, NDEV)
            start(device(t), t)
            return carry

        lax.fori_loop(1, NDEV, one, 0)

    def ar_send(a, at_once=False):
        to_others(
            lambda dev, t: remote(
                v.arb.at[a, me], v.arb.at[a, me], v.s_ar.at[a], v.r_ar.at[a], dev
            ).start(),
            at_once,
        )
        drains.append(lambda: wait_bytes(v.arb.at[a, pl.ds(0, NDEV - 1)], v.s_ar.at[a]))

    def ar_put(a, vectors):
        at = 0
        for vec in vectors:
            for i in range(vec.shape[1] // LANES):
                v.arb[a, me, at : at + 1, :] = vec[:, i * LANES : (i + 1) * LANES]
                at += 1
        if at < 4:
            v.arb[a, me, at:, :] = jnp.zeros((4 - at, LANES), F32)

    def ar_wait(a):
        wait_bytes(v.arb.at[a, pl.ds(0, NDEV - 1)], v.r_ar.at[a])
        return jnp.sum(v.arb[a], axis=0)

    def vec(total, i):
        return cat([total[i * HV + j : i * HV + j + 1] for j in range(HV)], 1)

    for part in range(2):
        ag_send(0, v.xown, v.xg, part)

    def w_ref(l):
        return v.wt0 if l == 0 else v.wtr.at[l - 1]

    def w_half(l, dd, core):
        at = lax.rem(c + dd, NC) * HC + core * (HC // 2)
        return w_ref(l).at[pl.ds(pl.multiple_of(at, HC // 2), HC // 2), :]

    def w_send(l):
        block = w_half(l, 0, k)
        for dd in range(1, NC):
            send(block, block, v.s_w.at[l, dd], v.r_w.at[l, dd], (n, lax.rem(c + dd, NC)))

    def w_pass(l):
        for dd in range(1, NC):
            block = w_half(l, NC - dd, k)
            wait_bytes(block, v.r_w.at[l, dd])
            send(block, block, v.s_wp.at[l, dd], v.r_wp.at[l, dd], sib)

    def w_wait(l):
        for dd in range(1, NC):
            wait_bytes(w_half(l, NC - dd, 1 - k), v.r_wp.at[l, dd])

    for copy in small_loads[1:]:
        copy.wait()
    v.wt0[own_rows, :] = jnp.zeros((HC, 2 * FR), F32)
    v.wt0[own_rows, :F] = v.w0_in[:, :F]
    v.wt0[own_rows, FR : FR + F] = v.w0_in[:, F:]
    w_send(0)
    for j in range(CH):
        send(adj_cols(j, 1 - k), v.adjb.at[1, j], v.s_adj.at[j], v.r_adj.at[j], sib)
    w_loads[0].wait()
    w_send(1)
    for copy in w_loads[1:]:
        copy.wait()

    def column(row):
        return jnp.broadcast_to(row.astype(F32), (LANES, R)).T

    v.valid[...] = column(v.nm_in[...])
    v.counted[...] = column(v.lm_in[...] * v.nm_in[...])
    v.label[...] = column(v.lb_in[...])
    v.whp[...] = jnp.zeros(v.whp.shape, F32)
    v.whp[: d.C, :] = v.whd_in[...]
    v.biasp[...] = jnp.zeros(v.biasp.shape, F32)
    v.biasp[:, : d.C] = v.bias_in[...]
    ar_put(
        8,
        [
            jnp.sum(v.valid[...], axis=0, keepdims=True),
            jnp.sum(v.counted[...], axis=0, keepdims=True),
        ],
    )
    ar_send(8)

    def adj_own(j, carry):
        pltpu.make_async_copy(adj_cols(j, k), v.adjb.at[0, j], v.ld.at[base + j]).wait()
        v.abf[j, :R, :] = v.adjb[0, j].astype(F32).astype(BF16)
        return carry

    def adj_sib(j, carry):
        wait_bytes(v.adjb.at[1, j], v.r_adj.at[j])
        v.abf[j, R:, :] = v.adjb[1, j].astype(F32).astype(BF16)
        return carry

    def adj_turn(j, carry):
        for side in range(2):
            v.at[side, j] = v.adjb[side, j].astype(F32).T.astype(BF16)
        return carry

    lax.fori_loop(0, CH, adj_own, 0)
    first_rows = len(drains)
    ag_forward(0, v.xg)
    lax.fori_loop(0, CH, adj_sib, 0)

    def wide(value):
        return cat([value] * HV, 1)

    RC = min(R // 2, 64)
    HALF = R // 2

    def activate(l, part):
        def chunk(i, carry):
            r = rows(i, RC)
            x = v.lin[r, :]
            square = x * x
            t = jnp.tanh(GELU_OUT * x * (1.0 + GELU_CUBE * square))
            half = 0.5 * (1.0 + t)
            act = x * half
            v.acts[l, r, :] = act
            v.gp[l, r, :] = half + (0.5 * GELU_OUT) * x * (1.0 - t * t) * (
                1.0 + (3.0 * GELU_CUBE) * square
            )
            masked = wide(v.valid[r, :]) * act
            return (
                carry[0] + jnp.sum(masked.reshape(RC // 8, 8, H), axis=0),
                carry[1] + jnp.sum((masked * act).reshape(RC // 8, 8, H), axis=0),
            )

        zero = jnp.zeros((8, H), F32)
        per = HALF // RC
        return lax.fori_loop(part * per, (part + 1) * per, chunk, (zero, zero))

    def over_rows(value):
        return jnp.sum(value, axis=0, keepdims=True)

    def keep_stats(l, total):
        count = jnp.max(v.count[0:1, :], axis=1, keepdims=True)
        mean = vec(total, 0) / count
        var = vec(total, 1) / count - mean * mean
        inverse = lax.rsqrt(var + NORM_EPS)
        gain, shift = v.npar_in[l, 0:1, :], v.npar_in[l, 1:2, :]
        v.vecs[l, 0:1, :] = mean
        v.vecs[l, 1:2, :] = inverse
        v.vecs[l, 2:3, :] = gain * inverse
        v.vecs[l, 3:4, :] = shift - mean * (gain * inverse)

    def finish(l, part_lin):
        sums = []
        for part in range(2):
            part_lin(part)
            sums.append(activate(l, part))
            if l < L - 1:
                ag_send(l + 1, v.acts.at[l], v.ag.at[l], part)
        ar_put(l, [over_rows(sums[0][i] + sums[1][i]) for i in range(2)])
        ar_send(l, l == L - 1)

    def add_first(chip, part, ref, last=False):
        high, low = split(ref[...])
        a = v.abf[chip]
        got = dot_t(cat([high, low], 1), cat([a, a], 1))
        first = -(-FR // 16) * 8
        r = slice(0, first) if part == 0 else slice(first, FR)
        seen = v.aggt[r, :]
        v.aggt[r, :] = seen + got

    v.aggt[...] = jnp.zeros((FR, 2 * R), F32)
    for part in range(2):
        add_first(ch, part, halves(v.xown)[part])
    w_pass(0)
    ag_blocks(0, v.xg, add_first)
    v.part0[...] = v.aggt[:, R:]
    send(v.part0, v.part0r, v.s_sib.at[0, 0], v.r_sib.at[0, 0], sib)
    w_wait(0)
    v.w0h[...], v.w0l[...] = split(v.wt0[...])
    feature = lax.broadcasted_iota(jnp.int32, (FR, R), 0) < F
    v.in0h[:FR, :], v.in0l[:FR, :] = split(jnp.where(feature, v.xown[...], 0.0))
    wait_bytes(v.part0r, v.r_sib.at[0, 0])
    total = v.aggt[:, :R] + v.part0r[...]
    degree = total[F : F + 1, :]
    v.in0h[FR:, :], v.in0l[FR:, :] = split(
        jnp.where(feature, total * (1.0 / jnp.maximum(degree, 1.0)), 0.0)
    )
    v.lin[...] = dot3((v.w0h[...], v.w0l[...]), (v.in0h[...], v.in0l[...])).T
    finish(0, lambda part: None)
    degree = column(degree)
    v.degree[...] = degree
    v.linked[...] = jnp.minimum(degree, 1.0)
    v.invdeg[...] = 1.0 / jnp.maximum(degree, 1.0)
    v.count[...] = ar_wait(8)[0:2]

    for l in range(1, L):
        if l == 1:
            lax.fori_loop(0, CH, adj_turn, 0)
        w_pass(l)
        ag_forward(l, v.ag.at[l - 1])
        w_wait(l)
        v.wh[l - 1], v.wl[l - 1] = split(v.wtr[l - 1])
        total = ar_wait(l - 1)
        if l < L - 1:
            w_send(l + 1)
        keep_stats(l - 1, total)
        scale, shift = v.vecs[l - 1, 2:3, :], v.vecs[l - 1, 3:4, :]
        v.inh[l - 1, :, :H], v.inl[l - 1, :, :H] = split(v.acts[l - 1] * scale + shift)
        v.lin[...] = dot3_t(
            (v.inh[l - 1, :, :H], v.inl[l - 1, :, :H]), (v.wh[l - 1, :, :H], v.wl[l - 1, :, :H])
        )

        parts, partr = v.parts.at[l - 1], v.partr.at[l - 1]

        def share(a, both, first=False):
            for at, total in ((R, parts), (0, v.agg)):
                got = dot(cat([a[at : at + R]] * 2, 1), both)
                total[...] = got if first else total[...] + got
                if at and a is v.last_columns:
                    for part in range(2):
                        send(
                            halves(parts)[part], halves(partr)[part], v.s_sib.at[l, part],
                            v.r_sib.at[l, part], sib,
                        )

        def add(chip, part, ref, last=False):
            columns = v.abf[chip, :, part * HALF : (part + 1) * HALF]
            v.last_columns = columns if last else None
            share(columns, cat(list(split(ref[...])), 0))

        v.last_columns = None
        share(v.abf[ch], cat(list(split(v.acts[l - 1])), 0), True)
        ag_blocks(l, v.ag.at[l - 1], add)

        def part_lin(part):
            r = slice(part * HALF, (part + 1) * HALF)
            wait_bytes(halves(partr)[part], v.r_sib.at[l, part])
            agg = v.agg[r, :] + partr[r, :]
            v.kept[l - 1, r, :] = agg
            v.inh[l - 1, r, H:], v.inl[l - 1, r, H:] = split(
                agg * wide(v.invdeg[r, :]) * scale + wide(v.linked[r, :]) * shift
            )
            v.lin[r, :] += dot3_t(
                (v.inh[l - 1, r, H:], v.inl[l - 1, r, H:]), (v.wh[l - 1, :, H:], v.wl[l - 1, :, H:])
            )

        finish(l, part_lin)

    for drain in drains[first_rows:]:
        drain()
    del drains[first_rows:]

    head = split(v.whp[...])
    lane = lax.broadcasted_iota(jnp.int32, (R, LANES), 1)
    onehot = jnp.where(lane.astype(F32) == v.label[...], 1.0, 0.0)
    real = lane < d.C
    counted = v.counted[...]
    label_count = jnp.max(v.count[1:2, :], axis=1, keepdims=True)
    keep_stats(L - 1, ar_wait(L - 1))
    last = split(v.acts[L - 1] * v.vecs[L - 1, 2:3, :] + v.vecs[L - 1, 3:4, :])
    logits = dot3_t(last, head) + v.biasp[...]
    top = jnp.max(jnp.where(real, logits, -3.0e38), axis=1, keepdims=True)
    moved = logits - top
    power = jnp.where(real, jnp.exp(moved), 0.0)
    power_sum = jnp.sum(power, axis=1, keepdims=True)
    g_logits = counted * (power / power_sum - onehot) / label_count
    gl_split = split(g_logits)
    v.gout[...] = dot3(gl_split, head)

    def last_sums():
        mean, inverse = v.vecs[L - 1, 0:1, :], v.vecs[L - 1, 1:2, :]

        def chunk(i, carry):
            r = rows(i, RC)
            g = v.gout[r, :]
            normed = (v.acts[L - 1, r, :] - mean) * inverse
            return (
                carry[0] + jnp.sum((g * normed).reshape(RC // 8, 8, H), axis=0),
                carry[1] + jnp.sum(g.reshape(RC // 8, 8, H), axis=0),
            )

        zero = jnp.zeros((8, H), F32)
        return [over_rows(s) for s in lax.fori_loop(0, R // RC, chunk, (zero, zero))]

    ar_put(3, last_sums())
    ar_send(3, True)
    logp = moved - jnp.log(power_sum)
    rows_loss = jnp.sum(jnp.where(real, onehot * logp, 0.0), axis=1, keepdims=True) * counted
    ar_put(6, [-over_rows(rows_loss), over_rows(g_logits)])
    ar_send(6)
    head_grad = dot3(split(g_logits.T[:CR, :]), last)
    HT = d.HT
    for t in range(HT):
        i, j = t // HV, t % HV
        v.hg[t] = head_grad[8 * i : 8 * i + 8, j * LANES : (j + 1) * LANES]

    def others(index, size, ref_of, init):
        return lax.fori_loop(1, size, lambda i, s: s + ref_of(lax.rem(index + i, size)), init)

    owners = [t * NDEV // HT for t in range(HT)]
    tile = lax.div(me * HT + NDEV - 1, NDEV)
    adds_tile = jnp.logical_and(tile < HT, lax.div(tile * NDEV, HT) == me)
    tile = jnp.minimum(tile, HT - 1)
    for t, owner in enumerate(owners):

        def go(t=t, owner=owner):
            remote(
                v.hg.at[t], v.hrecv.at[me], v.s_h.at[0], v.r_h.at[0], (owner // NC, owner % NC)
            ).start()

        either(False, me != owner, go)
    drains.append(
        lambda: either(
            HT == NDEV,
            adds_tile,
            lambda: wait_bytes(v.hrecv.at[pl.ds(0, HT - 1)], v.s_h.at[0]),
            lambda: wait_bytes(v.hrecv.at[pl.ds(0, HT)], v.s_h.at[0]),
        )
    )

    def head_gather():
        def go():
            wait_bytes(v.hrecv.at[pl.ds(0, NDEV - 1)], v.r_h.at[0])
            v.hfin[tile] = others(me, NDEV, lambda s: v.hrecv[s], v.hg[tile])

            def one(i, carry):
                remote(
                    v.hfin.at[tile], v.hfin.at[tile], v.s_h.at[1], v.r_h.at[1],
                    device(lax.rem(me + i, NDEV)),
                ).start()
                return carry

            lax.fori_loop(1, NDEV, one, 0)

        either(HT == NDEV, adds_tile, go)
        drains.append(
            lambda: either(
                HT == NDEV,
                adds_tile,
                lambda: wait_bytes(v.hrecv.at[pl.ds(0, NDEV - 1)], v.s_h.at[1]),
            )
        )

    def sibling_send(i):
        send(v.dwb.at[i, 1 - k], v.dwr.at[i], v.s_d.at[i], v.r_d.at[i], sib)

    def cols_send(i):
        wait_bytes(v.dwr.at[i], v.r_d.at[i])
        v.dwb[i, k] += v.dwr[i]
        for dd in range(1, NC):
            t = lax.rem(c + dd, NC)
            remote(v.dwb.at[i, k, t], v.zrecv.at[i, c], v.s_z.at[i], v.r_z.at[i], (n, t)).start()
        drains.append(lambda: wait_bytes(v.zrecv.at[i, pl.ds(0, NC - 1)], v.s_z.at[i]))

    def nodes_send(i):
        wait_bytes(v.zrecv.at[i, pl.ds(0, NC - 1)], v.r_z.at[i])
        v.zs[i] = others(c, NC, lambda s: v.zrecv[i, s], v.dwb[i, k, c])

        def one(j, carry):
            t = lax.rem(ch + j, CH)
            either(
                PH == CH,
                t < PH,
                lambda: remote(
                    v.zs.at[i, rows(t, RPP), :], v.nrecv.at[i, ch], v.s_n.at[i], v.r_n.at[i],
                    (t * 2 + k, c),
                ).start(),
            )
            return carry

        lax.fori_loop(1, CH, one, 0)
        drains.append(
            lambda: either(
                PH == CH,
                ch < PH,
                lambda: wait_bytes(v.zs.at[i, pl.ds(0, (PH - 1) * RPP), :], v.s_n.at[i]),
                lambda: wait_bytes(v.zs.at[i, pl.ds(0, PH * RPP), :], v.s_n.at[i]),
            )
        )

    def pieces_out(i, fin, at, piece, away=True):
        mine = pl.ds(pl.multiple_of(at, RPP), RPP)
        fin[mine, :] = piece
        square = jnp.sum((piece * piece).reshape(RPP // 8, 8, piece.shape[1]), axis=0)
        v.sq[...] += jnp.sum(square, axis=1, keepdims=True)

        if away:
            pieces_away(i, fin, at)

    def pieces_away(i, fin, at):
        block = fin.at[pl.ds(pl.multiple_of(at, RPP), RPP), :]

        def one(j, carry):
            remote(block, block, v.s_f.at[i], v.r_f.at[i], (lax.rem(n + j, NN), c)).start()
            return carry

        if NN <= 8:
            for j in range(1, NN):
                one(j, 0)
        else:
            lax.fori_loop(1, NN, one, 0)

    def pieces_drain(i, fin):
        drains.append(
            lambda: either(
                PPC == NN,
                n < PPC if i == L - 1 else ch < PH,
                lambda: lax.fori_loop(
                    1, NN, lambda j, carry: (wait_bytes(fin.at[pl.ds(0, RPP), :], v.s_f.at[i]), carry)[1], 0
                ),
            )
        )

    def nodes_gather(i):
        def go():
            wait_bytes(v.nrecv.at[i, pl.ds(0, CH - 1)], v.r_n.at[i])
            piece = others(ch, CH, lambda s: v.nrecv[i, s], v.zs[i, rows(ch, RPP), :])
            pieces_out(i, v.fin.at[i], k * (HC // 2) + ch * RPP, piece)

        either(PH == CH, ch < PH, go)
        pieces_drain(i, v.fin.at[i])

    v.sq[...] = jnp.zeros((8, LANES), F32)

    def fin_wait(i, fin):
        either(
            PPC == NN,
            n < PPC if i == L - 1 else ch < PH,
            lambda: wait_bytes(fin.at[pl.ds(0, (PPC - 1) * RPP), :], v.r_f.at[i]),
            lambda: wait_bytes(fin.at[pl.ds(0, PPC * RPP), :], v.r_f.at[i]),
        )

    def give(i, src, dst):
        copy = pltpu.make_async_copy(src, dst, v.s_out.at[i])
        copy.start()
        drains.append(copy.wait)

    def linear_grad(l, a):
        total = ar_wait(a)
        g_gain, g_shift = vec(total, 0), vec(total, 1)
        v.gn_o[l, 0:1, :] = g_gain
        v.gn_o[l, 1:2, :] = g_shift
        mean, inverse, scale = v.vecs[l, 0:1, :], v.vecs[l, 1:2, :], v.vecs[l, 2:3, :]
        count = jnp.max(v.count[0:1, :], axis=1, keepdims=True)
        by_one = scale * g_shift / count
        by_normed = scale * g_gain / count

        def chunk(i, carry):
            r = rows(i, RC)
            normed = (v.acts[l, r, :] - mean) * inverse
            g_active = scale * v.gout[r, :] - wide(v.valid[r, :]) * (by_one + normed * by_normed)
            g_linear = v.gp[l, r, :] * g_active
            v.lin[r, :] = g_linear
            v.glh[r, :], v.gll[r, :] = split(g_linear)
            return carry

        lax.fori_loop(0, R // RC, chunk, 0)

    for l in (2, 1):
        g = l - 1
        linear_grad(l, 5 - l)
        gl = (v.glh[...], v.gll[...])
        back = v.ag.at[2 - l]
        for part in range(2):
            r = slice(part * HALF, (part + 1) * HALF)
            spread = dot3((v.glh[r, :], v.gll[r, :]), (v.wh[g, :, H:], v.wl[g, :, H:]))
            v.spreads[g, r, :] = spread * wide(v.invdeg[r, :])
            send(
                halves(v.spreads.at[g])[part], halves(v.spreadr.at[g])[part],
                v.s_sib.at[L + g, part], v.r_sib.at[L + g, part], sib,
            )
        if g == 0:
            for drain in scatter_drains:
                drain()
        own = cat(list(split(v.spreads[g])), 0)
        for dd in reversed(range(CH)):
            t = v.at[0, flip(ch, dd)]
            v.out[dd] = dot(cat([t, t], 1), own)
        for part in range(2):
            wait_bytes(halves(v.spreadr.at[g])[part], v.r_sib.at[L + g, part])
        other = cat(list(split(v.spreadr[g])), 0)

        def complete(dd):
            t = v.at[1, flip(ch, dd)]
            v.out[dd] += dot(cat([t, t], 1), other)

        s, r = v.s_rs.at[g], v.r_rs.at[g]
        kept_drains, drains = drains, []
        if CH == 4:
            x, y, z = (halves(v.out.at[dd]) for dd in (1, 2, 3))
            from_x, from_y, via = (halves(back.at[i]) for i in range(3))
            complete(3)
            send(z[0], via[0], s.at[0], r.at[0], peer(1))
            send(z[1], via[1], s.at[1], r.at[1], peer(2))
            complete(1)
            send(x[0], from_x[0], s.at[2], r.at[2], peer(1))
            complete(2)
            send(y[1], from_y[1], s.at[3], r.at[3], peer(2))
            complete(0)
        else:
            for dd in reversed(range(1, CH)):
                complete(dd)
                send(v.out.at[dd], back.at[dd], s.at[dd], r.at[dd], peer(dd))
            complete(0)
        v.gout[...] = dot3(gl, (v.wh[g, :, :H], v.wl[g, :, :H]))
        mean, inverse = v.vecs[g, 0:1, :], v.vecs[g, 1:2, :]

        def chunk(i, carry):
            r = rows(i, RC)
            self, spread, degree = v.gout[r, :], v.spreads[g, r, :], wide(v.degree[r, :])
            normed = (v.acts[g, r, :] - mean) * inverse
            reached = (v.kept[g, r, :] - degree * mean) * inverse
            v.gout[r, :] = self + v.out[0, r, :]
            return (
                carry[0] + jnp.sum((self * normed + spread * reached).reshape(RC // 8, 8, H), axis=0),
                carry[1] + jnp.sum((self + spread * degree).reshape(RC // 8, 8, H), axis=0),
            )

        zero = jnp.zeros((8, H), F32)
        ar_put(6 - l, [over_rows(t) for t in lax.fori_loop(0, R // RC, chunk, (zero, zero))])
        ar_send(6 - l, True)
        grad = dot3(split(v.lin[...].T), (v.inh[g], v.inl[g]))
        for t in range(NC):
            for half in range(2):
                at = t * HC + half * (HC // 2)
                v.dwb[g, half, t] = grad[at : at + HC // 2, :]
        sibling_send(g)
        if CH == 4:
            wait_bytes(via[0], r.at[0])
            y[0][...] += via[0][...]
            send(y[0], from_y[0], s.at[5], r.at[5], peer(2))
            wait_bytes(via[1], r.at[1])
            x[1][...] += via[1][...]
            send(x[1], from_x[1], s.at[4], r.at[4], peer(1))
        scatter_drains, drains = drains, kept_drains
        if l == 2:
            head_gather()
        else:
            nodes_send(1)
        cols_send(g)
        if l == 1:
            nodes_gather(1)
        if CH == 4:
            for half, i in ((from_x[0], 2), (from_y[1], 3), (from_y[0], 5), (from_x[1], 4)):
                wait_bytes(half, r.at[i])
            v.gout[...] += back[0] + back[1]
        else:
            for dd in range(1, CH):
                wait_bytes(back.at[dd], r.at[dd])
                v.gout[...] += back[dd]
    drains += scatter_drains

    linear_grad(0, 5)
    grad = dot3_t(split(v.lin[...].T), (v.in0h[...], v.in0l[...]))
    for t in range(NC):
        v.d0[t] = grad[t * HC : (t + 1) * HC, :]

    def own_piece():
        v.recv0[me] = v.d0[c, rows(n, RPP), :]

    def first_scatter(dev, t):
        tn, tc = dev
        either(
            PPC == NN,
            tn < PPC,
            lambda: remote(
                v.d0.at[tc, rows(tn, RPP), :], v.recv0.at[me], v.s_0.at[0], v.r_0.at[0], dev
            ).start(),
        )

    to_others(first_scatter, True)
    either(PPC == NN, n < PPC, own_piece)
    drains.append(
        lambda: either(
            PPC == NN,
            n < PPC,
            lambda: wait_bytes(v.recv0.at[pl.ds(0, PPC * NC - 1)], v.s_0.at[0]),
            lambda: wait_bytes(v.recv0.at[pl.ds(0, PPC * NC)], v.s_0.at[0]),
        )
    )
    nodes_send(0)
    nodes_gather(0)

    def first_gather():
        wait_bytes(v.recv0.at[pl.ds(0, NDEV - 1)], v.r_0.at[0])
        piece = jnp.sum(v.recv0[...], axis=0)
        pieces_out(L - 1, v.fin0, n * RPP, piece, False)

    either(PPC == NN, n < PPC, first_gather)
    pieces_drain(L - 1, v.fin0)
    ar_put(7, [over_rows(v.sq[...])])
    ar_send(7, True)
    either(PPC == NN, n < PPC, lambda: pieces_away(L - 1, v.fin0, n * RPP))

    total = ar_wait(6)
    bias_grad = total[1:2]
    v.misc_o[...] = jnp.zeros((8, LANES), F32)
    v.misc_o[0:1, :] = total[0:1]
    v.misc_o[1:2, :] = v.count[1:2, :]
    v.misc_o[3:4, :] = bias_grad
    either(
        HT == NDEV,
        adds_tile,
        lambda: wait_bytes(v.hfin.at[pl.ds(0, HT - 1)], v.r_h.at[1]),
        lambda: wait_bytes(v.hfin.at[pl.ds(0, HT)], v.r_h.at[1]),
    )
    give(2, v.gn_o, v.gn)
    give(3, v.hfin, v.gh)
    square = jnp.zeros((8, LANES), F32)
    for t in range(HT):
        square += v.hfin[t] * v.hfin[t]
    replicated = over_rows(square) + bias_grad * bias_grad
    small = jnp.zeros((1, H), F32)
    for l in range(L):
        small += over_rows(v.gn_o[l] * v.gn_o[l])
    for j in range(HV):
        replicated += small[:, j * LANES : (j + 1) * LANES]
    for i in range(L - 1):
        fin_wait(i, v.fin.at[i])
        give(5 + i, v.fin.at[i], v.gr.at[i])
    total = ar_wait(7)
    squares = total[0:1, 0:1] + jnp.sum(replicated, axis=1, keepdims=True)
    norm = jnp.sqrt(squares)
    v.misc_o[2:3, :] = jnp.broadcast_to(norm, (1, LANES))
    v.misc_o[4:5, :] = jnp.broadcast_to(CLIP / jnp.maximum(norm, CLIP), (1, LANES))
    give(4, v.misc_o, v.misc)
    fin_wait(L - 1, v.fin0)
    give(0, v.fin0, v.g0)

    for drain in drains:
        drain()


def gradients(NN, NC, feat, adj, nm, lb, lm, w0, wr, npar, whd, bias):
    F, _, R = feat.shape
    C, H = whd.shape
    HC = w0.shape[0]
    CH, NDEV = NN // 2, NN * NC
    up = lambda size: -(-size // 8) * 8
    FR, CR = up(F + 1), up(C)
    RPP = max(8, HC // NN)
    HV = H // LANES
    d = types.SimpleNamespace(
        NN=NN, NC=NC, R=R, F=F, H=H, C=C, HC=HC, CH=CH, NDEV=NDEV, FR=FR, CR=CR, RPP=RPP,
        PPC=HC // RPP, PH=HC // RPP // 2, HV=HV, HT=CR // 8 * HV,
    )
    dma = pltpu.SemaphoreType.DMA
    L = LAYERS
    inputs = {
        "feat": feat, "adj": adj, "nm": nm, "lb": lb, "lm": lm, "w0": w0, "wr": wr, "npar": npar,
        "whd": whd, "bias": bias,
    }
    small = [name for name in inputs if name not in ("adj", "wr")]
    d.small = small
    scratch = {
        "xown": pltpu.VMEM((FR, R), F32),
        "xg": pltpu.VMEM((CH, FR, R), F32),
        "ag": pltpu.VMEM((L - 1, CH, R, H), F32),
        "acts": pltpu.VMEM((L, R, H), F32),
        "gp": pltpu.VMEM((L, R, H), F32),
        "adjb": pltpu.VMEM((2, CH, R, R), jnp.int32),
        "abf": pltpu.VMEM((CH, 2 * R, R), BF16),
        "at": pltpu.VMEM((2, CH, R, R), BF16),
        "wt0": pltpu.VMEM((H, 2 * FR), F32),
        "wtr": pltpu.VMEM((L - 1, H, 2 * H), F32),
        "w0h": pltpu.VMEM((H, 2 * FR), BF16),
        "w0l": pltpu.VMEM((H, 2 * FR), BF16),
        "wh": pltpu.VMEM((L - 1, H, 2 * H), BF16),
        "wl": pltpu.VMEM((L - 1, H, 2 * H), BF16),
        "whp": pltpu.VMEM((LANES, H), F32),
        "biasp": pltpu.VMEM((1, LANES), F32),
        "in0h": pltpu.VMEM((2 * FR, R), BF16),
        "in0l": pltpu.VMEM((2 * FR, R), BF16),
        "inh": pltpu.VMEM((L - 1, R, 2 * H), BF16),
        "inl": pltpu.VMEM((L - 1, R, 2 * H), BF16),
        "aggt": pltpu.VMEM((FR, 2 * R), F32),
        "part0": pltpu.VMEM((FR, R), F32),
        "part0r": pltpu.VMEM((FR, R), F32),
        "agg": pltpu.VMEM((R, H), F32),
        "parts": pltpu.VMEM((L - 1, R, H), F32),
        "partr": pltpu.VMEM((L - 1, R, H), F32),
        "kept": pltpu.VMEM((L - 1, R, H), F32),
        "lin": pltpu.VMEM((R, H), F32),
        "gout": pltpu.VMEM((R, H), F32),
        "glh": pltpu.VMEM((R, H), BF16),
        "gll": pltpu.VMEM((R, H), BF16),
        "spreads": pltpu.VMEM((L - 1, R, H), F32),
        "spreadr": pltpu.VMEM((L - 1, R, H), F32),
        "out": pltpu.VMEM((CH, R, H), F32),
        "valid": pltpu.VMEM((R, LANES), F32),
        "counted": pltpu.VMEM((R, LANES), F32),
        "label": pltpu.VMEM((R, LANES), F32),
        "degree": pltpu.VMEM((R, LANES), F32),
        "invdeg": pltpu.VMEM((R, LANES), F32),
        "linked": pltpu.VMEM((R, LANES), F32),
        "count": pltpu.VMEM((2, LANES), F32),
        "vecs": pltpu.VMEM((L, 8, H), F32),
        "sq": pltpu.VMEM((8, LANES), F32),
        "arb": pltpu.VMEM((9, NDEV, 4, LANES), F32),
        "dwb": pltpu.VMEM((L - 1, 2, NC, HC // 2, 2 * H), F32),
        "dwr": pltpu.VMEM((L - 1, NC, HC // 2, 2 * H), F32),
        "zrecv": pltpu.VMEM((L - 1, NC, HC // 2, 2 * H), F32),
        "zs": pltpu.VMEM((L - 1, HC // 2, 2 * H), F32),
        "nrecv": pltpu.VMEM((L - 1, CH, RPP, 2 * H), F32),
        "fin": pltpu.VMEM((L - 1, HC, 2 * H), F32),
        "d0": pltpu.VMEM((NC, HC, 2 * FR), F32),
        "recv0": pltpu.VMEM((NDEV, RPP, 2 * FR), F32),
        "fin0": pltpu.VMEM((HC, 2 * FR), F32),
        "hg": pltpu.VMEM((d.HT, 8, LANES), F32),
        "hrecv": pltpu.VMEM((NDEV, 8, LANES), F32),
        "hfin": pltpu.VMEM((d.HT, 8, LANES), F32),
        "ld": dma((L - 1 + len(small) + CH,)),
        "s_adj": dma((CH,)),
        "r_adj": dma((CH,)),
        "s_ag": dma((L, max(CH, 6))),
        "r_ag": dma((L, max(CH, 6))),
        "s_sib": dma((2 * L - 1, 2)),
        "r_sib": dma((2 * L - 1, 2)),
        "s_w": dma((L, NC)),
        "r_w": dma((L, NC)),
        "s_wp": dma((L, NC)),
        "r_wp": dma((L, NC)),
        "s_d": dma((L - 1,)),
        "r_d": dma((L - 1,)),
        "s_ar": dma((9,)),
        "r_ar": dma((9,)),
        "s_rs": dma((L - 1, max(CH, 6))),
        "r_rs": dma((L - 1, max(CH, 6))),
        "s_z": dma((L - 1,)),
        "r_z": dma((L - 1,)),
        "s_n": dma((L - 1,)),
        "r_n": dma((L - 1,)),
        "s_f": dma((L,)),
        "r_f": dma((L,)),
        "s_0": dma((1,)),
        "r_0": dma((1,)),
        "s_h": dma((2,)),
        "r_h": dma((2,)),
        "gn_o": pltpu.VMEM(npar.shape, F32),
        "misc_o": pltpu.VMEM((8, LANES), F32),
        "s_out": dma((L + 4,)),
    }
    for name in small:
        shape = (F, R) if name == "feat" else inputs[name].shape
        scratch[name + "_in"] = pltpu.VMEM(shape, inputs[name].dtype)
    ins = list(inputs)
    room = 6 * 2**20
    for ref in scratch.values():
        if ref.memory_space == pltpu.VMEM:
            size = jnp.dtype(ref.dtype).itemsize
            for i, length in enumerate(reversed(ref.shape)):
                size *= -(-length // LANES) * LANES if i == 0 else -(-length // 8) * 8 if i == 1 else length
            room += size
    outs = ["g0", "gr", "gn", "gh", "misc"]
    d.names = ins + outs + list(scratch)
    return pl.pallas_call(
        functools.partial(step_kernel, d),
        out_shape=[
            jax.ShapeDtypeStruct((HC, 2 * FR), F32),
            jax.ShapeDtypeStruct(wr.shape, F32),
            jax.ShapeDtypeStruct(npar.shape, F32),
            jax.ShapeDtypeStruct((d.HT, 8, LANES), F32),
            jax.ShapeDtypeStruct((8, LANES), F32),
        ],
        in_specs=[pl.BlockSpec(memory_space=pltpu.HBM)] * len(ins),
        out_specs=[pl.BlockSpec(memory_space=pl.ANY)] * len(outs),
        scratch_shapes=list(scratch.values()),
        compiler_params=pltpu.CompilerParams(
            collective_id=0, has_side_effects=True, vmem_limit_bytes=min(room, 60 * 2**20)
        ),
    )(*(pltpu.with_memory_space_constraint(a, pltpu.HBM) for a in inputs.values()))


def adamw(weight, first, second, average, grad, rate):
    first = BETA_ONE * first + (1.0 - BETA_ONE) * grad
    second = BETA_TWO * second + (1.0 - BETA_TWO) * grad * grad
    fix_one = 1.0 - BETA_ONE**ADAM_STEP
    fix_two = 1.0 - BETA_TWO**ADAM_STEP
    update = first / fix_one / (jnp.sqrt(second / fix_two) + ADAM_EPS)
    weight = weight - rate * (update + DECAY * weight)
    average = AVERAGE * average + (1.0 - AVERAGE) * weight
    return (first, second, weight, average)


def update_kernel(*refs):
    grads, state, scalars, results = refs[:5], refs[5:25], refs[25:28], refs[28:]
    misc = grads[4]
    scale = misc[4:5, 0:1]
    for i in range(3):
        scalars[i][...] = misc[i : i + 1, 0:1]
    for group in range(5):
        weight, first, second, average = (state[group + 5 * j] for j in range(4))
        rate = RATE_SMALL if group in (2, 4) else RATE_MATRIX
        shape = weight.shape
        if group == 4:
            grad = misc[3:4, : shape[1]]
        elif group == 3:
            wide = shape[1] // LANES
            grad = cat(
                [
                    cat([grads[3][wide * i + j] for j in range(wide)], 1)
                    for i in range(grads[3].shape[0] // wide)
                ],
                0,
            )[: shape[0]]
        elif group == 0:
            half = shape[1] // 2
            at = grads[0].shape[1] // 2
            grad = cat([grads[0][:, :half], grads[0][:, at : at + half]], 1)
        else:
            grad = grads[group][...]
        done = adamw(weight[...], first[...], second[...], average[...], grad * scale, rate)
        for ref, value in zip(results[4 * group : 4 * group + 4], done, strict=True):
            ref[...] = value


def local(
    nodes, cols, features, adjacency, node_mask, labels, label_mask, *state
):
    turn = (
        lambda a: a.T,
        lambda a: a.transpose(0, 2, 1),
        lambda a: a.transpose(1, 0, 2),
        lambda a: a.T,
        lambda a: a.reshape(1, -1),
    )
    back = turn[:4] + (lambda a: a.reshape(-1),)
    state = [turn[i % 5](a) for i, a in enumerate(state)]
    grads = gradients(
        nodes, cols, features.transpose(2, 0, 1), adjacency[0], node_mask, labels, label_mask, *state[:5]
    )
    outs = [jax.ShapeDtypeStruct((1, 1), F32)] * 3
    outs += [jax.ShapeDtypeStruct(a.shape, F32) for a in state[:5] for _ in range(4)]
    grads = [pltpu.with_memory_space_constraint(a, pltpu.VMEM) for a in grads]
    state = [pltpu.with_memory_space_constraint(a, pltpu.HBM) for a in state]
    done = pl.pallas_call(update_kernel, out_shape=outs)(*grads, *state)
    return (
        *(a.reshape(()) for a in done[:3]),
        *(back[i // 4](a) for i, a in enumerate(done[3:])),
    )


def solution(mesh):
    rows, first, rest, all_of = P("cols", "nodes", None), P(None, "cols"), P(None, None, "cols"), P()
    state = [first, rest, all_of, all_of, all_of]
    return jax.shard_map(
        functools.partial(local, mesh.shape["nodes"], mesh.shape["cols"]),
        mesh=mesh,
        in_specs=(rows, rows) + (P("cols", "nodes"),) * 3 + tuple(state * 4),
        out_specs=(all_of,) * 3 + tuple(spec for spec in state for _ in range(4)),
        check_vma=False,
    )
```

```python
import functools
import types

import jax
import jax.numpy as jnp
from jax import lax
from jax.experimental import pallas as pl
from jax.experimental.pallas import tpu as pltpu
from jax.sharding import PartitionSpec as P

LAYERS = 3
ADAM_STEP = 10
CLIP = 0.02
RATE_MATRIX = 0.03
RATE_SMALL = 0.3
BETA_ONE = 0.9
BETA_TWO = 0.999
ADAM_EPS = 1e-08
DECAY = 0.01
AVERAGE = 0.9
NORM_EPS = 1e-05

MESH = pl.DeviceIdType.MESH
F32 = jnp.float32
BF16 = jnp.bfloat16
LANES = 128
GELU_OUT = 0.7978845608028654
GELU_CUBE = 0.044715


def cat(values, axis):
    return values[0] if len(values) == 1 else jnp.concatenate(values, axis=axis)


def split(value):
    high = value.astype(BF16)
    return high, (value - high.astype(F32)).astype(BF16)


def dot(left, right):
    return lax.dot_general(left, right, (((1,), (0,)), ((), ())), preferred_element_type=F32)


def dot_t(left, right):
    return lax.dot_general(left, right, (((1,), (1,)), ((), ())), preferred_element_type=F32)


def dot3(left, right):
    (lh, ll), (rh, rl) = left, right
    return dot(cat([lh, lh, ll], 1), cat([rh, rl, rh], 0))


def dot3_t(left, right):
    (lh, ll), (rh, rl) = left, right
    return dot_t(cat([lh, lh, ll], 1), cat([rh, rl, rh], 1))


def remote(src, dst, send, recv, device):
    return pltpu.make_async_remote_copy(
        src_ref=src, dst_ref=dst, send_sem=send, recv_sem=recv, device_id=device, device_id_type=MESH
    )


def wait_bytes(ref, sem):
    pltpu.make_async_copy(ref, ref, sem).wait()


def flip(index, distance):
    bit = 1
    while bit <= distance:
        if distance & bit:
            index = index + (1 - 2 * lax.rem(lax.div(index, bit), 2)) * bit
        bit *= 2
    return index


def step_kernel(d, *refs):
    v = types.SimpleNamespace(**dict(zip(d.names, refs, strict=True)))
    NN, NC, R, H, HC, CH, L = d.NN, d.NC, d.R, d.H, d.HC, d.CH, LAYERS
    NDEV, RPP, PPC, PH, HV, F, FR, CR = d.NDEV, d.RPP, d.PPC, d.PH, d.HV, d.F, d.FR, d.CR
    n, c = lax.axis_index("nodes"), lax.axis_index("cols")
    me = n * NC + c
    ch, k = lax.div(n, 2), lax.rem(n, 2)
    sib = (ch * 2 + 1 - k, c)
    drains = []

    def device(index):
        return lax.div(index, NC), lax.rem(index, NC)

    def peer(dd):
        return flip(ch, dd) * 2 + k, c

    def rows(i, size):
        return pl.ds(pl.multiple_of(i * size, size), size)

    def send(src, dst, ssem, rsem, dev):
        remote(src, dst, ssem, rsem, dev).start()
        drains.append(lambda: wait_bytes(src, ssem))

    def either(always, condition, fn, other=None):
        if always:
            fn()
            return

        @pl.when(condition)
        def _():
            fn()

        if other is not None:

            @pl.when(jnp.logical_not(condition))
            def _():
                other()

    barrier = pltpu.get_barrier_semaphore()

    def adj_cols(j, core):
        return v.adj.at[:, rows(j * 2 + core, R)]

    own_rows = rows(c, HC)
    w_loads = [
        pltpu.make_async_copy(v.wr.at[i], v.wtr.at[i, own_rows, :], v.ld.at[i]) for i in range(L - 1)
    ]
    small_loads = [
        pltpu.make_async_copy(
            v.feat.at[:, 0, :] if name == "feat" else getattr(v, name),
            getattr(v, name + "_in"),
            v.ld.at[L - 1 + i],
        )
        for i, name in enumerate(d.small)
    ]
    for copy in small_loads + w_loads:
        copy.start()
    base = L - 1 + len(d.small)
    for j in range(CH):
        pltpu.make_async_copy(adj_cols(j, k), v.adjb.at[0, j], v.ld.at[base + j]).start()
    def greet(i, carry):
        pl.semaphore_signal(
            barrier, inc=1, device_id=device(lax.rem(me + i, NDEV)), device_id_type=MESH
        )
        return carry

    lax.fori_loop(1, NDEV, greet, 0)

    small_loads[0].wait()
    v.xown[:F, :] = v.feat_in[...]
    v.xown[F:, :] = jnp.ones((FR - F, R), F32)
    pl.semaphore_wait(barrier, NDEV - 1)

    def halves(ref):
        size = ref.shape[0]
        first = -(-size // 16) * 8
        return ref.at[:first], ref.at[first:]

    def ag_send(g, src, buf, part):
        s, r = v.s_ag.at[g], v.r_ag.at[g]
        mine = halves(src)
        slot = halves(buf.at[ch])
        if CH == 4:
            send(mine[part], slot[part], s.at[part], r.at[part], peer(1))
            if part == 1:
                send(mine[1], slot[1], s.at[3], r.at[3], peer(2))
                send(mine[0], slot[0], s.at[2], r.at[2], peer(2))
        elif part == 1:
            for dd in reversed(range(1, CH)):
                send(src, buf.at[ch], s.at[dd], r.at[dd], peer(dd))

    def ag_forward(g, buf):
        s, r = v.s_ag.at[g], v.r_ag.at[g]
        if CH == 4:
            x, y = (halves(buf.at[flip(ch, dd)]) for dd in (1, 2))
            wait_bytes(x[0], r.at[0])
            send(x[0], x[0], s.at[4], r.at[4], peer(2))
            wait_bytes(y[1], r.at[3])
            send(y[1], y[1], s.at[5], r.at[5], peer(1))

    def ag_blocks(g, buf, add):
        r = v.r_ag.at[g]
        if CH == 4:
            x, y, z = (halves(buf.at[flip(ch, dd)]) for dd in (1, 2, 3))
            add(flip(ch, 1), 0, x[0])
            add(flip(ch, 2), 1, y[1])
            wait_bytes(x[1], r.at[1])
            add(flip(ch, 1), 1, x[1])
            wait_bytes(y[0], r.at[2])
            add(flip(ch, 2), 0, y[0])
            wait_bytes(z[0], r.at[4])
            add(flip(ch, 3), 0, z[0])
            wait_bytes(z[1], r.at[5])
            add(flip(ch, 3), 1, z[1], True)
        else:
            for dd in range(1, CH):
                wait_bytes(buf.at[flip(ch, dd)], r.at[dd])
                for part in range(2):
                    add(flip(ch, dd), part, halves(buf.at[flip(ch, dd)])[part], dd == CH - 1 and part == 1)

    def to_others(start, at_once=False):
        if at_once and NDEV <= 32:
            for dc in [*reversed(range(1, NC)), 0]:
                for dn in reversed(range(NN)):
                    if dn or dc:
                        tn, tc = lax.rem(n + dn, NN) if dn else n, lax.rem(c + dc, NC) if dc else c
                        start((tn, tc), tn * NC + tc)
            return

        def one(i, carry):
            t = lax.rem(me + i, NDEV)
            start(device(t), t)
            return carry

        lax.fori_loop(1, NDEV, one, 0)

    def ar_send(a, at_once=False):
        to_others(
            lambda dev, t: remote(
                v.arb.at[a, me], v.arb.at[a, me], v.s_ar.at[a], v.r_ar.at[a], dev
            ).start(),
            at_once,
        )
        drains.append(lambda: wait_bytes(v.arb.at[a, pl.ds(0, NDEV - 1)], v.s_ar.at[a]))

    def ar_put(a, vectors):
        at = 0
        for vec in vectors:
            for i in range(vec.shape[1] // LANES):
                v.arb[a, me, at : at + 1, :] = vec[:, i * LANES : (i + 1) * LANES]
                at += 1
        if at < 4:
            v.arb[a, me, at:, :] = jnp.zeros((4 - at, LANES), F32)

    def ar_wait(a):
        wait_bytes(v.arb.at[a, pl.ds(0, NDEV - 1)], v.r_ar.at[a])
        return jnp.sum(v.arb[a], axis=0)

    def vec(total, i):
        return cat([total[i * HV + j : i * HV + j + 1] for j in range(HV)], 1)

    for part in range(2):
        ag_send(0, v.xown, v.xg, part)

    def w_ref(l):
        return v.wt0 if l == 0 else v.wtr.at[l - 1]

    def w_half(l, dd, core):
        at = lax.rem(c + dd, NC) * HC + core * (HC // 2)
        return w_ref(l).at[pl.ds(pl.multiple_of(at, HC // 2), HC // 2), :]

    def w_send(l):
        block = w_half(l, 0, k)
        for dd in range(1, NC):
            send(block, block, v.s_w.at[l, dd], v.r_w.at[l, dd], (n, lax.rem(c + dd, NC)))

    def w_pass(l):
        for dd in range(1, NC):
            block = w_half(l, NC - dd, k)
            wait_bytes(block, v.r_w.at[l, dd])
            send(block, block, v.s_wp.at[l, dd], v.r_wp.at[l, dd], sib)

    def w_wait(l):
        for dd in range(1, NC):
            wait_bytes(w_half(l, NC - dd, 1 - k), v.r_wp.at[l, dd])

    for copy in small_loads[1:]:
        copy.wait()
    v.wt0[own_rows, :] = jnp.zeros((HC, 2 * FR), F32)
    v.wt0[own_rows, :F] = v.w0_in[:, :F]
    v.wt0[own_rows, FR : FR + F] = v.w0_in[:, F:]
    w_send(0)
    for j in range(CH):
        send(adj_cols(j, 1 - k), v.adjb.at[1, j], v.s_adj.at[j], v.r_adj.at[j], sib)
    w_loads[0].wait()
    w_send(1)
    for copy in w_loads[1:]:
        copy.wait()

    def column(row):
        return jnp.broadcast_to(row.astype(F32), (LANES, R)).T

    v.valid[...] = column(v.nm_in[...])
    v.counted[...] = column(v.lm_in[...] * v.nm_in[...])
    v.label[...] = column(v.lb_in[...])
    v.whp[...] = jnp.zeros(v.whp.shape, F32)
    v.whp[: d.C, :] = v.whd_in[...]
    v.biasp[...] = jnp.zeros(v.biasp.shape, F32)
    v.biasp[:, : d.C] = v.bias_in[...]
    ar_put(
        8,
        [
            jnp.sum(v.valid[...], axis=0, keepdims=True),
            jnp.sum(v.counted[...], axis=0, keepdims=True),
        ],
    )
    ar_send(8)

    def adj_own(j, carry):
        pltpu.make_async_copy(adj_cols(j, k), v.adjb.at[0, j], v.ld.at[base + j]).wait()
        v.abf[j, :R, :] = v.adjb[0, j].astype(F32).astype(BF16)
        return carry

    def adj_sib(j, carry):
        wait_bytes(v.adjb.at[1, j], v.r_adj.at[j])
        v.abf[j, R:, :] = v.adjb[1, j].astype(F32).astype(BF16)
        return carry

    def adj_turn(j, carry):
        for side in range(2):
            v.at[side, j] = v.adjb[side, j].astype(F32).T.astype(BF16)
        return carry

    lax.fori_loop(0, CH, adj_own, 0)
    first_rows = len(drains)
    ag_forward(0, v.xg)
    lax.fori_loop(0, CH, adj_sib, 0)

    def wide(value):
        return cat([value] * HV, 1)

    RC = min(R // 2, 64)
    HALF = R // 2

    def activate(l, part):
        def chunk(i, carry):
            r = rows(i, RC)
            x = v.lin[r, :]
            square = x * x
            t = jnp.tanh(GELU_OUT * x * (1.0 + GELU_CUBE * square))
            half = 0.5 * (1.0 + t)
            act = x * half
            v.acts[l, r, :] = act
            v.gp[l, r, :] = half + (0.5 * GELU_OUT) * x * (1.0 - t * t) * (
                1.0 + (3.0 * GELU_CUBE) * square
            )
            masked = wide(v.valid[r, :]) * act
            return (
                carry[0] + jnp.sum(masked.reshape(RC // 8, 8, H), axis=0),
                carry[1] + jnp.sum((masked * act).reshape(RC // 8, 8, H), axis=0),
            )

        zero = jnp.zeros((8, H), F32)
        per = HALF // RC
        return lax.fori_loop(part * per, (part + 1) * per, chunk, (zero, zero))

    def over_rows(value):
        return jnp.sum(value, axis=0, keepdims=True)

    def keep_stats(l, total):
        count = jnp.max(v.count[0:1, :], axis=1, keepdims=True)
        mean = vec(total, 0) / count
        var = vec(total, 1) / count - mean * mean
        inverse = lax.rsqrt(var + NORM_EPS)
        gain, shift = v.npar_in[l, 0:1, :], v.npar_in[l, 1:2, :]
        v.vecs[l, 0:1, :] = mean
        v.vecs[l, 1:2, :] = inverse
        v.vecs[l, 2:3, :] = gain * inverse
        v.vecs[l, 3:4, :] = shift - mean * (gain * inverse)

    def finish(l, part_lin):
        sums = []
        for part in range(2):
            part_lin(part)
            sums.append(activate(l, part))
            if l < L - 1:
                ag_send(l + 1, v.acts.at[l], v.ag.at[l], part)
        ar_put(l, [over_rows(sums[0][i] + sums[1][i]) for i in range(2)])
        ar_send(l, l == L - 1)

    def add_first(chip, part, ref, last=False):
        high, low = split(ref[...])
        a = v.abf[chip]
        got = dot_t(cat([high, low], 1), cat([a, a], 1))
        first = -(-FR // 16) * 8
        r = slice(0, first) if part == 0 else slice(first, FR)
        seen = v.aggt[r, :]
        v.aggt[r, :] = seen + got

    v.aggt[...] = jnp.zeros((FR, 2 * R), F32)
    for part in range(2):
        add_first(ch, part, halves(v.xown)[part])
    w_pass(0)
    ag_blocks(0, v.xg, add_first)
    v.part0[...] = v.aggt[:, R:]
    send(v.part0, v.part0r, v.s_sib.at[0, 0], v.r_sib.at[0, 0], sib)
    w_wait(0)
    v.w0h[...], v.w0l[...] = split(v.wt0[...])
    feature = lax.broadcasted_iota(jnp.int32, (FR, R), 0) < F
    v.in0h[:FR, :], v.in0l[:FR, :] = split(jnp.where(feature, v.xown[...], 0.0))
    wait_bytes(v.part0r, v.r_sib.at[0, 0])
    total = v.aggt[:, :R] + v.part0r[...]
    degree = total[F : F + 1, :]
    v.in0h[FR:, :], v.in0l[FR:, :] = split(
        jnp.where(feature, total * (1.0 / jnp.maximum(degree, 1.0)), 0.0)
    )
    v.lin[...] = dot3((v.w0h[...], v.w0l[...]), (v.in0h[...], v.in0l[...])).T
    finish(0, lambda part: None)
    degree = column(degree)
    v.degree[...] = degree
    v.linked[...] = jnp.minimum(degree, 1.0)
    v.invdeg[...] = 1.0 / jnp.maximum(degree, 1.0)
    v.count[...] = ar_wait(8)[0:2]

    for l in range(1, L):
        if l == 1:
            lax.fori_loop(0, CH, adj_turn, 0)
        w_pass(l)
        ag_forward(l, v.ag.at[l - 1])
        w_wait(l)
        v.wh[l - 1], v.wl[l - 1] = split(v.wtr[l - 1])
        total = ar_wait(l - 1)
        if l < L - 1:
            w_send(l + 1)
        keep_stats(l - 1, total)
        scale, shift = v.vecs[l - 1, 2:3, :], v.vecs[l - 1, 3:4, :]
        v.inh[l - 1, :, :H], v.inl[l - 1, :, :H] = split(v.acts[l - 1] * scale + shift)
        v.lin[...] = dot3_t(
            (v.inh[l - 1, :, :H], v.inl[l - 1, :, :H]), (v.wh[l - 1, :, :H], v.wl[l - 1, :, :H])
        )

        parts, partr = v.parts.at[l - 1], v.partr.at[l - 1]

        def share(a, both, first=False):
            for at, total in ((R, parts), (0, v.agg)):
                got = dot(cat([a[at : at + R]] * 2, 1), both)
                total[...] = got if first else total[...] + got
                if at and a is v.last_columns:
                    for part in range(2):
                        send(
                            halves(parts)[part], halves(partr)[part], v.s_sib.at[l, part],
                            v.r_sib.at[l, part], sib,
                        )

        def add(chip, part, ref, last=False):
            columns = v.abf[chip, :, part * HALF : (part + 1) * HALF]
            v.last_columns = columns if last else None
            share(columns, cat(list(split(ref[...])), 0))

        v.last_columns = None
        share(v.abf[ch], cat(list(split(v.acts[l - 1])), 0), True)
        ag_blocks(l, v.ag.at[l - 1], add)

        def part_lin(part):
            r = slice(part * HALF, (part + 1) * HALF)
            wait_bytes(halves(partr)[part], v.r_sib.at[l, part])
            agg = v.agg[r, :] + partr[r, :]
            v.kept[l - 1, r, :] = agg
            v.inh[l - 1, r, H:], v.inl[l - 1, r, H:] = split(
                agg * wide(v.invdeg[r, :]) * scale + wide(v.linked[r, :]) * shift
            )
            v.lin[r, :] += dot3_t(
                (v.inh[l - 1, r, H:], v.inl[l - 1, r, H:]), (v.wh[l - 1, :, H:], v.wl[l - 1, :, H:])
            )

        finish(l, part_lin)

    for drain in drains[first_rows:]:
        drain()
    del drains[first_rows:]

    head = split(v.whp[...])
    lane = lax.broadcasted_iota(jnp.int32, (R, LANES), 1)
    onehot = jnp.where(lane.astype(F32) == v.label[...], 1.0, 0.0)
    real = lane < d.C
    counted = v.counted[...]
    label_count = jnp.max(v.count[1:2, :], axis=1, keepdims=True)
    keep_stats(L - 1, ar_wait(L - 1))
    last = split(v.acts[L - 1] * v.vecs[L - 1, 2:3, :] + v.vecs[L - 1, 3:4, :])
    logits = dot3_t(last, head) + v.biasp[...]
    top = jnp.max(jnp.where(real, logits, -3.0e38), axis=1, keepdims=True)
    moved = logits - top
    power = jnp.where(real, jnp.exp(moved), 0.0)
    power_sum = jnp.sum(power, axis=1, keepdims=True)
    g_logits = counted * (power / power_sum - onehot) / label_count
    gl_split = split(g_logits)
    v.gout[...] = dot3(gl_split, head)

    def last_sums():
        mean, inverse = v.vecs[L - 1, 0:1, :], v.vecs[L - 1, 1:2, :]

        def chunk(i, carry):
            r = rows(i, RC)
            g = v.gout[r, :]
            normed = (v.acts[L - 1, r, :] - mean) * inverse
            return (
                carry[0] + jnp.sum((g * normed).reshape(RC // 8, 8, H), axis=0),
                carry[1] + jnp.sum(g.reshape(RC // 8, 8, H), axis=0),
            )

        zero = jnp.zeros((8, H), F32)
        return [over_rows(s) for s in lax.fori_loop(0, R // RC, chunk, (zero, zero))]

    ar_put(3, last_sums())
    ar_send(3, True)
    logp = moved - jnp.log(power_sum)
    rows_loss = jnp.sum(jnp.where(real, onehot * logp, 0.0), axis=1, keepdims=True) * counted
    ar_put(6, [-over_rows(rows_loss), over_rows(g_logits)])
    ar_send(6)
    head_grad = dot3(split(g_logits.T[:CR, :]), last)
    HT = d.HT
    for t in range(HT):
        i, j = t // HV, t % HV
        v.hg[t] = head_grad[8 * i : 8 * i + 8, j * LANES : (j + 1) * LANES]

    def others(index, size, ref_of, init):
        if size <= 8:
            for i in range(1, size):
                init = init + ref_of(lax.rem(index + i, size))
            return init
        return lax.fori_loop(1, size, lambda i, s: s + ref_of(lax.rem(index + i, size)), init)

    owners = [t * NDEV // HT for t in range(HT)]
    tile = lax.div(me * HT + NDEV - 1, NDEV)
    adds_tile = jnp.logical_and(tile < HT, lax.div(tile * NDEV, HT) == me)
    tile = jnp.minimum(tile, HT - 1)
    for t, owner in enumerate(owners):

        def go(t=t, owner=owner):
            remote(
                v.hg.at[t], v.hrecv.at[me], v.s_h.at[0], v.r_h.at[0], (owner // NC, owner % NC)
            ).start()

        either(False, me != owner, go)
    drains.append(
        lambda: either(
            HT == NDEV,
            adds_tile,
            lambda: wait_bytes(v.hrecv.at[pl.ds(0, HT - 1)], v.s_h.at[0]),
            lambda: wait_bytes(v.hrecv.at[pl.ds(0, HT)], v.s_h.at[0]),
        )
    )

    def head_gather():
        def go():
            wait_bytes(v.hrecv.at[pl.ds(0, NDEV - 1)], v.r_h.at[0])
            v.hfin[tile] = others(me, NDEV, lambda s: v.hrecv[s], v.hg[tile])

            def one(i, carry):
                remote(
                    v.hfin.at[tile], v.hfin.at[tile], v.s_h.at[1], v.r_h.at[1],
                    device(lax.rem(me + i, NDEV)),
                ).start()
                return carry

            lax.fori_loop(1, NDEV, one, 0)

        either(HT == NDEV, adds_tile, go)
        drains.append(
            lambda: either(
                HT == NDEV,
                adds_tile,
                lambda: wait_bytes(v.hrecv.at[pl.ds(0, NDEV - 1)], v.s_h.at[1]),
            )
        )

    def sibling_send(i):
        send(v.dwb.at[i, 1 - k], v.dwr.at[i], v.s_d.at[i], v.r_d.at[i], sib)

    def cols_send(i):
        wait_bytes(v.dwr.at[i], v.r_d.at[i])
        v.dwb[i, k] += v.dwr[i]
        for dd in range(1, NC):
            t = lax.rem(c + dd, NC)
            remote(v.dwb.at[i, k, t], v.zrecv.at[i, c], v.s_z.at[i], v.r_z.at[i], (n, t)).start()
        drains.append(lambda: wait_bytes(v.zrecv.at[i, pl.ds(0, NC - 1)], v.s_z.at[i]))

    def nodes_send(i):
        wait_bytes(v.zrecv.at[i, pl.ds(0, NC - 1)], v.r_z.at[i])
        v.zs[i] = others(c, NC, lambda s: v.zrecv[i, s], v.dwb[i, k, c])

        def one(j, carry):
            t = lax.rem(ch + j, CH)
            either(
                PH == CH,
                t < PH,
                lambda: remote(
                    v.zs.at[i, rows(t, RPP), :], v.nrecv.at[i, ch], v.s_n.at[i], v.r_n.at[i],
                    (t * 2 + k, c),
                ).start(),
            )
            return carry

        if CH <= 8:
            for j in range(1, CH):
                one(j, 0)
        else:
            lax.fori_loop(1, CH, one, 0)
        drains.append(
            lambda: either(
                PH == CH,
                ch < PH,
                lambda: wait_bytes(v.zs.at[i, pl.ds(0, (PH - 1) * RPP), :], v.s_n.at[i]),
                lambda: wait_bytes(v.zs.at[i, pl.ds(0, PH * RPP), :], v.s_n.at[i]),
            )
        )

    def pieces_out(i, fin, at, piece, away=True):
        mine = pl.ds(pl.multiple_of(at, RPP), RPP)
        fin[mine, :] = piece
        square = jnp.sum((piece * piece).reshape(RPP // 8, 8, piece.shape[1]), axis=0)
        v.sq[...] += jnp.sum(square, axis=1, keepdims=True)

        if away:
            pieces_away(i, fin, at)

    def pieces_away(i, fin, at):
        block = fin.at[pl.ds(pl.multiple_of(at, RPP), RPP), :]

        def one(j, carry):
            remote(block, block, v.s_f.at[i], v.r_f.at[i], (lax.rem(n + j, NN), c)).start()
            return carry

        if NN <= 8:
            for j in range(1, NN):
                one(j, 0)
        else:
            lax.fori_loop(1, NN, one, 0)

    def pieces_drain(i, fin):
        drains.append(
            lambda: either(
                PPC == NN,
                n < PPC if i == L - 1 else ch < PH,
                lambda: lax.fori_loop(
                    1, NN, lambda j, carry: (wait_bytes(fin.at[pl.ds(0, RPP), :], v.s_f.at[i]), carry)[1], 0
                ),
            )
        )

    def nodes_gather(i):
        def go():
            wait_bytes(v.nrecv.at[i, pl.ds(0, CH - 1)], v.r_n.at[i])
            piece = others(ch, CH, lambda s: v.nrecv[i, s], v.zs[i, rows(ch, RPP), :])
            pieces_out(i, v.fin.at[i], k * (HC // 2) + ch * RPP, piece)

        either(PH == CH, ch < PH, go)
        pieces_drain(i, v.fin.at[i])

    v.sq[...] = jnp.zeros((8, LANES), F32)

    def fin_wait(i, fin):
        either(
            PPC == NN,
            n < PPC if i == L - 1 else ch < PH,
            lambda: wait_bytes(fin.at[pl.ds(0, (PPC - 1) * RPP), :], v.r_f.at[i]),
            lambda: wait_bytes(fin.at[pl.ds(0, PPC * RPP), :], v.r_f.at[i]),
        )

    def give(i, src, dst):
        copy = pltpu.make_async_copy(src, dst, v.s_out.at[i])
        copy.start()
        drains.append(copy.wait)

    def linear_grad(l, a):
        total = ar_wait(a)
        g_gain, g_shift = vec(total, 0), vec(total, 1)
        v.gn_o[l, 0:1, :] = g_gain
        v.gn_o[l, 1:2, :] = g_shift
        mean, inverse, scale = v.vecs[l, 0:1, :], v.vecs[l, 1:2, :], v.vecs[l, 2:3, :]
        count = jnp.max(v.count[0:1, :], axis=1, keepdims=True)
        by_one = scale * g_shift / count
        by_normed = scale * g_gain / count

        def chunk(i, carry):
            r = rows(i, RC)
            normed = (v.acts[l, r, :] - mean) * inverse
            g_active = scale * v.gout[r, :] - wide(v.valid[r, :]) * (by_one + normed * by_normed)
            g_linear = v.gp[l, r, :] * g_active
            v.lin[r, :] = g_linear
            v.glh[r, :], v.gll[r, :] = split(g_linear)
            return carry

        lax.fori_loop(0, R // RC, chunk, 0)

    for l in (2, 1):
        g = l - 1
        linear_grad(l, 5 - l)
        gl = (v.glh[...], v.gll[...])
        back = v.ag.at[2 - l]
        for part in range(2):
            r = slice(part * HALF, (part + 1) * HALF)
            spread = dot3((v.glh[r, :], v.gll[r, :]), (v.wh[g, :, H:], v.wl[g, :, H:]))
            v.spreads[g, r, :] = spread * wide(v.invdeg[r, :])
            send(
                halves(v.spreads.at[g])[part], halves(v.spreadr.at[g])[part],
                v.s_sib.at[L + g, part], v.r_sib.at[L + g, part], sib,
            )
        if g == 0:
            for drain in scatter_drains:
                drain()
        own = cat(list(split(v.spreads[g])), 0)
        for dd in reversed(range(CH)):
            t = v.at[0, flip(ch, dd)]
            v.out[dd] = dot(cat([t, t], 1), own)
        for part in range(2):
            wait_bytes(halves(v.spreadr.at[g])[part], v.r_sib.at[L + g, part])
        other = cat(list(split(v.spreadr[g])), 0)

        def complete(dd):
            t = v.at[1, flip(ch, dd)]
            v.out[dd] += dot(cat([t, t], 1), other)

        s, r = v.s_rs.at[g], v.r_rs.at[g]
        kept_drains, drains = drains, []
        if CH == 4:
            x, y, z = (halves(v.out.at[dd]) for dd in (1, 2, 3))
            from_x, from_y, via = (halves(back.at[i]) for i in range(3))
            complete(3)
            send(z[0], via[0], s.at[0], r.at[0], peer(1))
            send(z[1], via[1], s.at[1], r.at[1], peer(2))
            complete(1)
            send(x[0], from_x[0], s.at[2], r.at[2], peer(1))
            complete(2)
            send(y[1], from_y[1], s.at[3], r.at[3], peer(2))
            complete(0)
        else:
            for dd in reversed(range(1, CH)):
                complete(dd)
                send(v.out.at[dd], back.at[dd], s.at[dd], r.at[dd], peer(dd))
            complete(0)
        v.gout[...] = dot3(gl, (v.wh[g, :, :H], v.wl[g, :, :H]))
        mean, inverse = v.vecs[g, 0:1, :], v.vecs[g, 1:2, :]

        def chunk(i, carry):
            r = rows(i, RC)
            self, spread, degree = v.gout[r, :], v.spreads[g, r, :], wide(v.degree[r, :])
            normed = (v.acts[g, r, :] - mean) * inverse
            reached = (v.kept[g, r, :] - degree * mean) * inverse
            v.gout[r, :] = self + v.out[0, r, :]
            return (
                carry[0] + jnp.sum((self * normed + spread * reached).reshape(RC // 8, 8, H), axis=0),
                carry[1] + jnp.sum((self + spread * degree).reshape(RC // 8, 8, H), axis=0),
            )

        zero = jnp.zeros((8, H), F32)
        ar_put(6 - l, [over_rows(t) for t in lax.fori_loop(0, R // RC, chunk, (zero, zero))])
        ar_send(6 - l, True)
        grad = dot3(split(v.lin[...].T), (v.inh[g], v.inl[g]))
        for t in range(NC):
            for half in range(2):
                at = t * HC + half * (HC // 2)
                v.dwb[g, half, t] = grad[at : at + HC // 2, :]
        sibling_send(g)
        if CH == 4:
            wait_bytes(via[0], r.at[0])
            y[0][...] += via[0][...]
            send(y[0], from_y[0], s.at[5], r.at[5], peer(2))
            wait_bytes(via[1], r.at[1])
            x[1][...] += via[1][...]
            send(x[1], from_x[1], s.at[4], r.at[4], peer(1))
        scatter_drains, drains = drains, kept_drains
        if l == 2:
            head_gather()
        else:
            nodes_send(1)
        cols_send(g)
        if l == 1:
            nodes_gather(1)
        if CH == 4:
            for half, i in ((from_x[0], 2), (from_y[1], 3), (from_y[0], 5), (from_x[1], 4)):
                wait_bytes(half, r.at[i])
            v.gout[...] += back[0] + back[1]
        else:
            for dd in range(1, CH):
                wait_bytes(back.at[dd], r.at[dd])
                v.gout[...] += back[dd]
    drains += scatter_drains

    linear_grad(0, 5)
    grad = dot3_t(split(v.lin[...].T), (v.in0h[...], v.in0l[...]))
    for t in range(NC):
        v.d0[t] = grad[t * HC : (t + 1) * HC, :]

    def own_piece():
        v.recv0[me] = v.d0[c, rows(n, RPP), :]

    def first_scatter(dev, t):
        tn, tc = dev
        either(
            PPC == NN,
            tn < PPC,
            lambda: remote(
                v.d0.at[tc, rows(tn, RPP), :], v.recv0.at[me], v.s_0.at[0], v.r_0.at[0], dev
            ).start(),
        )

    to_others(first_scatter, True)
    either(PPC == NN, n < PPC, own_piece)
    drains.append(
        lambda: either(
            PPC == NN,
            n < PPC,
            lambda: wait_bytes(v.recv0.at[pl.ds(0, PPC * NC - 1)], v.s_0.at[0]),
            lambda: wait_bytes(v.recv0.at[pl.ds(0, PPC * NC)], v.s_0.at[0]),
        )
    )
    nodes_send(0)
    nodes_gather(0)

    def first_gather():
        wait_bytes(v.recv0.at[pl.ds(0, NDEV - 1)], v.r_0.at[0])
        piece = jnp.sum(v.recv0[...], axis=0)
        pieces_out(L - 1, v.fin0, n * RPP, piece, False)

    either(PPC == NN, n < PPC, first_gather)
    pieces_drain(L - 1, v.fin0)
    ar_put(7, [over_rows(v.sq[...])])
    ar_send(7, True)
    either(PPC == NN, n < PPC, lambda: pieces_away(L - 1, v.fin0, n * RPP))

    total = ar_wait(6)
    bias_grad = total[1:2]
    v.misc_o[...] = jnp.zeros((8, LANES), F32)
    v.misc_o[0:1, :] = total[0:1]
    v.misc_o[1:2, :] = v.count[1:2, :]
    v.misc_o[3:4, :] = bias_grad
    either(
        HT == NDEV,
        adds_tile,
        lambda: wait_bytes(v.hfin.at[pl.ds(0, HT - 1)], v.r_h.at[1]),
        lambda: wait_bytes(v.hfin.at[pl.ds(0, HT)], v.r_h.at[1]),
    )
    give(2, v.gn_o, v.gn)
    give(3, v.hfin, v.gh)
    square = jnp.zeros((8, LANES), F32)
    for t in range(HT):
        square += v.hfin[t] * v.hfin[t]
    replicated = over_rows(square) + bias_grad * bias_grad
    small = jnp.zeros((1, H), F32)
    for l in range(L):
        small += over_rows(v.gn_o[l] * v.gn_o[l])
    for j in range(HV):
        replicated += small[:, j * LANES : (j + 1) * LANES]
    for i in range(L - 1):
        fin_wait(i, v.fin.at[i])
        give(5 + i, v.fin.at[i], v.gr.at[i])
    total = ar_wait(7)
    squares = total[0:1, 0:1] + jnp.sum(replicated, axis=1, keepdims=True)
    norm = jnp.sqrt(squares)
    v.misc_o[2:3, :] = jnp.broadcast_to(norm, (1, LANES))
    v.misc_o[4:5, :] = jnp.broadcast_to(CLIP / jnp.maximum(norm, CLIP), (1, LANES))
    give(4, v.misc_o, v.misc)
    fin_wait(L - 1, v.fin0)
    give(0, v.fin0, v.g0)

    for drain in drains:
        drain()


def gradients(NN, NC, feat, adj, nm, lb, lm, w0, wr, npar, whd, bias):
    F, _, R = feat.shape
    C, H = whd.shape
    HC = w0.shape[0]
    CH, NDEV = NN // 2, NN * NC
    up = lambda size: -(-size // 8) * 8
    FR, CR = up(F + 1), up(C)
    RPP = max(8, HC // NN)
    HV = H // LANES
    d = types.SimpleNamespace(
        NN=NN, NC=NC, R=R, F=F, H=H, C=C, HC=HC, CH=CH, NDEV=NDEV, FR=FR, CR=CR, RPP=RPP,
        PPC=HC // RPP, PH=HC // RPP // 2, HV=HV, HT=CR // 8 * HV,
    )
    dma = pltpu.SemaphoreType.DMA
    L = LAYERS
    inputs = {
        "feat": feat, "adj": adj, "nm": nm, "lb": lb, "lm": lm, "w0": w0, "wr": wr, "npar": npar,
        "whd": whd, "bias": bias,
    }
    small = [name for name in inputs if name not in ("adj", "wr")]
    d.small = small
    scratch = {
        "xown": pltpu.VMEM((FR, R), F32),
        "xg": pltpu.VMEM((CH, FR, R), F32),
        "ag": pltpu.VMEM((L - 1, CH, R, H), F32),
        "acts": pltpu.VMEM((L, R, H), F32),
        "gp": pltpu.VMEM((L, R, H), F32),
        "adjb": pltpu.VMEM((2, CH, R, R), jnp.int32),
        "abf": pltpu.VMEM((CH, 2 * R, R), BF16),
        "at": pltpu.VMEM((2, CH, R, R), BF16),
        "wt0": pltpu.VMEM((H, 2 * FR), F32),
        "wtr": pltpu.VMEM((L - 1, H, 2 * H), F32),
        "w0h": pltpu.VMEM((H, 2 * FR), BF16),
        "w0l": pltpu.VMEM((H, 2 * FR), BF16),
        "wh": pltpu.VMEM((L - 1, H, 2 * H), BF16),
        "wl": pltpu.VMEM((L - 1, H, 2 * H), BF16),
        "whp": pltpu.VMEM((LANES, H), F32),
        "biasp": pltpu.VMEM((1, LANES), F32),
        "in0h": pltpu.VMEM((2 * FR, R), BF16),
        "in0l": pltpu.VMEM((2 * FR, R), BF16),
        "inh": pltpu.VMEM((L - 1, R, 2 * H), BF16),
        "inl": pltpu.VMEM((L - 1, R, 2 * H), BF16),
        "aggt": pltpu.VMEM((FR, 2 * R), F32),
        "part0": pltpu.VMEM((FR, R), F32),
        "part0r": pltpu.VMEM((FR, R), F32),
        "agg": pltpu.VMEM((R, H), F32),
        "parts": pltpu.VMEM((L - 1, R, H), F32),
        "partr": pltpu.VMEM((L - 1, R, H), F32),
        "kept": pltpu.VMEM((L - 1, R, H), F32),
        "lin": pltpu.VMEM((R, H), F32),
        "gout": pltpu.VMEM((R, H), F32),
        "glh": pltpu.VMEM((R, H), BF16),
        "gll": pltpu.VMEM((R, H), BF16),
        "spreads": pltpu.VMEM((L - 1, R, H), F32),
        "spreadr": pltpu.VMEM((L - 1, R, H), F32),
        "out": pltpu.VMEM((CH, R, H), F32),
        "valid": pltpu.VMEM((R, LANES), F32),
        "counted": pltpu.VMEM((R, LANES), F32),
        "label": pltpu.VMEM((R, LANES), F32),
        "degree": pltpu.VMEM((R, LANES), F32),
        "invdeg": pltpu.VMEM((R, LANES), F32),
        "linked": pltpu.VMEM((R, LANES), F32),
        "count": pltpu.VMEM((2, LANES), F32),
        "vecs": pltpu.VMEM((L, 8, H), F32),
        "sq": pltpu.VMEM((8, LANES), F32),
        "arb": pltpu.VMEM((9, NDEV, 4, LANES), F32),
        "dwb": pltpu.VMEM((L - 1, 2, NC, HC // 2, 2 * H), F32),
        "dwr": pltpu.VMEM((L - 1, NC, HC // 2, 2 * H), F32),
        "zrecv": pltpu.VMEM((L - 1, NC, HC // 2, 2 * H), F32),
        "zs": pltpu.VMEM((L - 1, HC // 2, 2 * H), F32),
        "nrecv": pltpu.VMEM((L - 1, CH, RPP, 2 * H), F32),
        "fin": pltpu.VMEM((L - 1, HC, 2 * H), F32),
        "d0": pltpu.VMEM((NC, HC, 2 * FR), F32),
        "recv0": pltpu.VMEM((NDEV, RPP, 2 * FR), F32),
        "fin0": pltpu.VMEM((HC, 2 * FR), F32),
        "hg": pltpu.VMEM((d.HT, 8, LANES), F32),
        "hrecv": pltpu.VMEM((NDEV, 8, LANES), F32),
        "hfin": pltpu.VMEM((d.HT, 8, LANES), F32),
        "ld": dma((L - 1 + len(small) + CH,)),
        "s_adj": dma((CH,)),
        "r_adj": dma((CH,)),
        "s_ag": dma((L, max(CH, 6))),
        "r_ag": dma((L, max(CH, 6))),
        "s_sib": dma((2 * L - 1, 2)),
        "r_sib": dma((2 * L - 1, 2)),
        "s_w": dma((L, NC)),
        "r_w": dma((L, NC)),
        "s_wp": dma((L, NC)),
        "r_wp": dma((L, NC)),
        "s_d": dma((L - 1,)),
        "r_d": dma((L - 1,)),
        "s_ar": dma((9,)),
        "r_ar": dma((9,)),
        "s_rs": dma((L - 1, max(CH, 6))),
        "r_rs": dma((L - 1, max(CH, 6))),
        "s_z": dma((L - 1,)),
        "r_z": dma((L - 1,)),
        "s_n": dma((L - 1,)),
        "r_n": dma((L - 1,)),
        "s_f": dma((L,)),
        "r_f": dma((L,)),
        "s_0": dma((1,)),
        "r_0": dma((1,)),
        "s_h": dma((2,)),
        "r_h": dma((2,)),
        "gn_o": pltpu.VMEM(npar.shape, F32),
        "misc_o": pltpu.VMEM((8, LANES), F32),
        "s_out": dma((L + 4,)),
    }
    for name in small:
        shape = (F, R) if name == "feat" else inputs[name].shape
        scratch[name + "_in"] = pltpu.VMEM(shape, inputs[name].dtype)
    ins = list(inputs)
    room = 6 * 2**20
    for ref in scratch.values():
        if ref.memory_space == pltpu.VMEM:
            size = jnp.dtype(ref.dtype).itemsize
            for i, length in enumerate(reversed(ref.shape)):
                size *= -(-length // LANES) * LANES if i == 0 else -(-length // 8) * 8 if i == 1 else length
            room += size
    outs = ["g0", "gr", "gn", "gh", "misc"]
    d.names = ins + outs + list(scratch)
    return pl.pallas_call(
        functools.partial(step_kernel, d),
        out_shape=[
            jax.ShapeDtypeStruct((HC, 2 * FR), F32),
            jax.ShapeDtypeStruct(wr.shape, F32),
            jax.ShapeDtypeStruct(npar.shape, F32),
            jax.ShapeDtypeStruct((d.HT, 8, LANES), F32),
            jax.ShapeDtypeStruct((8, LANES), F32),
        ],
        in_specs=[pl.BlockSpec(memory_space=pltpu.HBM)] * len(ins),
        out_specs=[pl.BlockSpec(memory_space=pl.ANY)] * len(outs),
        scratch_shapes=list(scratch.values()),
        compiler_params=pltpu.CompilerParams(
            collective_id=0, has_side_effects=True, vmem_limit_bytes=min(room, 60 * 2**20)
        ),
    )(*(pltpu.with_memory_space_constraint(a, pltpu.HBM) for a in inputs.values()))


def adamw(weight, first, second, average, grad, rate):
    first = BETA_ONE * first + (1.0 - BETA_ONE) * grad
    second = BETA_TWO * second + (1.0 - BETA_TWO) * grad * grad
    fix_one = 1.0 - BETA_ONE**ADAM_STEP
    fix_two = 1.0 - BETA_TWO**ADAM_STEP
    update = first / fix_one / (jnp.sqrt(second / fix_two) + ADAM_EPS)
    weight = weight - rate * (update + DECAY * weight)
    average = AVERAGE * average + (1.0 - AVERAGE) * weight
    return (first, second, weight, average)


def update_kernel(*refs):
    grads, state, scalars, results = refs[:5], refs[5:25], refs[25:28], refs[28:]
    misc = grads[4]
    scale = misc[4:5, 0:1]
    for i in range(3):
        scalars[i][...] = misc[i : i + 1, 0:1]
    for group in range(5):
        weight, first, second, average = (state[group + 5 * j] for j in range(4))
        rate = RATE_SMALL if group in (2, 4) else RATE_MATRIX
        shape = weight.shape
        if group == 4:
            grad = misc[3:4, : shape[1]]
        elif group == 3:
            wide = shape[1] // LANES
            grad = cat(
                [
                    cat([grads[3][wide * i + j] for j in range(wide)], 1)
                    for i in range(grads[3].shape[0] // wide)
                ],
                0,
            )[: shape[0]]
        elif group == 0:
            half = shape[1] // 2
            at = grads[0].shape[1] // 2
            grad = cat([grads[0][:, :half], grads[0][:, at : at + half]], 1)
        else:
            grad = grads[group][...]
        done = adamw(weight[...], first[...], second[...], average[...], grad * scale, rate)
        for ref, value in zip(results[4 * group : 4 * group + 4], done, strict=True):
            ref[...] = value


def local(
    nodes, cols, features, adjacency, node_mask, labels, label_mask, *state
):
    turn = (
        lambda a: a.T,
        lambda a: a.transpose(0, 2, 1),
        lambda a: a.transpose(1, 0, 2),
        lambda a: a.T,
        lambda a: a.reshape(1, -1),
    )
    back = turn[:4] + (lambda a: a.reshape(-1),)
    state = [turn[i % 5](a) for i, a in enumerate(state)]
    grads = gradients(
        nodes, cols, features.transpose(2, 0, 1), adjacency[0], node_mask, labels, label_mask, *state[:5]
    )
    outs = [jax.ShapeDtypeStruct((1, 1), F32)] * 3
    outs += [jax.ShapeDtypeStruct(a.shape, F32) for a in state[:5] for _ in range(4)]
    grads = [pltpu.with_memory_space_constraint(a, pltpu.VMEM) for a in grads]
    state = [pltpu.with_memory_space_constraint(a, pltpu.HBM) for a in state]
    done = pl.pallas_call(update_kernel, out_shape=outs)(*grads, *state)
    return (
        *(a.reshape(()) for a in done[:3]),
        *(back[i // 4](a) for i, a in enumerate(done[3:])),
    )


def solution(mesh):
    rows, first, rest, all_of = P("cols", "nodes", None), P(None, "cols"), P(None, None, "cols"), P()
    state = [first, rest, all_of, all_of, all_of]
    return jax.shard_map(
        functools.partial(local, mesh.shape["nodes"], mesh.shape["cols"]),
        mesh=mesh,
        in_specs=(rows, rows) + (P("cols", "nodes"),) * 3 + tuple(state * 4),
        out_specs=(all_of,) * 3 + tuple(spec for spec in state for _ in range(4)),
        check_vma=False,
    )
```
